32 devices in a mesh: dp: 8 (over z, x), tensor: 4 (over y, core).
Axes of the slice: x: 2, y: 2, z: 4, core: 2. Of those that a mesh axis runs over, the one named last changes fastest.
Arguments:
- activations: bfloat16 [8192, 4096], P('dp', 'tensor'), may hold values from -6 to 6
- out_grad: bfloat16 [8192, 4096], P('dp', 'tensor'), may hold values from -6 to 6
- weight: bfloat16 [4096, 4096], P(None, 'tensor'), may hold values from -0.09375 to 0.09375
- error: float32 [8, 4096, 4096], P('dp', None, 'tensor'), may hold values from -6 to 6
- q_start: float32 [4096, 32], P('tensor'), may hold values from -0.09375 to 0.09375
Outputs:
- input_grad: float32 [8192, 4096], P('dp', 'tensor')
- new_error: float32 [8, 4096, 4096], P('dp', None, 'tensor')
- q_factor: float32 [4096, 32], P('tensor')
The draws below stay inside these ranges and needn't reach their ends.
All inputs are finite; a program needn't handle non-finite values.
Results may differ from the reference program's by a relative error of at most 0.0003.
Values may be sent and summed in bfloat16 or wider, within the bound.
No kernel may reach another device: no remote copies, remote signals or barrier semaphores. Data moves between devices by JAX's collectives and lax.ppermute only.
A program may use at most 128 MiB of HBM per device.

```python
import math
import jax
import jax.numpy as jnp
from jax import lax

DIN = 4096
DOUT = 4096
RANK = 32
TOK_DEV = 1024
TOKENS = 8192
N_DP = 8


def levels(stream_key, extent, shards, low, largest):
    factor_of, own = 1.0, jax.random.fold_in(stream_key, 6)
    for position, blocks in shards:
        heights = jnp.exp(jax.random.uniform(jax.random.fold_in(own, position), (blocks,), jnp.float32, low / len(shards), largest / len(shards)))
        factor_of = factor_of * jnp.repeat(heights, extent[position] // blocks).reshape([-1 if axis == position else 1 for axis in range(len(extent))])
    return factor_of


def scatter_about(stream_key, extent, deviation, reach, split=(), held_as=jnp.bfloat16):
    values = jax.random.normal(stream_key, extent, jnp.float32) * deviation
    if len(split) > 0:
        values = levels(stream_key, extent, split, -0.22, 0.18) * values
    return jnp.clip(values, min=-reach, max=reach).astype(held_as)


def setup_inputs(seed: int = 0) -> dict:
    key_of = jax.random.split(jax.random.key(seed), 6)
    activations = scatter_about(key_of[0], (TOKENS, DIN), 1.0, 6.0, ((0, 8), (1, 4)))
    out_grad = scatter_about(key_of[1], (TOKENS, DOUT), 1.0, 6.0, ((0, 8), (1, 4)))
    weight = scatter_about(key_of[2], (DIN, DOUT), DOUT ** -0.5, 0.09375, ((1, 4),))
    error = scatter_about(key_of[3], (N_DP, DIN, DOUT), 1.0, 6.0, ((0, 8), (2, 4)), jnp.float32)
    q_start = scatter_about(key_of[4], (DOUT, RANK), DOUT ** -0.5, 0.09375, ((0, 4),), jnp.float32)
    return dict(activations=activations, out_grad=out_grad, weight=weight, error=error, q_start=q_start)


def reference(activations, out_grad, weight, error, q_start):
    grad_scale = 1.0 / math.sqrt(TOK_DEV)
    input_grad = jnp.dot(out_grad.astype(jnp.float32), weight.T.astype(jnp.float32), preferred_element_type=jnp.float32)
    x_blocks = activations.reshape(N_DP, TOK_DEV, DIN)
    g_blocks = out_grad.reshape(N_DP, TOK_DEV, DOUT)

    def merge_one(items):
        x_block, g_block, e_block = items
        local = lax.dot_general(x_block.astype(jnp.float32), g_block.astype(jnp.float32), (((0,), (0,)), ((), ())), preferred_element_type=jnp.float32)
        return local * grad_scale + e_block
    merged = lax.map(merge_one, (x_blocks, g_blocks, error))

    def sketch_one(block):
        return jnp.dot(block, q_start, precision=lax.Precision.HIGHEST)
    sketch = lax.optimization_barrier(jnp.sum(lax.map(sketch_one, merged), axis=0)) / N_DP
    gram = jnp.dot(sketch.T, sketch, precision=lax.Precision.HIGHEST)
    factor_low = jnp.linalg.cholesky(gram)
    basis = lax.linalg.triangular_solve(factor_low, sketch, left_side=False, lower=True, transpose_a=True)

    def right_one(block):
        return jnp.dot(block.T, basis, precision=lax.Precision.HIGHEST)
    q_factor = lax.optimization_barrier(jnp.sum(lax.map(right_one, merged), axis=0)) / N_DP
    approx = jnp.dot(basis, q_factor.T, precision=lax.Precision.HIGHEST)
    new_error = merged - approx[None]
    return (input_grad, new_error, q_factor)
```

```python
import functools
import math

import jax
import jax.numpy as jnp
from jax import lax
from jax.experimental import pallas as pl
from jax.experimental.pallas import tpu as pltpu
from jax.sharding import PartitionSpec as P

TOK_DEV = 1024
RANK = 32
MIB = 1 << 20
F32 = jnp.float32
BF16 = jnp.bfloat16


def dot(a, b, ca, cb, precision=None):
    return lax.dot_general(
        a, b, (((ca,), (cb,)), ((), ())), precision=precision, preferred_element_type=F32
    )


def split(a):
    high = a.astype(BF16)
    return high, (a - high.astype(F32)).astype(BF16)


def params(mib):
    return pltpu.CompilerParams(vmem_limit_bytes=mib * MIB)


def cost(flops, nbytes):
    return pl.CostEstimate(flops=int(flops), bytes_accessed=int(nbytes), transcendentals=0)


def sketch_kernel(ids, e_ref, qt_ref, g_ref, send_ref, keep_ref, y_ref, qs_ref, *, tok):
    phase = pl.program_id(0)
    first = (phase == 0) & (pl.program_id(1) == 0) & (pl.program_id(2) == 0)

    @pl.when(first)
    def _():
        high, low = split(qt_ref[...])
        qs_ref[0:RANK, :] = high
        qs_ref[RANK : 2 * RANK, :] = low
        both = dot(qs_ref[...], g_ref[...], 1, 1)
        y_ref[...] = both[0:RANK, :] + both[RANK : 2 * RANK, :]

    high, low = split(e_ref[...])
    main = dot(high, qs_ref[...], 1, 1)
    rest = dot(low, qs_ref[0:RANK, :], 1, 1)
    rows = (main[:, 0:RANK] + main[:, RANK : 2 * RANK] + rest).T

    @pl.when(phase == 0)
    def _():
        send_ref[0] = rows

    @pl.when(phase == 1)
    def _():
        keep_ref[0] = rows


def local_sketch(error, q_t, out_grad, core, chips, part):
    blk = min(512, part)
    per = part // blk
    tok, outs = out_grad.shape
    last = (chips - 1, per - 1)

    def e_map(p, y, j, ids):
        return ((2 * y + jnp.where(p == 0, 1 - ids[0], ids[0])) * per + j, 0)

    def send_map(p, y, j, ids):
        return (jnp.where(p == 0, y, last[0]), 0, jnp.where(p == 0, j, last[1]))

    def keep_map(p, y, j, ids):
        return (jnp.where(p == 1, y, 0), 0, jnp.where(p == 1, j, 0))

    half = jax.ShapeDtypeStruct((chips, RANK, part), F32)
    return pl.pallas_call(
        functools.partial(sketch_kernel, tok=tok),
        grid_spec=pltpu.PrefetchScalarGridSpec(
            num_scalar_prefetch=1,
            grid=(2, chips, per),
            in_specs=[
                pl.BlockSpec((blk, outs), e_map),
                pl.BlockSpec((RANK, outs), lambda p, y, j, ids: (0, 0)),
                pl.BlockSpec((tok, outs), lambda p, y, j, ids: (0, 0)),
            ],
            out_specs=[
                pl.BlockSpec((1, RANK, blk), send_map),
                pl.BlockSpec((1, RANK, blk), keep_map),
                pl.BlockSpec((RANK, tok), lambda p, y, j, ids: (0, 0)),
            ],
            scratch_shapes=[pltpu.VMEM((2 * RANK, outs), BF16)],
        ),
        out_shape=[half, half, jax.ShapeDtypeStruct((RANK, tok), F32)],
        compiler_params=params(32),
        cost_estimate=cost(6e9, error.size * 4),
        name="error_sketch",
    )(jnp.reshape(core, (1,)), error, q_t, out_grad)


def sketch_rows_kernel(*refs, n_in, n_y, n_out, scale):
    ids = refs[0]
    e_refs = refs[1 : 1 + n_in]
    y_refs = refs[1 + n_in : 1 + n_in + n_y]
    x_ref = refs[1 + n_in + n_y]
    outs = refs[2 + n_in + n_y :]
    scr = outs[-1]
    outs = outs[:-1]
    y = sum(r[...] for r in y_refs[1:]) + y_refs[0][...]
    high, low = split(y)
    both = dot(jnp.concatenate([high, low], axis=0), x_ref[...], 1, 0)
    total = (both[0:RANK, :] + both[RANK:, :]) * scale
    for r in e_refs:
        total = total + r[...]
    scr[...] = total
    width = total.shape[1] // n_out
    for k in range(n_out):
        at = pl.multiple_of((ids[0] ^ k) * width, width)
        outs[k][...] = scr[:, pl.ds(at, width)]


def sketch_rows(me, e_list, y_list, acts, n_out, scale):
    part = acts.shape[1]
    vm = pl.BlockSpec(memory_space=pltpu.VMEM)
    n = len(e_list) + len(y_list) + 1
    return pl.pallas_call(
        functools.partial(
            sketch_rows_kernel, n_in=len(e_list), n_y=len(y_list), n_out=n_out, scale=scale
        ),
        in_specs=[pl.BlockSpec(memory_space=pltpu.SMEM)] + [vm] * n,
        out_specs=[vm] * n_out,
        out_shape=[jax.ShapeDtypeStruct((RANK, part // n_out), F32)] * n_out,
        scratch_shapes=[pltpu.VMEM((RANK, part), F32)],
        compiler_params=params(24),
        cost_estimate=cost(1e9, 3e6),
        name="sketch_rows",
    )(jnp.reshape(me, (1,)), *e_list, *y_list, acts)


def basis_kernel(*refs, n_dp, n_t, width, part, inv_n, groups):
    ids, src = refs[0], refs[1]
    pieces = refs[2 : 2 + groups]
    out = refs[2 + groups]
    sk = refs[3 + groups]
    for k in range(groups):
        for r in range(n_t):
            at = pl.multiple_of(src[r] * part + (ids[0] ^ k) * width, width)
            sk[:, pl.ds(at, width)] = pieces[k][r] * inv_n
    s = sk[...]
    gram = dot(s, s, 1, 1, lax.Precision.HIGHEST)
    row = lax.broadcasted_iota(jnp.int32, (RANK, RANK), 0)
    col = lax.broadcasted_iota(jnp.int32, (RANK, RANK), 1)
    eye = (row == col).astype(F32)
    m = jnp.concatenate([gram, eye, jnp.zeros((RANK, 2 * RANK), F32)], axis=1)
    index = lax.broadcasted_iota(jnp.int32, (RANK, 1), 0)
    for j in range(RANK - 1):
        factor = jnp.where(index > j, m[:, j : j + 1] / m[j : j + 1, j : j + 1], 0.0)
        m = m - factor * m[j : j + 1, :]
    diag = jnp.sum(jnp.where(row == col, m[:, 0:RANK], 0.0), axis=1, keepdims=True)
    inverse = m[:, RANK : 2 * RANK] / jnp.sqrt(diag)
    out[...] = dot(inverse, s, 1, 0, lax.Precision.HIGHEST)


def make_basis(me, src, pieces, n_dp, part, din):
    groups = len(pieces)
    n_t, _, width = pieces[0].shape
    vm = pl.BlockSpec(memory_space=pltpu.VMEM)
    sm = pl.BlockSpec(memory_space=pltpu.SMEM)
    return pl.pallas_call(
        functools.partial(
            basis_kernel, n_dp=n_dp, n_t=n_t, width=width, part=part, inv_n=1.0 / n_dp, groups=groups
        ),
        in_specs=[sm, sm] + [vm] * groups,
        out_specs=vm,
        out_shape=jax.ShapeDtypeStruct((RANK, din), F32),
        scratch_shapes=[pltpu.VMEM((RANK, din), F32)],
        compiler_params=params(24),
        cost_estimate=cost(6e9, 2e6),
        name="basis",
    )(jnp.reshape(me, (1,)), src, *pieces)


def right_kernel(*refs, n_t, per, n_out, scale):
    ids, src = refs[0], refs[1]
    e_ref, b_ref, g_ref = refs[2:5]
    x_refs = refs[5 : 5 + n_t]
    outs = refs[5 + n_t : 5 + n_t + n_out]
    acc, vacc = refs[5 + n_t + n_out :]
    r, j = pl.program_id(0), pl.program_id(1)

    @pl.when((r == 0) & (j == 0))
    def _():
        acc[...] = jnp.zeros_like(acc)
        vacc[...] = jnp.zeros_like(vacc)

    bh, bl = split(b_ref[...])
    both = jnp.concatenate([bh, bl], axis=0)
    eh, el = split(e_ref[...])
    main = dot(both, eh, 1, 0)
    rest = dot(bh, el, 1, 0)
    acc[...] += main[0:RANK, :] + main[RANK:, :] + rest
    for n in range(n_t):

        @pl.when(r == n)
        def _(n=n):
            v = dot(both, x_refs[n][...], 1, 0)
            vacc[...] += v[0:RANK, :] + v[RANK:, :]

    @pl.when((r == n_t - 1) & (j == per - 1))
    def _():
        vh, vl = split(vacc[...])
        w = dot(jnp.concatenate([vh, vl], axis=0), g_ref[...], 1, 0)
        acc[...] += (w[0:RANK, :] + w[RANK:, :]) * scale
        width = acc.shape[1] // n_out
        for k in range(n_out):
            at = pl.multiple_of((ids[0] ^ k) * width, width)
            outs[k][...] = acc[:, pl.ds(at, width)]


def x_map(n, per, r, j, *_):
    return (jnp.clip((r - n) * per + j, 0, per - 1), 0)


def right_factor(me, src, error, basis_t, out_grad, xts, n_out, scale):
    part = xts[0].shape[0]
    tok, outs = out_grad.shape
    n_t = len(xts)
    blk = min(512, part)
    per = part // blk
    return pl.pallas_call(
        functools.partial(right_kernel, n_t=n_t, per=per, n_out=n_out, scale=scale),
        grid_spec=pltpu.PrefetchScalarGridSpec(
            num_scalar_prefetch=2,
            grid=(n_t, per),
            in_specs=[
                pl.BlockSpec((blk, outs), lambda r, j, ids, src: (src[r] * per + j, 0)),
                pl.BlockSpec((RANK, blk), lambda r, j, ids, src: (0, src[r] * per + j)),
                pl.BlockSpec((tok, outs), lambda r, j, ids, src: (0, 0)),
            ]
            + [pl.BlockSpec((blk, tok), functools.partial(x_map, n, per)) for n in range(n_t)],
            out_specs=[pl.BlockSpec((RANK, outs // n_out), lambda r, j, ids, src: (0, 0))] * n_out,
            scratch_shapes=[pltpu.VMEM((RANK, outs), F32), pltpu.VMEM((RANK, tok), F32)],
        ),
        out_shape=[jax.ShapeDtypeStruct((RANK, outs // n_out), F32)] * n_out,
        compiler_params=params(40),
        cost_estimate=cost(9e9, error.size * 4 + n_t * part * tok * 2),
        name="right_factor",
    )(jnp.reshape(me, (1,)), src, error, basis_t, out_grad, *xts)


def update_kernel(*refs, n_t, groups, width, inv_n, scale):
    ids, src = refs[0], refs[1]
    e_ref, b_ref, g_ref = refs[2:5]
    x_refs = refs[5 : 5 + n_t]
    q_refs = refs[5 + n_t : 5 + n_t + groups]
    out, qt_out, qs = refs[5 + n_t + groups :]
    r, j = pl.program_id(0), pl.program_id(1)

    @pl.when((r == 0) & (j == 0))
    def _():
        for k in range(groups):
            at = pl.multiple_of((ids[0] ^ k) * width, width)
            qt_out[:, pl.ds(at, width)] = q_refs[k][...] * inv_n
        high, low = split(qt_out[...])
        qs[0:RANK, :] = high
        qs[RANK : 2 * RANK, :] = low
        qs[2 * RANK : 3 * RANK, :] = high

    bh, bl = split(b_ref[...].T)
    approx = dot(jnp.concatenate([bh, bh, bl], axis=1), qs[...], 1, 0)
    base = e_ref[...] - approx
    for n in range(n_t):

        @pl.when(r == n)
        def _(n=n):
            out[...] = base + dot(x_refs[n][...], g_ref[...], 1, 0) * scale


def update_error(me, src, error, basis_t, out_grad, xts, q_pieces, n_dp, scale):
    part = xts[0].shape[0]
    tok, outs = out_grad.shape
    n_t = len(xts)
    blk = min(512, part)
    per = part // blk
    groups = len(q_pieces)
    width = outs // groups
    return pl.pallas_call(
        functools.partial(
            update_kernel, n_t=n_t, groups=groups, width=width, inv_n=1.0 / n_dp, scale=scale
        ),
        grid_spec=pltpu.PrefetchScalarGridSpec(
            num_scalar_prefetch=2,
            grid=(n_t, per),
            in_specs=[
                pl.BlockSpec((blk, outs), lambda r, j, ids, src: (src[r] * per + j, 0)),
                pl.BlockSpec((RANK, blk), lambda r, j, ids, src: (0, src[r] * per + j)),
                pl.BlockSpec((tok, outs), lambda r, j, ids, src: (0, 0)),
            ]
            + [pl.BlockSpec((blk, tok), functools.partial(x_map, n, per)) for n in range(n_t)]
            + [pl.BlockSpec((RANK, width), lambda r, j, ids, src: (0, 0))] * groups,
            out_specs=[
                pl.BlockSpec((blk, outs), lambda r, j, ids, src: (src[r] * per + j, 0)),
                pl.BlockSpec((RANK, outs), lambda r, j, ids, src: (0, 0)),
            ],
            scratch_shapes=[pltpu.VMEM((3 * RANK, outs), BF16)],
        ),
        out_shape=[
            jax.ShapeDtypeStruct(error.shape, F32),
            jax.ShapeDtypeStruct((RANK, outs), F32),
        ],
        compiler_params=params(48),
        cost_estimate=cost(9e9, error.size * 8 + n_t * part * tok * 2),
        name="update_error",
    )(jnp.reshape(me, (1,)), src, error, basis_t, out_grad, *xts, *q_pieces)


def near_kernel(ids, g_ref, gs_ref, w_ref, ws_ref, out):
    out[...] = dot(g_ref[...], w_ref[...], 1, 1) + dot(gs_ref[...], ws_ref[...], 1, 1)


def near_input_grad(me_t, g_own, g_sib, weight, w_sib):
    tok, outs = g_own.shape
    part = w_sib.shape[0]
    blk = 256
    row = pl.BlockSpec((blk, outs), lambda i, ids: (i, 0))
    return pl.pallas_call(
        near_kernel,
        grid_spec=pltpu.PrefetchScalarGridSpec(
            num_scalar_prefetch=1,
            grid=(tok // blk,),
            in_specs=[
                row,
                row,
                pl.BlockSpec((part, outs), lambda i, ids: (ids[0], 0)),
                pl.BlockSpec((part, outs), lambda i, ids: (0, 0)),
            ],
            out_specs=pl.BlockSpec((blk, part), lambda i, ids: (i, 0)),
        ),
        out_shape=jax.ShapeDtypeStruct((tok, part), F32),
        compiler_params=params(32),
        cost_estimate=cost(4 * tok * outs * part, 12e6),
        name="input_grad_near",
    )(jnp.reshape(me_t, (1,)), g_own, g_sib, weight, w_sib)


def far_kernel(*refs):
    prev, w_ref = refs[0], refs[1]
    g_refs, out = refs[2:-1], refs[-1]
    width = g_refs[0].shape[1]
    total = prev[...]
    for n, g in enumerate(g_refs):
        total = total + dot(g[...], w_ref[:, n * width : (n + 1) * width], 1, 1)
    out[...] = total


def far_input_grad(prev, w_far, gs, start):
    rows, outs = gs[0].shape
    tok, part = prev.shape
    blk = 256
    row = pl.BlockSpec((blk, outs), lambda i: (i, 0))
    to = pl.BlockSpec((blk, part), lambda i: (i + start // blk, 0))
    return pl.pallas_call(
        far_kernel,
        grid=(rows // blk,),
        in_specs=[to, pl.BlockSpec(w_far.shape, lambda i: (0, 0))] + [row] * len(gs),
        out_specs=to,
        out_shape=jax.ShapeDtypeStruct((tok, part), F32),
        input_output_aliases={0: 0},
        compiler_params=params(40),
        cost_estimate=cost(2 * len(gs) * rows * outs * part, 10e6),
        name="input_grad_far",
    )(prev, w_far, *gs)


def per_device(activations, out_grad, weight, error, q_start):
    scale = 1.0 / math.sqrt(TOK_DEV)
    n_t = lax.axis_size("tensor")
    n_dp = lax.axis_size("dp")
    chips = n_t // 2
    t = lax.axis_index("tensor").astype(jnp.int32)
    d = lax.axis_index("dp").astype(jnp.int32)
    y, c = t // 2, t % 2
    tok, part = activations.shape
    outs = out_grad.shape[1]
    din = weight.shape[0]
    error = error[0]

    def to_sibling(a):
        return lax.ppermute(a, "tensor", [(i, i ^ 1) for i in range(n_t)])

    def to_chip(a, k):
        return lax.ppermute(
            a, "tensor", [(i, ((i // 2 + k) % chips) * 2 + i % 2) for i in range(n_t)]
        )

    def to_replica(a, k):
        return lax.ppermute(a, "dp", [(i, i ^ k) for i in range(n_dp)])

    src = jnp.stack([((y - k) % chips) * 2 + (c ^ e) for k in range(chips) for e in range(2)])
    src = src.astype(jnp.int32)
    steps = range(1, chips)

    x_t = activations.T
    x_far = [to_chip(x_t, k) for k in steps]
    share = part // n_dp
    w_parts = []
    for k in steps:
        for e in range(2):
            dest = ((y + k) % chips) * 2 + (c ^ e)
            piece = lax.dynamic_slice(weight, (dest * part + d * share, 0), (share, outs))
            w_parts.append(
                lax.ppermute(
                    piece,
                    "tensor",
                    [(i, ((i // 2 + k) % chips) * 2 + ((i % 2) ^ e)) for i in range(n_t)],
                )
            )
    w_far = lax.all_gather(jnp.concatenate(w_parts, axis=1), "dp", axis=0, tiled=True)
    w_sib = to_sibling(lax.dynamic_slice(weight, ((t ^ 1) * part, 0), (part, outs)))
    n_chunk = 2
    rows = tok // n_chunk
    g_far = [
        [to_chip(out_grad[i * rows : (i + 1) * rows], k) for k in steps] for i in range(n_chunk)
    ]
    g_sib = to_sibling(out_grad)

    send, keep, y_t = local_sketch(error, q_start.T, out_grad, c, chips, part)
    got = to_sibling(send)
    y_t = y_t + to_sibling(y_t)
    summed = keep + got
    e_list = [lax.dynamic_index_in_dim(summed, y, 0, keepdims=False)]
    y_list = [y_t]
    for k in steps:
        e_list.append(
            to_chip(lax.dynamic_index_in_dim(summed, (y + k) % chips, 0, keepdims=False), k)
        )
        y_list.append(to_chip(y_t, k))
    direct = part % (n_dp * 128) == 0 and outs % (n_dp * 128) == 0
    groups = n_dp if direct else 1
    me = d if direct else jnp.zeros_like(d)

    def reduce_pieces(pieces):
        if not direct:
            return lax.psum(pieces[0], "dp")
        total = pieces[0]
        for k in range(1, n_dp):
            total = total + to_replica(pieces[k], k)
        return total

    def gather_pieces(piece):
        return [piece] + [to_replica(piece, k) for k in range(1, groups)]

    piece = reduce_pieces(sketch_rows(me, e_list, y_list, activations, groups, scale))
    stacked = jnp.stack([piece] + [to_chip(piece, k) for k in steps])
    other = to_sibling(stacked)
    stacked = jnp.stack([stacked, other], axis=1).reshape(n_t, RANK, part // groups)
    basis_t = make_basis(me, src, gather_pieces(stacked), n_dp, part, din)

    xts = [x_t, to_sibling(x_t)]
    for a in x_far:
        xts += [a, to_sibling(a)]
    piece = reduce_pieces(
        right_factor(me, src, error, basis_t, out_grad, xts, groups, scale)
    )
    new_error, q_t = update_error(
        me, src, error, basis_t, out_grad, xts, gather_pieces(piece), n_dp, scale
    )

    grad = near_input_grad(t, out_grad, g_sib, weight, w_sib)
    for i in range(n_chunk):
        gs = []
        for a in g_far[i]:
            gs += [a, to_sibling(a)]
        grad = far_input_grad(grad, w_far, gs, i * rows)
    return (grad, new_error[None], q_t.T)


def solution(mesh):
    placed = (
        P("dp", "tensor"),
        P("dp", "tensor"),
        P(None, "tensor"),
        P("dp", None, "tensor"),
        P("tensor", None),
    )
    return jax.shard_map(
        per_device,
        mesh=mesh,
        in_specs=placed,
        out_specs=(P("dp", "tensor"), P("dp", None, "tensor"), P("tensor", None)),
        check_vma=False,
    )
```

```python
import functools
import math

import jax
import jax.numpy as jnp
from jax import lax
from jax.experimental import pallas as pl
from jax.experimental.pallas import tpu as pltpu
from jax.sharding import PartitionSpec as P

TOK_DEV = 1024
RANK = 32
MIB = 1 << 20
F32 = jnp.float32
BF16 = jnp.bfloat16


def dot(a, b, ca, cb, precision=None):
    return lax.dot_general(
        a, b, (((ca,), (cb,)), ((), ())), precision=precision, preferred_element_type=F32
    )


def split(a):
    high = a.astype(BF16)
    return high, (a - high.astype(F32)).astype(BF16)


def params(mib):
    return pltpu.CompilerParams(vmem_limit_bytes=mib * MIB)


def cost(flops, nbytes):
    return pl.CostEstimate(flops=int(flops / 16), bytes_accessed=int(nbytes / 16), transcendentals=0)


def project_kernel(g_ref, qt_ref, y_ref):
    both = dot(jnp.concatenate(split(qt_ref[...]), axis=0), g_ref[...], 1, 1)
    y_ref[...] = both[0:RANK, :] + both[RANK:, :]


def project(out_grad, q_t):
    vm = pl.BlockSpec(memory_space=pltpu.VMEM)
    return pl.pallas_call(
        project_kernel,
        in_specs=[vm, vm],
        out_specs=vm,
        out_shape=jax.ShapeDtypeStruct((RANK, out_grad.shape[0]), F32),
        compiler_params=params(24),
        cost_estimate=cost(1e9, 2e6),
        name="project",
    )(out_grad, q_t)


def sketch_kernel(e_ref, qt_ref, s_ref, qs_ref, *, width):
    @pl.when((pl.program_id(0) == 0) & (pl.program_id(1) == 0))
    def _():
        high, low = split(qt_ref[...])
        qs_ref[0:RANK, :] = high
        qs_ref[RANK : 2 * RANK, :] = low

    high, low = split(e_ref[...])
    main = dot(high, qs_ref[...], 1, 1)
    rest = dot(low, qs_ref[0:RANK, :], 1, 1)
    rows = (main[:, 0:RANK] + main[:, RANK : 2 * RANK] + rest).T
    for k in range(s_ref.shape[0]):
        s_ref[k, 0] = rows[:, k * width : (k + 1) * width]


def local_sketch(error, q_t, n_dp, n_t, part):
    blk = min(512, part)
    per = part // blk
    width = part // n_dp
    outs = error.shape[1]
    return pl.pallas_call(
        functools.partial(sketch_kernel, width=width),
        grid=(n_t, per),
        in_specs=[
            pl.BlockSpec((blk, outs), lambda s, j: (s * per + j, 0)),
            pl.BlockSpec((RANK, outs), lambda s, j: (0, 0)),
        ],
        out_specs=pl.BlockSpec((n_dp // per, 1, RANK, width), lambda s, j: (j, s, 0, 0)),
        out_shape=jax.ShapeDtypeStruct((n_dp, n_t, RANK, width), F32),
        scratch_shapes=[pltpu.VMEM((2 * RANK, outs), BF16)],
        compiler_params=params(48),
        cost_estimate=cost(6e9, error.size * 4),
        name="error_sketch",
    )(error, q_t)


def sketch_rows_kernel(*refs, scale, width):
    s_ref, x_ref = refs[1], refs[2]
    y_refs, out = refs[3:-1], refs[-1]
    y = y_refs[0][...]
    for r in y_refs[1:]:
        y = y + r[...]
    both = dot(jnp.concatenate(split(y), axis=0), x_ref[...], 1, 0)
    total = (both[0:RANK, :] + both[RANK:, :]) * scale
    for k in range(out.shape[0]):
        out[k, 0] = s_ref[k, 0] + total[:, k * width : (k + 1) * width]


def sketch_rows(t, blocks, acts, y_list, scale):
    tok, part = acts.shape
    n_dp, n_t, _, width = blocks.shape
    own = pl.BlockSpec((n_dp, 1, RANK, width), lambda i, ids: (0, ids[0], 0, 0))
    whole = lambda i, ids: (0, 0)
    return pl.pallas_call(
        functools.partial(sketch_rows_kernel, scale=scale, width=width),
        grid_spec=pltpu.PrefetchScalarGridSpec(
            num_scalar_prefetch=1,
            grid=(1,),
            in_specs=[own, pl.BlockSpec((tok, part), whole)]
            + [pl.BlockSpec((RANK, tok), whole)] * len(y_list),
            out_specs=own,
        ),
        out_shape=jax.ShapeDtypeStruct(blocks.shape, F32),
        input_output_aliases={1: 0},
        compiler_params=params(24),
        cost_estimate=cost(1e9, 3e6),
        name="sketch_rows",
    )(jnp.reshape(t, (1,)), blocks, acts, *y_list)


def basis_kernel(pieces, out, sk, *, n_dp, n_t, width, part):
    for s in range(n_t):
        for k in range(n_dp):
            at = s * part + k * width
            sk[:, at : at + width] = pieces[k * n_t + s] * (1.0 / n_dp)
    s = sk[...]
    gram = dot(s, s, 1, 1, lax.Precision.HIGHEST)
    row = lax.broadcasted_iota(jnp.int32, (RANK, RANK), 0)
    col = lax.broadcasted_iota(jnp.int32, (RANK, RANK), 1)
    eye = (row == col).astype(F32)
    m = jnp.concatenate([gram, eye, jnp.zeros((RANK, 2 * RANK), F32)], axis=1)
    index = lax.broadcasted_iota(jnp.int32, (RANK, 1), 0)
    for j in range(RANK - 1):
        factor = jnp.where(index > j, m[:, j : j + 1] / m[j : j + 1, j : j + 1], 0.0)
        m = m - factor * m[j : j + 1, :]
    diag = jnp.sum(jnp.where(row == col, m[:, 0:RANK], 0.0), axis=1, keepdims=True)
    inverse = m[:, RANK : 2 * RANK] / jnp.sqrt(diag)
    out[...] = dot(inverse, s, 1, 0, lax.Precision.HIGHEST)


def make_basis(pieces, n_dp, n_t, part, din):
    width = pieces.shape[2]
    vm = pl.BlockSpec(memory_space=pltpu.VMEM)
    return pl.pallas_call(
        functools.partial(basis_kernel, n_dp=n_dp, n_t=n_t, width=width, part=part),
        in_specs=[vm],
        out_specs=vm,
        out_shape=jax.ShapeDtypeStruct((RANK, din), F32),
        scratch_shapes=[pltpu.VMEM((RANK, din), F32)],
        compiler_params=params(24),
        cost_estimate=cost(6e9, 2e6),
        name="basis",
    )(pieces)


def right_error_kernel(e_ref, b_ref, acc):
    @pl.when(pl.program_id(0) == 0)
    def _():
        acc[...] = jnp.zeros_like(acc)

    bh, bl = split(b_ref[...])
    eh, el = split(e_ref[...])
    main = dot(jnp.concatenate([bh, bl], axis=0), eh, 1, 0)
    acc[...] += main[0:RANK, :] + main[RANK:, :] + dot(bh, el, 1, 0)


def right_error(error, basis_t):
    din, outs = error.shape
    blk = 512
    return pl.pallas_call(
        right_error_kernel,
        grid=(din // blk,),
        in_specs=[
            pl.BlockSpec((blk, outs), lambda i: (i, 0)),
            pl.BlockSpec((RANK, blk), lambda i: (0, i)),
        ],
        out_specs=pl.BlockSpec((RANK, outs), lambda i: (0, 0)),
        out_shape=jax.ShapeDtypeStruct((RANK, outs), F32),
        compiler_params=params(48),
        cost_estimate=cost(8e9, error.size * 4),
        name="right_error",
    )(error, basis_t)


def right_grad_kernel(*refs, n_t, n_out, scale):
    src, b_ref, r_ref, g_ref = refs[0:4]
    x_refs = refs[4 : 4 + n_t]
    out, vacc = refs[4 + n_t :]
    r = pl.program_id(0)

    @pl.when(r == 0)
    def _():
        vacc[...] = jnp.zeros_like(vacc)

    both = jnp.concatenate(split(b_ref[...]), axis=0)
    for n in range(n_t):

        @pl.when(r == n)
        def _(n=n):
            v = dot(both, x_refs[n][...], 1, 0)
            vacc[...] += v[0:RANK, :] + v[RANK:, :]

    @pl.when(r == n_t - 1)
    def _():
        w = dot(jnp.concatenate(split(vacc[...]), axis=0), g_ref[...], 1, 0)
        total = r_ref[...] + (w[0:RANK, :] + w[RANK:, :]) * scale
        width = total.shape[1] // n_out
        for k in range(n_out):
            out[k] = total[:, k * width : (k + 1) * width]


def right_grad(src, basis_t, right_e, out_grad, xts, n_out, scale):
    part, tok = xts[0].shape
    outs = out_grad.shape[1]
    n_t = len(xts)
    same = lambda r, src: (0, 0)
    return pl.pallas_call(
        functools.partial(right_grad_kernel, n_t=n_t, n_out=n_out, scale=scale),
        grid_spec=pltpu.PrefetchScalarGridSpec(
            num_scalar_prefetch=1,
            grid=(n_t,),
            in_specs=[
                pl.BlockSpec((RANK, part), lambda r, src: (0, src[r])),
                pl.BlockSpec((RANK, outs), same),
                pl.BlockSpec((tok, outs), same),
            ]
            + [pl.BlockSpec((part, tok), same)] * n_t,
            out_specs=pl.BlockSpec((n_out, RANK, outs // n_out), lambda r, src: (0, 0, 0)),
            scratch_shapes=[pltpu.VMEM((RANK, tok), F32)],
        ),
        out_shape=jax.ShapeDtypeStruct((n_out, RANK, outs // n_out), F32),
        compiler_params=params(40),
        cost_estimate=cost(4e9, n_t * part * tok * 2),
        name="right_grad",
    )(src, basis_t, right_e, out_grad, *xts)


def x_map(n, per, r, j, *_):
    return (jnp.clip((r - n) * per + j, 0, per - 1), 0)


def right_factor(me, src, error, basis_t, out_grad, xts, n_out, scale):
    part = xts[0].shape[0]
    tok, outs = out_grad.shape
    n_t = len(xts)
    blk = min(512, part)
    per = part // blk
    return pl.pallas_call(
        functools.partial(right_kernel, n_t=n_t, per=per, n_out=n_out, scale=scale),
        grid_spec=pltpu.PrefetchScalarGridSpec(
            num_scalar_prefetch=2,
            grid=(n_t, per),
            in_specs=[
                pl.BlockSpec((blk, outs), lambda r, j, ids, src: (src[r] * per + j, 0)),
                pl.BlockSpec((RANK, blk), lambda r, j, ids, src: (0, src[r] * per + j)),
                pl.BlockSpec((tok, outs), lambda r, j, ids, src: (0, 0)),
            ]
            + [pl.BlockSpec((blk, tok), functools.partial(x_map, n, per)) for n in range(n_t)],
            out_specs=[pl.BlockSpec((RANK, outs // n_out), lambda r, j, ids, src: (0, 0))] * n_out,
            scratch_shapes=[pltpu.VMEM((RANK, outs), F32), pltpu.VMEM((RANK, tok), F32)],
        ),
        out_shape=[jax.ShapeDtypeStruct((RANK, outs // n_out), F32)] * n_out,
        compiler_params=params(40),
        cost_estimate=cost(9e9, error.size * 4 + n_t * part * tok * 2),
        name="right_factor",
    )(jnp.reshape(me, (1,)), src, error, basis_t, out_grad, *xts)


def update_kernel(*refs, n_t, n_dp, scale):
    e_ref, b_ref, g_ref, q_ref = refs[1:5]
    x_refs = refs[5 : 5 + n_t]
    out, qt_out, qs = refs[5 + n_t :]
    r, j = pl.program_id(0), pl.program_id(1)

    @pl.when((r == 0) & (j == 0))
    def _():
        q_t = jnp.concatenate([q_ref[k] for k in range(n_dp)], axis=1) * (1.0 / n_dp)
        qt_out[...] = q_t
        high, low = split(q_t)
        qs[0:RANK, :] = high
        qs[RANK : 2 * RANK, :] = low
        qs[2 * RANK : 3 * RANK, :] = high

    bh, bl = split(b_ref[...].T)
    both = jnp.concatenate([bh, bh, bl], axis=1)
    for n in range(n_t):

        @pl.when(r == n)
        def _(n=n):
            out[...] = (
                e_ref[...]
                + dot(x_refs[n][...], g_ref[...], 1, 0) * scale
                - dot(both, qs[...], 1, 0)
            )


def update_error(src, error, basis_t, out_grad, xts, q_pieces, n_dp, scale):
    part = xts[0].shape[0]
    tok, outs = out_grad.shape
    n_t = len(xts)
    blk = min(512, part)
    per = part // blk
    return pl.pallas_call(
        functools.partial(update_kernel, n_t=n_t, n_dp=n_dp, scale=scale),
        grid_spec=pltpu.PrefetchScalarGridSpec(
            num_scalar_prefetch=1,
            grid=(n_t, per),
            in_specs=[
                pl.BlockSpec((blk, outs), lambda r, j, src: (src[r] * per + j, 0)),
                pl.BlockSpec((RANK, blk), lambda r, j, src: (0, src[r] * per + j)),
                pl.BlockSpec((tok, outs), lambda r, j, src: (0, 0)),
                pl.BlockSpec(q_pieces.shape, lambda r, j, src: (0, 0, 0)),
            ]
            + [pl.BlockSpec((blk, tok), functools.partial(x_map, n, per)) for n in range(n_t)],
            out_specs=[
                pl.BlockSpec((blk, outs), lambda r, j, src: (src[r] * per + j, 0)),
                pl.BlockSpec((RANK, outs), lambda r, j, src: (0, 0)),
            ],
            scratch_shapes=[pltpu.VMEM((3 * RANK, outs), BF16)],
        ),
        out_shape=[
            jax.ShapeDtypeStruct(error.shape, F32),
            jax.ShapeDtypeStruct((RANK, outs), F32),
        ],
        compiler_params=params(48),
        cost_estimate=cost(9e9, error.size * 8 + n_t * part * tok * 2),
        name="update_error",
    )(src, error, basis_t, out_grad, q_pieces, *xts)


def near_kernel(ids, g_ref, gs_ref, w_ref, ws_ref, out):
    out[...] = dot(g_ref[...], w_ref[...], 1, 1) + dot(gs_ref[...], ws_ref[...], 1, 1)


def near_input_grad(me_t, g_own, g_sib, weight, w_sib):
    tok, outs = g_own.shape
    part = w_sib.shape[0]
    blk = 256
    row = pl.BlockSpec((blk, outs), lambda i, ids: (i, 0))
    return pl.pallas_call(
        near_kernel,
        grid_spec=pltpu.PrefetchScalarGridSpec(
            num_scalar_prefetch=1,
            grid=(tok // blk,),
            in_specs=[
                row,
                row,
                pl.BlockSpec((part, outs), lambda i, ids: (ids[0], 0)),
                pl.BlockSpec((part, outs), lambda i, ids: (0, 0)),
            ],
            out_specs=pl.BlockSpec((blk, part), lambda i, ids: (i, 0)),
        ),
        out_shape=jax.ShapeDtypeStruct((tok, part), F32),
        compiler_params=params(58),
        cost_estimate=cost(4 * tok * outs * part, 12e6),
        name="input_grad_near",
    )(jnp.reshape(me_t, (1,)), g_own, g_sib, weight, w_sib)


def far_kernel(*refs):
    prev, w_ref = refs[0], refs[1]
    g_refs, out = refs[2:-1], refs[-1]
    width = g_refs[0].shape[1]
    total = prev[...]
    for n, g in enumerate(g_refs):
        total = total + dot(g[...], w_ref[:, n * width : (n + 1) * width], 1, 1)
    out[...] = total


def far_input_grad(prev, w_far, gs, start):
    rows, outs = gs[0].shape
    tok, part = prev.shape
    blk = 256
    row = pl.BlockSpec((blk, outs), lambda i: (i, 0))
    to = pl.BlockSpec((blk, part), lambda i: (i + start // blk, 0))
    return pl.pallas_call(
        far_kernel,
        grid=(rows // blk,),
        in_specs=[to, pl.BlockSpec(w_far.shape, lambda i: (0, 0))] + [row] * len(gs),
        out_specs=to,
        out_shape=jax.ShapeDtypeStruct((tok, part), F32),
        input_output_aliases={0: 0},
        compiler_params=params(40),
        cost_estimate=cost(2 * len(gs) * rows * outs * part, 10e6),
        name="input_grad_far",
    )(prev, w_far, *gs)


def after(value, *others):
    return lax.optimization_barrier((value, others))[0]


def per_device(activations, out_grad, weight, error, q_start):
    scale = 1.0 / math.sqrt(TOK_DEV)
    n_t = lax.axis_size("tensor")
    n_dp = lax.axis_size("dp")
    chips = n_t // 2
    t = lax.axis_index("tensor").astype(jnp.int32)
    d = lax.axis_index("dp").astype(jnp.int32)
    y, c = t // 2, t % 2
    tok, part = activations.shape
    outs = out_grad.shape[1]
    din = weight.shape[0]
    error = error[0]
    q_t = q_start.T

    def to_sibling(a):
        return lax.ppermute(a, "tensor", [(i, i ^ 1) for i in range(n_t)])

    def to_chip(a, k, flip=0):
        pairs = [(i, ((i // 2 + k) % chips) * 2 + ((i % 2) ^ flip)) for i in range(n_t)]
        return lax.ppermute(a, "tensor", pairs)

    def exchange(a, axes):
        return lax.all_to_all(a, axes, 0, 0, tiled=True)

    def everywhere(a, axes, n):
        return exchange(jnp.broadcast_to(a, (n, *a.shape)), axes)

    src = jnp.stack([((y - k) % chips) * 2 + (c ^ e) for k in range(chips) for e in range(2)])
    src = src.astype(jnp.int32)
    steps = range(1, chips)

    share = part // n_dp
    pieces = []
    for k in steps:
        for e in range(2):
            dest = ((y + k) % chips) * 2 + (c ^ e)
            piece = lax.dynamic_slice(weight, (dest * part + d * share, 0), (share, outs))
            pieces.append(piece)
    x_t = after(activations, *pieces).T
    w_parts = [to_chip(p, k, e) for p, (k, e) in zip(pieces, [(k, e) for k in steps for e in range(2)])]
    x_far = [to_chip(x_t, k) for k in steps]
    n_chunk = 4
    rows = tok // n_chunk
    g_rows = after(out_grad, x_t)
    g_rows = [g_rows[i * rows : (i + 1) * rows] for i in range(n_chunk)]
    g_far = [[to_chip(a, k) for k in steps] for a in g_rows]
    w_far = lax.all_gather(jnp.concatenate(w_parts, axis=1), "dp", axis=0, tiled=True)
    w_sib = to_sibling(lax.dynamic_slice(weight, ((t ^ 1) * part, 0), (part, outs)))
    g_sib = to_sibling(out_grad)
    x_sib = to_sibling(x_t)

    y_t = project(out_grad, after(q_t, *g_rows))
    y_t = y_t + to_sibling(y_t)
    y_list = [y_t] + [to_chip(y_t, k) for k in steps]
    blocks = local_sketch(error, q_t, n_dp, n_t, part)
    blocks = sketch_rows(t, blocks, activations, y_list, scale)
    axes = ("dp", "tensor")
    n = n_dp * n_t
    blocks = exchange(blocks.reshape(n, RANK, part // n_dp), axes)
    pieces = everywhere(jnp.sum(blocks, axis=0), axes, n)
    basis_t = make_basis(pieces, n_dp, n_t, part, din)
    right_e = right_error(error, basis_t)
    grad = near_input_grad(t, out_grad, g_sib, weight, after(w_sib, right_e))

    xts = [x_t, x_sib]
    for a in x_far:
        a = after(a, grad)
        xts += [a, to_sibling(a)]
    right = right_grad(src, basis_t, right_e, out_grad, xts, n_dp, scale)
    right = jnp.sum(exchange(right, "dp"), axis=0)
    new_error, q_t = update_error(
        src, error, basis_t, out_grad, xts, everywhere(right, "dp", n_dp), n_dp, scale
    )

    for i in range(n_chunk):
        gs = []
        for a in g_far[i]:
            a = after(a, q_t)
            gs += [a, to_sibling(a)]
        grad = far_input_grad(grad, w_far, gs, i * rows)
    return (grad, new_error[None], q_t.T)


def solution(mesh):
    placed = (
        P("dp", "tensor"),
        P("dp", "tensor"),
        P(None, "tensor"),
        P("dp", None, "tensor"),
        P("tensor", None),
    )
    return jax.shard_map(
        per_device,
        mesh=mesh,
        in_specs=placed,
        out_specs=(P("dp", "tensor"), P("dp", None, "tensor"), P("tensor", None)),
        check_vma=False,
    )
```

```python
import functools
import math

import jax
import jax.numpy as jnp
from jax import lax
from jax.experimental import pallas as pl
from jax.experimental.pallas import tpu as pltpu
from jax.sharding import PartitionSpec as P

TOK_DEV = 1024
RANK = 32
MIB = 1 << 20
F32 = jnp.float32
BF16 = jnp.bfloat16


def dot(a, b, ca, cb, precision=None):
    return lax.dot_general(
        a, b, (((ca,), (cb,)), ((), ())), precision=precision, preferred_element_type=F32
    )


def split(a):
    high = a.astype(BF16)
    return high, (a - high.astype(F32)).astype(BF16)


def params(mib):
    return pltpu.CompilerParams(vmem_limit_bytes=mib * MIB)


def cost(flops, nbytes):
    return pl.CostEstimate(flops=int(flops / 1000), bytes_accessed=int(nbytes / 1000), transcendentals=0)


def project_kernel(g_ref, qt_ref, y_ref):
    both = dot(jnp.concatenate(split(qt_ref[...]), axis=0), g_ref[...], 1, 1)
    y_ref[...] = both[0:RANK, :] + both[RANK:, :]


def project(out_grad, q_t):
    vm = pl.BlockSpec(memory_space=pltpu.VMEM)
    return pl.pallas_call(
        project_kernel,
        in_specs=[vm, vm],
        out_specs=vm,
        out_shape=jax.ShapeDtypeStruct((RANK, out_grad.shape[0]), F32),
        compiler_params=params(24),
        cost_estimate=cost(1e9, 2e6),
        name="project",
    )(out_grad, q_t)


def sketch_kernel(ids, e_ref, qt_ref, send_ref, keep_ref, qs_ref, *, width):
    phase = pl.program_id(0)

    @pl.when((phase == 0) & (pl.program_id(1) == 0) & (pl.program_id(2) == 0))
    def _():
        high, low = split(qt_ref[...])
        qs_ref[0:RANK, :] = high
        qs_ref[RANK : 2 * RANK, :] = low

    high, low = split(e_ref[...])
    main = dot(high, qs_ref[...], 1, 1)
    rest = dot(low, qs_ref[0:RANK, :], 1, 1)
    rows = (main[:, 0:RANK] + main[:, RANK : 2 * RANK] + rest).T

    @pl.when(phase == 0)
    def _():
        for k in range(send_ref.shape[0]):
            send_ref[k, 0] = rows[:, k * width : (k + 1) * width]

    @pl.when(phase == 1)
    def _():
        for k in range(keep_ref.shape[0]):
            keep_ref[k, 0] = rows[:, k * width : (k + 1) * width]


def local_sketch(core, error, q_t, n_dp, chips, part):
    blk = min(512, part)
    per = part // blk
    width = part // n_dp
    outs = error.shape[1]

    def e_map(p, y, j, ids):
        return ((2 * y + jnp.where(p == 0, 1 - ids[0], ids[0])) * per + j, 0)

    def send_map(p, y, j, ids):
        return (jnp.where(p == 0, j, per - 1), jnp.where(p == 0, y, chips - 1), 0, 0)

    def keep_map(p, y, j, ids):
        return (jnp.where(p == 1, j, 0), jnp.where(p == 1, y, 0), 0, 0)

    half = jax.ShapeDtypeStruct((n_dp, chips, RANK, width), F32)
    return pl.pallas_call(
        functools.partial(sketch_kernel, width=width),
        grid_spec=pltpu.PrefetchScalarGridSpec(
            num_scalar_prefetch=1,
            grid=(2, chips, per),
            in_specs=[
                pl.BlockSpec((blk, outs), e_map),
                pl.BlockSpec((RANK, outs), lambda p, y, j, ids: (0, 0)),
            ],
            out_specs=[
                pl.BlockSpec((n_dp // per, 1, RANK, width), send_map),
                pl.BlockSpec((n_dp // per, 1, RANK, width), keep_map),
            ],
            scratch_shapes=[pltpu.VMEM((2 * RANK, outs), BF16)],
        ),
        out_shape=[half, half],
        compiler_params=params(48),
        cost_estimate=cost(6e9, error.size * 4),
        name="error_sketch",
    )(jnp.reshape(core, (1,)), error, q_t)


def sketch_rows_kernel(*refs, scale, width):
    chip, keep, got, x_ref = refs[0:4]
    y_refs, out = refs[4:-1], refs[-1]
    y = y_refs[0][...]
    for r in y_refs[1:]:
        y = y + r[...]
    both = dot(jnp.concatenate(split(y), axis=0), x_ref[...], 1, 0)
    total = (both[0:RANK, :] + both[RANK:, :]) * scale
    out[...] = keep[...] + got[...]
    for k in range(out.shape[0]):
        out[k, chip[0]] += total[:, k * width : (k + 1) * width]


def sketch_rows(chip, keep, got, acts, y_list, scale):
    vm = pl.BlockSpec(memory_space=pltpu.VMEM)
    return pl.pallas_call(
        functools.partial(sketch_rows_kernel, scale=scale, width=keep.shape[3]),
        in_specs=[pl.BlockSpec(memory_space=pltpu.SMEM)] + [vm] * (3 + len(y_list)),
        out_specs=vm,
        out_shape=jax.ShapeDtypeStruct(keep.shape, F32),
        compiler_params=params(24),
        cost_estimate=cost(1e9, 3e6),
        name="sketch_rows",
    )(jnp.reshape(chip, (1,)), keep, got, acts, *y_list)


def basis_kernel(core, mine, other, out, sk, *, n_dp, chips, width, part):
    first = core[0] == 0
    for k in range(n_dp):
        for y in range(chips):
            a, b = mine[k * chips + y], other[k * chips + y]
            for e in range(2):
                at = (2 * y + e) * part + k * width
                block = jnp.where(first, a, b) if e == 0 else jnp.where(first, b, a)
                sk[:, at : at + width] = block * (1.0 / n_dp)
    s = sk[...]
    gram = dot(s, s, 1, 1, lax.Precision.HIGHEST)
    row = lax.broadcasted_iota(jnp.int32, (RANK, RANK), 0)
    col = lax.broadcasted_iota(jnp.int32, (RANK, RANK), 1)
    eye = (row == col).astype(F32)
    m = jnp.concatenate([gram, eye, jnp.zeros((RANK, 2 * RANK), F32)], axis=1)
    index = lax.broadcasted_iota(jnp.int32, (RANK, 1), 0)
    for j in range(RANK - 1):
        factor = jnp.where(index > j, m[:, j : j + 1] / m[j : j + 1, j : j + 1], 0.0)
        m = m - factor * m[j : j + 1, :]
    diag = jnp.sum(jnp.where(row == col, m[:, 0:RANK], 0.0), axis=1, keepdims=True)
    inverse = m[:, RANK : 2 * RANK] / jnp.sqrt(diag)
    out[...] = dot(inverse, s, 1, 0, lax.Precision.HIGHEST)


def make_basis(core, mine, other, n_dp, chips, part, din):
    width = mine.shape[2]
    vm = pl.BlockSpec(memory_space=pltpu.VMEM)
    return pl.pallas_call(
        functools.partial(basis_kernel, n_dp=n_dp, chips=chips, width=width, part=part),
        in_specs=[pl.BlockSpec(memory_space=pltpu.SMEM), vm, vm],
        out_specs=vm,
        out_shape=jax.ShapeDtypeStruct((RANK, din), F32),
        scratch_shapes=[pltpu.VMEM((RANK, din), F32)],
        compiler_params=params(24),
        cost_estimate=cost(6e9, 2e6),
        name="basis",
    )(jnp.reshape(core, (1,)), mine, other)


def right_error_kernel(e_ref, b_ref, acc):
    @pl.when(pl.program_id(0) == 0)
    def _():
        acc[...] = jnp.zeros_like(acc)

    bh, bl = split(b_ref[...])
    eh, el = split(e_ref[...])
    main = dot(jnp.concatenate([bh, bl], axis=0), eh, 1, 0)
    acc[...] += main[0:RANK, :] + main[RANK:, :] + dot(bh, el, 1, 0)


def right_error(error, basis_t):
    din, outs = error.shape
    blk = 512
    return pl.pallas_call(
        right_error_kernel,
        grid=(din // blk,),
        in_specs=[
            pl.BlockSpec((blk, outs), lambda i: (i, 0)),
            pl.BlockSpec((RANK, blk), lambda i: (0, i)),
        ],
        out_specs=pl.BlockSpec((RANK, outs), lambda i: (0, 0)),
        out_shape=jax.ShapeDtypeStruct((RANK, outs), F32),
        compiler_params=params(48),
        cost_estimate=cost(8e9, error.size * 4),
        name="right_error",
    )(error, basis_t)


def piece_specs(pieces, blk):
    specs, ranges, first = [], [], 0
    for p in pieces:
        count = p.shape[0] // blk

        def at(i, rows, first=first, count=count):
            return (jnp.clip(i - first, 0, count - 1), 0)

        specs.append(pl.BlockSpec((blk, p.shape[1]), at))
        ranges.append((first, first + count))
        first += count
    return specs, ranges


def right_grad_kernel(*refs, ranges, n_out, scale):
    b_ref, r_ref, g_ref = refs[1:4]
    x_refs = refs[4 : 4 + len(ranges)]
    out, vacc = refs[4 + len(ranges) :]
    i = pl.program_id(0)

    @pl.when(i == 0)
    def _():
        vacc[...] = jnp.zeros_like(vacc)

    both = jnp.concatenate(split(b_ref[...]), axis=0)
    for x_ref, (lo, hi) in zip(x_refs, ranges):

        @pl.when((i >= lo) & (i < hi))
        def _(x_ref=x_ref):
            v = dot(both, x_ref[...], 1, 0)
            vacc[...] += v[0:RANK, :] + v[RANK:, :]

    @pl.when(i == ranges[-1][1] - 1)
    def _():
        w = dot(jnp.concatenate(split(vacc[...]), axis=0), g_ref[...], 1, 0)
        total = r_ref[...] + (w[0:RANK, :] + w[RANK:, :]) * scale
        width = total.shape[1] // n_out
        for k in range(n_out):
            out[k] = total[:, k * width : (k + 1) * width]


def right_grad(rows, basis_t, right_e, out_grad, pieces, blk, n_out, scale):
    tok, outs = out_grad.shape
    same = lambda i, rows: (0, 0)
    specs, ranges = piece_specs(pieces, blk)
    return pl.pallas_call(
        functools.partial(right_grad_kernel, ranges=ranges, n_out=n_out, scale=scale),
        grid_spec=pltpu.PrefetchScalarGridSpec(
            num_scalar_prefetch=1,
            grid=(ranges[-1][1],),
            in_specs=[
                pl.BlockSpec((RANK, blk), lambda i, rows: (0, rows[i])),
                pl.BlockSpec((RANK, outs), same),
                pl.BlockSpec((tok, outs), same),
            ]
            + specs,
            out_specs=pl.BlockSpec((n_out, RANK, outs // n_out), lambda i, rows: (0, 0, 0)),
            scratch_shapes=[pltpu.VMEM((RANK, tok), F32)],
        ),
        out_shape=jax.ShapeDtypeStruct((n_out, RANK, outs // n_out), F32),
        compiler_params=params(48),
        cost_estimate=cost(4e9, basis_t.shape[1] * tok * 2),
        name="right_grad",
    )(rows, basis_t, right_e, out_grad, *pieces)


def update_kernel(*refs, ranges, n_dp, scale):
    e_ref, b_ref, g_ref, q_ref = refs[1:5]
    x_refs = refs[5 : 5 + len(ranges)]
    out, qt_out, qs = refs[5 + len(ranges) :]
    i = pl.program_id(0)

    @pl.when(i == 0)
    def _():
        q_t = jnp.concatenate([q_ref[k] for k in range(n_dp)], axis=1) * (1.0 / n_dp)
        qt_out[...] = q_t
        high, low = split(q_t)
        qs[0:RANK, :] = high
        qs[RANK : 2 * RANK, :] = low
        qs[2 * RANK : 3 * RANK, :] = high

    bh, bl = split(b_ref[...].T)
    both = jnp.concatenate([bh, bh, bl], axis=1)
    for x_ref, (lo, hi) in zip(x_refs, ranges):

        @pl.when((i >= lo) & (i < hi))
        def _(x_ref=x_ref):
            out[...] = (
                e_ref[...]
                + dot(x_ref[...], g_ref[...], 1, 0) * scale
                - dot(both, qs[...], 1, 0)
            )


def update_error(rows, error, basis_t, out_grad, pieces, blk, q_pieces, n_dp, scale):
    tok, outs = out_grad.shape
    specs, ranges = piece_specs(pieces, blk)
    return pl.pallas_call(
        functools.partial(update_kernel, ranges=ranges, n_dp=n_dp, scale=scale),
        grid_spec=pltpu.PrefetchScalarGridSpec(
            num_scalar_prefetch=1,
            grid=(ranges[-1][1],),
            in_specs=[
                pl.BlockSpec((blk, outs), lambda i, rows: (rows[i], 0)),
                pl.BlockSpec((RANK, blk), lambda i, rows: (0, rows[i])),
                pl.BlockSpec((tok, outs), lambda i, rows: (0, 0)),
                pl.BlockSpec(q_pieces.shape, lambda i, rows: (0, 0, 0)),
            ]
            + specs,
            out_specs=[
                pl.BlockSpec((blk, outs), lambda i, rows: (rows[i], 0)),
                pl.BlockSpec((RANK, outs), lambda i, rows: (0, 0)),
            ],
            scratch_shapes=[pltpu.VMEM((3 * RANK, outs), BF16)],
        ),
        out_shape=[
            jax.ShapeDtypeStruct(error.shape, F32),
            jax.ShapeDtypeStruct((RANK, outs), F32),
        ],
        compiler_params=params(48),
        cost_estimate=cost(9e9, error.size * 8 + basis_t.shape[1] * tok * 2),
        name="update_error",
    )(rows, error, basis_t, out_grad, q_pieces, *pieces)


def near_kernel(ids, g_ref, gs_ref, w_ref, ws_ref, out):
    out[...] = dot(g_ref[...], w_ref[...], 1, 1) + dot(gs_ref[...], ws_ref[...], 1, 1)


def near_input_grad(me_t, g_own, g_sib, weight, w_sib):
    tok, outs = g_own.shape
    part = w_sib.shape[0]
    blk = min(256, part)
    per = part // blk
    whole = pl.BlockSpec((tok, outs), lambda i, ids: (0, 0))
    return pl.pallas_call(
        near_kernel,
        grid_spec=pltpu.PrefetchScalarGridSpec(
            num_scalar_prefetch=1,
            grid=(per,),
            in_specs=[
                whole,
                whole,
                pl.BlockSpec((blk, outs), lambda i, ids: (ids[0] * per + i, 0)),
                pl.BlockSpec((blk, outs), lambda i, ids: (i, 0)),
            ],
            out_specs=pl.BlockSpec((tok, blk), lambda i, ids: (0, i)),
        ),
        out_shape=jax.ShapeDtypeStruct((tok, part), F32),
        compiler_params=params(48),
        cost_estimate=cost(4 * tok * outs * part, 12e6),
        name="input_grad_near",
    )(jnp.reshape(me_t, (1,)), g_own, g_sib, weight, w_sib)


def far_kernel(*refs):
    prev, w_ref = refs[0], refs[1]
    g_refs, out = refs[2:-1], refs[-1]
    width = g_refs[0].shape[1]
    total = prev[...]
    for n, g in enumerate(g_refs):
        total = total + dot(g[...], w_ref[:, n * width : (n + 1) * width], 1, 1)
    out[...] = total


def far_input_grad(prev, w_far, gs, start):
    rows, outs = gs[0].shape
    tok, part = prev.shape
    blk = min(256, part)
    to = pl.BlockSpec((rows, blk), lambda i: (start // rows, i))
    return pl.pallas_call(
        far_kernel,
        grid=(part // blk,),
        in_specs=[to, pl.BlockSpec((blk, w_far.shape[1]), lambda i: (i, 0))]
        + [pl.BlockSpec((rows, outs), lambda i: (0, 0))] * len(gs),
        out_specs=to,
        out_shape=jax.ShapeDtypeStruct((tok, part), F32),
        input_output_aliases={0: 0},
        compiler_params=params(48),
        cost_estimate=cost(2 * len(gs) * rows * outs * part, 10e6),
        name="input_grad_far",
    )(prev, w_far, *gs)


def after(value, *others):
    return lax.optimization_barrier((value, others))[0]


def per_device(activations, out_grad, weight, error, q_start):
    scale = 1.0 / math.sqrt(TOK_DEV)
    n_dp = lax.axis_size("dp")
    chips = lax.axis_size("chip")
    n_t = 2 * chips
    d = lax.axis_index("dp").astype(jnp.int32)
    y = lax.axis_index("chip").astype(jnp.int32)
    c = lax.axis_index("core").astype(jnp.int32)
    t = 2 * y + c
    tok, part = activations.shape
    outs = out_grad.shape[1]
    din = weight.shape[0]
    error = error[0]
    q_t = q_start.T
    steps = range(1, chips)
    share = part // n_dp
    spread = ("dp", "chip")
    n = n_dp * chips

    def to_sibling(a):
        return lax.ppermute(a, "core", [(0, 1), (1, 0)])

    def to_chip(a, k, flip=0):
        pairs = [(i, ((i // 2 + k) % chips) * 2 + ((i % 2) ^ flip)) for i in range(n_t)]
        return lax.ppermute(a, ("chip", "core"), pairs)

    def exchange(a, axes):
        return lax.all_to_all(a, axes, 0, 0, tiled=True)

    def everywhere(a, axes, n):
        return exchange(jnp.broadcast_to(a, (n, *a.shape)), axes)

    moves = [(k, e) for k in steps for e in range(2)]
    w_parts = []
    for k, e in moves:
        dest = ((y + k) % chips) * 2 + (c ^ e)
        w_parts.append(lax.dynamic_slice(weight, (dest * part + d * share, 0), (share, outs)))
    x_t = after(activations, *w_parts).T
    w_parts = [to_chip(a, k, e) for a, (k, e) in zip(w_parts, moves)]
    blk = min(512, part)
    per = part // blk
    x_far = [[to_chip(x_t[j * blk : (j + 1) * blk], k) for k in steps] for j in range(per)]

    y_t = project(out_grad, after(q_t, x_t))
    y_t = y_t + to_sibling(y_t)
    y_list = [y_t] + [to_chip(y_t, k) for k in steps]
    send, keep = local_sketch(c, error, after(q_t, y_t), n_dp, chips, part)
    w_parts = jnp.concatenate([after(a, send) for a in w_parts], axis=1)
    blocks = sketch_rows(y, keep, to_sibling(send), activations, after(y_list, w_parts), scale)
    w_far = lax.all_gather(w_parts, "dp", axis=0, tiled=True)

    g_sib = to_sibling(out_grad)
    w_sib = to_sibling(lax.dynamic_slice(after(weight, send), ((t ^ 1) * part, 0), (part, outs)))
    grad = near_input_grad(t, out_grad, g_sib, weight, after(w_sib, blocks))

    blocks = exchange(blocks.reshape(n, RANK, share), spread)
    x_far[0] = after(x_far[0], grad)
    mine = everywhere(after(jnp.sum(blocks, axis=0), x_far[0]), spread, n)
    basis_t = make_basis(c, mine, to_sibling(mine), n_dp, chips, part, din)
    right_e = right_error(error, basis_t)

    pieces = [x_t, to_sibling(x_t)]
    rows = [(2 * y + (c ^ e)) * per + j for e in range(2) for j in range(per)]
    for j in range(per):
        if j > 0:
            x_far[j] = after(x_far[j], right_e)
        for k, a in zip(steps, x_far[j]):
            for e in range(2):
                pieces.append(to_sibling(a) if e else a)
                rows.append((2 * ((y - k) % chips) + (c ^ e)) * per + j)
    rows = jnp.stack(rows).astype(jnp.int32)

    n_chunk = 2
    span = tok // n_chunk
    g_far = []
    for i in range(n_chunk):
        g = after(out_grad, mine if i == 0 else right_e)[i * span : (i + 1) * span]
        g_far.append([to_chip(g, k) for k in steps])

    def far(grad, i):
        gs = []
        for a in g_far[i]:
            gs += [a, to_sibling(a)]
        return far_input_grad(grad, w_far, gs, i * span)

    right = right_grad(rows, basis_t, right_e, out_grad, pieces, blk, n_dp, scale)
    right = jnp.sum(exchange(right, "dp"), axis=0)
    g_far[0] = after(g_far[0], right)
    q_pieces = everywhere(after(right, g_far[0]), "dp", n_dp)
    new_error, q_t = update_error(
        rows, error, basis_t, out_grad, pieces, blk, q_pieces, n_dp, scale
    )
    for i in range(n_chunk):
        if i > 0:
            g_far[i] = after(g_far[i], q_t)
        grad = far(grad, i)
    return (grad, new_error[None], q_t.T)


def solution(mesh):
    n_dp, n_t = mesh.devices.shape
    mesh = jax.sharding.Mesh(mesh.devices.reshape(n_dp, n_t // 2, 2), ("dp", "chip", "core"))
    tensor = ("chip", "core")
    placed = (
        P("dp", tensor),
        P("dp", tensor),
        P(None, tensor),
        P("dp", None, tensor),
        P(tensor, None),
    )
    return jax.shard_map(
        per_device,
        mesh=mesh,
        in_specs=placed,
        out_specs=(P("dp", tensor), P("dp", None, tensor), P(tensor, None)),
        check_vma=False,
    )
```

```python
import functools
import math

import jax
import jax.numpy as jnp
from jax import lax
from jax.experimental import pallas as pl
from jax.experimental.pallas import tpu as pltpu
from jax.sharding import PartitionSpec as P

TOK_DEV = 1024
RANK = 32
MIB = 1 << 20
F32 = jnp.float32
BF16 = jnp.bfloat16


def dot(a, b, ca, cb, precision=None):
    return lax.dot_general(
        a, b, (((ca,), (cb,)), ((), ())), precision=precision, preferred_element_type=F32
    )


def split(a):
    high = a.astype(BF16)
    return high, (a - high.astype(F32)).astype(BF16)


def params(mib):
    return pltpu.CompilerParams(vmem_limit_bytes=mib * MIB)


def cost(flops, nbytes, weight=0.001):
    return pl.CostEstimate(
        flops=int(flops * weight), bytes_accessed=int(nbytes * weight), transcendentals=0
    )


def project_kernel(g_ref, qt_ref, y_ref):
    both = dot(jnp.concatenate(split(qt_ref[...]), axis=0), g_ref[...], 1, 1)
    y_ref[...] = both[0:RANK, :] + both[RANK:, :]


def project(out_grad, q_t):
    vm = pl.BlockSpec(memory_space=pltpu.VMEM)
    return pl.pallas_call(
        project_kernel,
        in_specs=[vm, vm],
        out_specs=vm,
        out_shape=jax.ShapeDtypeStruct((RANK, out_grad.shape[0]), F32),
        compiler_params=params(24),
        cost_estimate=cost(1e9, 2e6),
        name="project",
    )(out_grad, q_t)


def sketch_kernel(ids, e_ref, qt_ref, send_ref, keep_ref, qs_ref, *, width):
    phase = pl.program_id(0)

    @pl.when((phase == 0) & (pl.program_id(1) == 0) & (pl.program_id(2) == 0))
    def _():
        high, low = split(qt_ref[...])
        qs_ref[0:RANK, :] = high
        qs_ref[RANK : 2 * RANK, :] = low

    high, low = split(e_ref[...])
    main = dot(high, qs_ref[...], 1, 1)
    rest = dot(low, qs_ref[0:RANK, :], 1, 1)
    rows = (main[:, 0:RANK] + main[:, RANK : 2 * RANK] + rest).T

    @pl.when(phase == 0)
    def _():
        for k in range(send_ref.shape[0]):
            send_ref[k, 0] = rows[:, k * width : (k + 1) * width]

    @pl.when(phase == 1)
    def _():
        for k in range(keep_ref.shape[0]):
            keep_ref[k, 0] = rows[:, k * width : (k + 1) * width]


def local_sketch(core, error, q_t, n_dp, chips, part):
    blk = min(512, part)
    per = part // blk
    width = part // n_dp
    outs = error.shape[1]

    def e_map(p, y, j, ids):
        return ((2 * y + jnp.where(p == 0, 1 - ids[0], ids[0])) * per + j, 0)

    def send_map(p, y, j, ids):
        return (jnp.where(p == 0, j, per - 1), jnp.where(p == 0, y, chips - 1), 0, 0)

    def keep_map(p, y, j, ids):
        return (jnp.where(p == 1, j, 0), jnp.where(p == 1, y, 0), 0, 0)

    half = jax.ShapeDtypeStruct((n_dp, chips, RANK, width), F32)
    return pl.pallas_call(
        functools.partial(sketch_kernel, width=width),
        grid_spec=pltpu.PrefetchScalarGridSpec(
            num_scalar_prefetch=1,
            grid=(2, chips, per),
            in_specs=[
                pl.BlockSpec((blk, outs), e_map),
                pl.BlockSpec((RANK, outs), lambda p, y, j, ids: (0, 0)),
            ],
            out_specs=[
                pl.BlockSpec((n_dp // per, 1, RANK, width), send_map),
                pl.BlockSpec((n_dp // per, 1, RANK, width), keep_map),
            ],
            scratch_shapes=[pltpu.VMEM((2 * RANK, outs), BF16)],
        ),
        out_shape=[half, half],
        compiler_params=params(48),
        cost_estimate=cost(6e9, error.size * 4, 2),
        name="error_sketch",
    )(jnp.reshape(core, (1,)), error, q_t)


def sketch_rows_kernel(*refs, scale, width):
    chip, keep, got, x_ref = refs[0:4]
    y_refs, out = refs[4:-1], refs[-1]
    y = y_refs[0][...]
    for r in y_refs[1:]:
        y = y + r[...]
    both = dot(jnp.concatenate(split(y), axis=0), x_ref[...], 1, 0)
    total = (both[0:RANK, :] + both[RANK:, :]) * scale
    out[...] = keep[...] + got[...]
    for k in range(out.shape[0]):
        out[k, chip[0]] += total[:, k * width : (k + 1) * width]


def sketch_rows(chip, keep, got, acts, y_list, scale):
    vm = pl.BlockSpec(memory_space=pltpu.VMEM)
    return pl.pallas_call(
        functools.partial(sketch_rows_kernel, scale=scale, width=keep.shape[3]),
        in_specs=[pl.BlockSpec(memory_space=pltpu.SMEM)] + [vm] * (3 + len(y_list)),
        out_specs=vm,
        out_shape=jax.ShapeDtypeStruct(keep.shape, F32),
        compiler_params=params(24),
        cost_estimate=cost(1e9, 3e6),
        name="sketch_rows",
    )(jnp.reshape(chip, (1,)), keep, got, acts, *y_list)


def basis_kernel(core, mine, other, out, sk, *, n_dp, chips, width, part):
    first = core[0] == 0
    for k in range(n_dp):
        for y in range(chips):
            a, b = mine[k * chips + y], other[k * chips + y]
            for e in range(2):
                at = (2 * y + e) * part + k * width
                block = jnp.where(first, a, b) if e == 0 else jnp.where(first, b, a)
                sk[:, at : at + width] = block * (1.0 / n_dp)
    s = sk[...]
    gram = dot(s, s, 1, 1, lax.Precision.HIGHEST)
    row = lax.broadcasted_iota(jnp.int32, (RANK, RANK), 0)
    col = lax.broadcasted_iota(jnp.int32, (RANK, RANK), 1)
    eye = (row == col).astype(F32)
    m = jnp.concatenate([gram, eye, jnp.zeros((RANK, 2 * RANK), F32)], axis=1)
    index = lax.broadcasted_iota(jnp.int32, (RANK, 1), 0)
    for j in range(RANK - 1):
        factor = jnp.where(index > j, m[:, j : j + 1] / m[j : j + 1, j : j + 1], 0.0)
        m = m - factor * m[j : j + 1, :]
    diag = jnp.sum(jnp.where(row == col, m[:, 0:RANK], 0.0), axis=1, keepdims=True)
    inverse = m[:, RANK : 2 * RANK] / jnp.sqrt(diag)
    out[...] = dot(inverse, s, 1, 0, lax.Precision.HIGHEST)


def make_basis(core, mine, other, n_dp, chips, part, din):
    width = mine.shape[2]
    vm = pl.BlockSpec(memory_space=pltpu.VMEM)
    return pl.pallas_call(
        functools.partial(basis_kernel, n_dp=n_dp, chips=chips, width=width, part=part),
        in_specs=[pl.BlockSpec(memory_space=pltpu.SMEM), vm, vm],
        out_specs=vm,
        out_shape=jax.ShapeDtypeStruct((RANK, din), F32),
        scratch_shapes=[pltpu.VMEM((RANK, din), F32)],
        compiler_params=params(24),
        cost_estimate=cost(6e9, 2e6),
        name="basis",
    )(jnp.reshape(core, (1,)), mine, other)


def right_rows_kernel(rows, m_ref, e_ref, b_ref, acc, *, near):
    i = pl.program_id(0)

    @pl.when(i == 0)
    def _():
        acc[...] = jnp.zeros_like(acc)

    bh, bl = split(b_ref[...])
    both = jnp.concatenate([bh, bl], axis=0)

    def add(ref):
        high, low = split(ref[...])
        main = dot(both, high, 1, 0)
        acc[...] += main[0:RANK, :] + main[RANK:, :] + dot(bh, low, 1, 0)

    @pl.when(i < near)
    def _():
        add(m_ref)

    @pl.when(i >= near)
    def _():
        add(e_ref)


def right_rows(rows, near, merged, error, basis_t, blk):
    din, outs = error.shape
    return pl.pallas_call(
        functools.partial(right_rows_kernel, near=near),
        grid_spec=pltpu.PrefetchScalarGridSpec(
            num_scalar_prefetch=1,
            grid=(din // blk,),
            in_specs=[
                pl.BlockSpec((blk, outs), lambda i, rows: (rows[jnp.minimum(i, near - 1)], 0)),
                pl.BlockSpec((blk, outs), lambda i, rows: (rows[jnp.maximum(i, near)], 0)),
                pl.BlockSpec((RANK, blk), lambda i, rows: (0, rows[i])),
            ],
            out_specs=pl.BlockSpec((RANK, outs), lambda i, rows: (0, 0)),
        ),
        out_shape=jax.ShapeDtypeStruct((RANK, outs), F32),
        compiler_params=params(48),
        cost_estimate=cost(8e9, error.size * 4),
        name="right_rows",
    )(rows, merged, error, basis_t)


def piece_specs(pieces, blk):
    specs, ranges, first = [], [], 0
    for p in pieces:
        count = p.shape[0] // blk

        def at(i, rows, first=first, count=count):
            return (jnp.clip(i - first, 0, count - 1), 0)

        specs.append(pl.BlockSpec((blk, p.shape[1]), at))
        ranges.append((first, first + count))
        first += count
    return specs, ranges


def right_grad_kernel(*refs, ranges, n_out, scale):
    b_ref, r_ref, g_ref = refs[1:4]
    x_refs = refs[4 : 4 + len(ranges)]
    out, vacc = refs[4 + len(ranges) :]
    i = pl.program_id(0)

    @pl.when(i == 0)
    def _():
        vacc[...] = jnp.zeros_like(vacc)

    both = jnp.concatenate(split(b_ref[...]), axis=0)
    for x_ref, (lo, hi) in zip(x_refs, ranges):

        @pl.when((i >= lo) & (i < hi))
        def _(x_ref=x_ref):
            v = dot(both, x_ref[...], 1, 0)
            vacc[...] += v[0:RANK, :] + v[RANK:, :]

    @pl.when(i == ranges[-1][1] - 1)
    def _():
        w = dot(jnp.concatenate(split(vacc[...]), axis=0), g_ref[...], 1, 0)
        total = r_ref[...] + (w[0:RANK, :] + w[RANK:, :]) * scale
        width = total.shape[1] // n_out
        for k in range(n_out):
            out[k] = total[:, k * width : (k + 1) * width]


def right_grad(rows, basis_t, right_e, out_grad, pieces, blk, n_out, scale):
    tok, outs = out_grad.shape
    same = lambda i, rows: (0, 0)
    specs, ranges = piece_specs(pieces, blk)
    return pl.pallas_call(
        functools.partial(right_grad_kernel, ranges=ranges, n_out=n_out, scale=scale),
        grid_spec=pltpu.PrefetchScalarGridSpec(
            num_scalar_prefetch=1,
            grid=(ranges[-1][1],),
            in_specs=[
                pl.BlockSpec((RANK, blk), lambda i, rows: (0, rows[i])),
                pl.BlockSpec((RANK, outs), same),
                pl.BlockSpec((tok, outs), same),
            ]
            + specs,
            out_specs=pl.BlockSpec((n_out, RANK, outs // n_out), lambda i, rows: (0, 0, 0)),
            scratch_shapes=[pltpu.VMEM((RANK, tok), F32)],
        ),
        out_shape=jax.ShapeDtypeStruct((n_out, RANK, outs // n_out), F32),
        compiler_params=params(48),
        cost_estimate=cost(4e9, basis_t.shape[1] * tok * 2),
        name="right_grad",
    )(rows, basis_t, right_e, out_grad, *pieces)


def merge_kernel(*refs, ranges, scale, kept):
    e_ref, g_ref = refs[1 + kept : 3 + kept]
    x_refs, out = refs[3 + kept : -1], refs[-1]
    i = pl.program_id(0)
    for x_ref, (lo, hi) in zip(x_refs, ranges):

        @pl.when((i >= lo) & (i < hi))
        def _(x_ref=x_ref):
            out[...] = e_ref[...] + dot(x_ref[...], g_ref[...], 1, 0) * scale


def merge(rows, kept, error, out_grad, pieces, blk, scale):
    tok, outs = out_grad.shape
    specs, ranges = piece_specs(pieces, blk)
    block = pl.BlockSpec((blk, outs), lambda i, rows: (rows[i], 0))
    return pl.pallas_call(
        functools.partial(merge_kernel, ranges=ranges, scale=scale, kept=len(kept)),
        grid_spec=pltpu.PrefetchScalarGridSpec(
            num_scalar_prefetch=1,
            grid=(ranges[-1][1],),
            in_specs=[pl.BlockSpec(memory_space=pl.ANY)] * len(kept)
            + [block, pl.BlockSpec((tok, outs), lambda i, rows: (0, 0))]
            + specs,
            out_specs=block,
        ),
        out_shape=jax.ShapeDtypeStruct(error.shape, F32),
        input_output_aliases={1: 0} if kept else {},
        compiler_params=params(48),
        cost_estimate=cost(5e9, error.size * 4, 2),
        name="merge",
    )(rows, *kept, error, out_grad, *pieces)


def update_kernel(m_ref, b_ref, q_ref, out, qt_out, qs, *, n_dp):
    @pl.when(pl.program_id(0) == 0)
    def _():
        q_t = jnp.concatenate([q_ref[k] for k in range(n_dp)], axis=1) * (1.0 / n_dp)
        qt_out[...] = q_t
        high, low = split(q_t)
        qs[0:RANK, :] = high
        qs[RANK : 2 * RANK, :] = low
        qs[2 * RANK : 3 * RANK, :] = high

    bh, bl = split(b_ref[...].T)
    out[...] = m_ref[...] - dot(jnp.concatenate([bh, bh, bl], axis=1), qs[...], 1, 0)


def update_error(merged, basis_t, q_pieces, n_dp):
    din, outs = merged.shape
    blk = 512
    block = pl.BlockSpec((blk, outs), lambda i: (i, 0))
    return pl.pallas_call(
        functools.partial(update_kernel, n_dp=n_dp),
        grid=(din // blk,),
        in_specs=[
            block,
            pl.BlockSpec((RANK, blk), lambda i: (0, i)),
            pl.BlockSpec(q_pieces.shape, lambda i: (0, 0, 0)),
        ],
        out_specs=[block, pl.BlockSpec((RANK, outs), lambda i: (0, 0))],
        out_shape=[
            jax.ShapeDtypeStruct(merged.shape, F32),
            jax.ShapeDtypeStruct((RANK, outs), F32),
        ],
        scratch_shapes=[pltpu.VMEM((3 * RANK, outs), BF16)],
        input_output_aliases={0: 0},
        compiler_params=params(48),
        cost_estimate=cost(2e9, merged.size * 8),
        name="update_error",
    )(merged, basis_t, q_pieces)


def near_kernel(ids, g_ref, gs_ref, w_ref, ws_ref, out):
    out[...] = dot(g_ref[...], w_ref[...], 1, 1) + dot(gs_ref[...], ws_ref[...], 1, 1)


def near_input_grad(me_t, g_own, g_sib, weight, w_sib):
    tok, outs = g_own.shape
    part = w_sib.shape[0]
    blk = min(256, part)
    per = part // blk
    whole = pl.BlockSpec((tok, outs), lambda i, ids: (0, 0))
    return pl.pallas_call(
        near_kernel,
        grid_spec=pltpu.PrefetchScalarGridSpec(
            num_scalar_prefetch=1,
            grid=(per,),
            in_specs=[
                whole,
                whole,
                pl.BlockSpec((blk, outs), lambda i, ids: (ids[0] * per + i, 0)),
                pl.BlockSpec((blk, outs), lambda i, ids: (i, 0)),
            ],
            out_specs=pl.BlockSpec((tok, blk), lambda i, ids: (0, i)),
        ),
        out_shape=jax.ShapeDtypeStruct((tok, part), F32),
        compiler_params=params(48),
        cost_estimate=cost(4 * tok * outs * part, 12e6, 2),
        name="input_grad_near",
    )(jnp.reshape(me_t, (1,)), g_own, g_sib, weight, w_sib)


def far_kernel(*refs):
    prev, w_ref = refs[0], refs[1]
    g_refs, out = refs[2:-1], refs[-1]
    width = g_refs[0].shape[1]
    total = prev[...]
    for n, g in enumerate(g_refs):
        total = total + dot(g[...], w_ref[:, n * width : (n + 1) * width], 1, 1)
    out[...] = total


def far_input_grad(prev, w_far, gs, start):
    rows, outs = gs[0].shape
    tok, part = prev.shape
    blk = min(256, part)
    to = pl.BlockSpec((rows, blk), lambda i: (start // rows, i))
    return pl.pallas_call(
        far_kernel,
        grid=(part // blk,),
        in_specs=[to, pl.BlockSpec((blk, w_far.shape[1]), lambda i: (i, 0))]
        + [pl.BlockSpec((rows, outs), lambda i: (0, 0))] * len(gs),
        out_specs=to,
        out_shape=jax.ShapeDtypeStruct((tok, part), F32),
        input_output_aliases={0: 0},
        compiler_params=params(48),
        cost_estimate=cost(2 * len(gs) * rows * outs * part, 10e6),
        name="input_grad_far",
    )(prev, w_far, *gs)


def after(value, *others):
    return lax.optimization_barrier((value, others))[0]


def per_device(activations, out_grad, weight, error, q_start):
    scale = 1.0 / math.sqrt(TOK_DEV)
    n_dp = lax.axis_size("dp")
    chips = lax.axis_size("chip")
    n_t = 2 * chips
    d = lax.axis_index("dp").astype(jnp.int32)
    y = lax.axis_index("chip").astype(jnp.int32)
    c = lax.axis_index("core").astype(jnp.int32)
    t = 2 * y + c
    tok, part = activations.shape
    outs = out_grad.shape[1]
    din = weight.shape[0]
    error = error[0]
    q_t = q_start.T
    steps = range(1, chips)
    share = part // n_dp
    spread = ("dp", "chip")
    n = n_dp * chips

    def to_sibling(a):
        return lax.ppermute(a, "core", [(0, 1), (1, 0)])

    def to_chip(a, k, flip=0):
        pairs = [(i, ((i // 2 + k) % chips) * 2 + ((i % 2) ^ flip)) for i in range(n_t)]
        return lax.ppermute(a, ("chip", "core"), pairs)

    def exchange(a, axes):
        return lax.all_to_all(a, axes, 0, 0, tiled=True)

    def everywhere(a, axes, n):
        return exchange(jnp.broadcast_to(a, (n, *a.shape)), axes)

    y_t = project(out_grad, q_t)
    y_t = y_t + to_sibling(y_t)
    y_list = [y_t] + [to_chip(y_t, k) for k in steps]

    moves = [(k, e) for k in steps for e in range(2)]
    w_parts = []
    for k, e in moves:
        dest = ((y + k) % chips) * 2 + (c ^ e)
        w_parts.append(lax.dynamic_slice(weight, (dest * part + d * share, 0), (share, outs)))
    w_parts = after(w_parts, y_t)
    x_t = after(activations, *w_parts).T
    w_parts = [to_chip(a, k, e) for a, (k, e) in zip(w_parts, moves)]
    tall = min(512, part)
    short = part // 4
    starts = [0, short, 3 * short, part]
    x_rows = [x_t[lo:hi] for lo, hi in zip(starts[:-1], starts[1:])]
    x_far = [[to_chip(a, k) for k in steps] for a in x_rows]

    send, keep = local_sketch(c, error, after(q_t, *x_rows), n_dp, chips, part)
    w_parts = jnp.concatenate([after(a, send) for a in w_parts], axis=1)
    y_list, x_far[0] = after((y_list, x_far[0]), w_parts)
    blocks = sketch_rows(y, keep, to_sibling(send), activations, y_list, scale)
    w_far = lax.all_gather(w_parts, "dp", axis=0, tiled=True)

    g_sib = to_sibling(out_grad)
    w_sib = to_sibling(lax.dynamic_slice(after(weight, send), ((t ^ 1) * part, 0), (part, outs)))
    grad = near_input_grad(t, out_grad, g_sib, weight, after(w_sib, blocks))
    blocks = after(blocks, x_far[0])
    blocks = after(exchange(blocks.reshape(n, RANK, share), spread), grad)
    piece = jnp.sum(blocks, axis=0)

    per = part // tall
    rows_near = [(2 * y + (c ^ e)) * per + j for e in range(2) for j in range(per)]
    rows_all = list(rows_near)
    for k in steps:
        rows_all += [(2 * ((y - k) % chips) + e) * per + j for e in range(2) for j in range(per)]
    rows_near = jnp.stack(rows_near).astype(jnp.int32)
    rows_all = jnp.stack(rows_all).astype(jnp.int32)
    x_near = [x_t, to_sibling(x_t)]
    merged = merge(rows_near, [], error, out_grad, after(x_near, piece), tall, scale)

    mine = everywhere(after(piece, x_far[1]), spread, n)
    basis_t = make_basis(c, after(mine, merged), to_sibling(mine), n_dp, chips, part, din)
    right_e = right_rows(rows_all, 2 * per, merged, error, basis_t, tall)

    pieces, rows = [], []
    for j in range(3):
        a = after(x_far[j], right_e if j == 2 else mine)
        for k, a in zip(steps, a):
            for e in range(2):
                pieces.append(to_sibling(a) if e else a)
                base = (2 * ((y - k) % chips) + (c ^ e)) * 4 + starts[j] // short
                rows += [base + i for i in range((starts[j + 1] - starts[j]) // short)]
    rows = jnp.stack(rows).astype(jnp.int32)

    n_chunk = 2
    span = tok // n_chunk
    g_far = []
    for i in range(n_chunk):
        g = after(out_grad, mine if i == 0 else right_e)[i * span : (i + 1) * span]
        g_far.append([to_chip(g, k) for k in steps])

    right = right_grad(rows, basis_t, right_e, out_grad, pieces, short, n_dp, scale)
    merged = merge(rows, [merged], error, after(out_grad, right), pieces, short, scale)
    right = jnp.sum(after(exchange(right, "dp"), merged), axis=0)
    q_pieces = everywhere(right, "dp", n_dp)
    new_error, q_t = update_error(merged, basis_t, q_pieces, n_dp)
    for i in range(n_chunk):
        gs = []
        for a in after(g_far[i], right if i == 0 else q_t):
            gs += [a, to_sibling(a)]
        grad = far_input_grad(after(grad, q_t), w_far, gs, i * span)
    return (grad, new_error[None], q_t.T)


def solution(mesh):
    n_dp, n_t = mesh.devices.shape
    mesh = jax.sharding.Mesh(mesh.devices.reshape(n_dp, n_t // 2, 2), ("dp", "chip", "core"))
    tensor = ("chip", "core")
    placed = (
        P("dp", tensor),
        P("dp", tensor),
        P(None, tensor),
        P("dp", None, tensor),
        P(tensor, None),
    )
    return jax.shard_map(
        per_device,
        mesh=mesh,
        in_specs=placed,
        out_specs=(P("dp", tensor), P("dp", None, tensor), P(tensor, None)),
        check_vma=False,
    )
```

```python
import functools
import math

import jax
import jax.numpy as jnp
from jax import lax
from jax.experimental import pallas as pl
from jax.experimental.pallas import tpu as pltpu
from jax.sharding import PartitionSpec as P

TOK_DEV = 1024
RANK = 32
MIB = 1 << 20
F32 = jnp.float32
BF16 = jnp.bfloat16


def dot(a, b, ca, cb, precision=None):
    return lax.dot_general(
        a, b, (((ca,), (cb,)), ((), ())), precision=precision, preferred_element_type=F32
    )


def split(a):
    high = a.astype(BF16)
    return high, (a - high.astype(F32)).astype(BF16)


def params(mib):
    return pltpu.CompilerParams(vmem_limit_bytes=mib * MIB)


def cost(flops, nbytes, weight=0.001):
    return pl.CostEstimate(
        flops=int(flops * weight), bytes_accessed=int(nbytes * weight), transcendentals=0
    )


def project_kernel(g_ref, qt_ref, y_ref):
    both = dot(jnp.concatenate(split(qt_ref[...]), axis=0), g_ref[...], 1, 1)
    y_ref[...] = both[0:RANK, :] + both[RANK:, :]


def project(out_grad, q_t):
    vm = pl.BlockSpec(memory_space=pltpu.VMEM)
    return pl.pallas_call(
        project_kernel,
        in_specs=[vm, vm],
        out_specs=vm,
        out_shape=jax.ShapeDtypeStruct((RANK, out_grad.shape[0]), F32),
        compiler_params=params(24),
        cost_estimate=cost(1e9, 2e6),
        name="project",
    )(out_grad, q_t)


def sketch_kernel(ids, e_ref, qt_ref, send_ref, keep_ref, qs_ref):
    phase = pl.program_id(0)

    @pl.when((phase == 0) & (pl.program_id(1) == 0))
    def _():
        high, low = split(qt_ref[...])
        qs_ref[0:RANK, :] = high
        qs_ref[RANK : 2 * RANK, :] = low

    high, low = split(e_ref[...])
    main = dot(high, qs_ref[...], 1, 1)
    rest = dot(low, qs_ref[0:RANK, :], 1, 1)
    rows = (main[:, 0:RANK] + main[:, RANK : 2 * RANK] + rest).T

    @pl.when(phase == 0)
    def _():
        send_ref[0] = rows

    @pl.when(phase == 1)
    def _():
        keep_ref[0] = rows


def local_sketch(core, error, q_t, chips, part):
    outs = error.shape[1]

    def e_map(p, y, ids):
        return (2 * y + jnp.where(p == 0, 1 - ids[0], ids[0]), 0)

    half = jax.ShapeDtypeStruct((chips, RANK, part), F32)
    return pl.pallas_call(
        sketch_kernel,
        grid_spec=pltpu.PrefetchScalarGridSpec(
            num_scalar_prefetch=1,
            grid=(2, chips),
            in_specs=[
                pl.BlockSpec((part, outs), e_map),
                pl.BlockSpec((RANK, outs), lambda p, y, ids: (0, 0)),
            ],
            out_specs=[
                pl.BlockSpec((1, RANK, part), lambda p, y, ids: (jnp.where(p == 0, y, chips - 1), 0, 0)),
                pl.BlockSpec((1, RANK, part), lambda p, y, ids: (jnp.where(p == 1, y, 0), 0, 0)),
            ],
            scratch_shapes=[pltpu.VMEM((2 * RANK, outs), BF16)],
        ),
        out_shape=[half, half],
        compiler_params=params(48),
        cost_estimate=cost(6e9, error.size * 4, 2),
        name="error_sketch",
    )(jnp.reshape(core, (1,)), error, q_t)


def sketch_rows_kernel(*refs, n_e, scale):
    e_refs, y_refs, x_ref, out = refs[:n_e], refs[n_e:-2], refs[-2], refs[-1]
    y = y_refs[0][...]
    for r in y_refs[1:]:
        y = y + r[...]
    both = dot(jnp.concatenate(split(y), axis=0), x_ref[...], 1, 0)
    total = (both[0:RANK, :] + both[RANK:, :]) * scale
    for r in e_refs:
        total = total + r[...]
    out[...] = total


def sketch_rows(e_list, y_list, acts, scale):
    vm = pl.BlockSpec(memory_space=pltpu.VMEM)
    return pl.pallas_call(
        functools.partial(sketch_rows_kernel, n_e=len(e_list), scale=scale),
        in_specs=[vm] * (1 + len(e_list) + len(y_list)),
        out_specs=vm,
        out_shape=jax.ShapeDtypeStruct((RANK, acts.shape[1]), F32),
        compiler_params=params(24),
        cost_estimate=cost(1e9, 3e6),
        name="sketch_rows",
    )(*e_list, *y_list, acts)


def basis_kernel(src, mine, other, out, sk, *, n_dp, chips, part):
    for k in range(chips):
        for e, ref in enumerate((mine, other)):
            at = pl.multiple_of(src[2 * k + e] * part, part)
            sk[:, pl.ds(at, part)] = ref[k] * (1.0 / n_dp)
    s = sk[...]
    gram = dot(s, s, 1, 1, lax.Precision.HIGHEST)
    row = lax.broadcasted_iota(jnp.int32, (RANK, RANK), 0)
    col = lax.broadcasted_iota(jnp.int32, (RANK, RANK), 1)
    eye = (row == col).astype(F32)
    m = jnp.concatenate([gram, eye, jnp.zeros((RANK, 2 * RANK), F32)], axis=1)
    index = lax.broadcasted_iota(jnp.int32, (RANK, 1), 0)
    for j in range(RANK - 1):
        factor = jnp.where(index > j, m[:, j : j + 1] / m[j : j + 1, j : j + 1], 0.0)
        m = m - factor * m[j : j + 1, :]
    diag = jnp.sum(jnp.where(row == col, m[:, 0:RANK], 0.0), axis=1, keepdims=True)
    inverse = m[:, RANK : 2 * RANK] / jnp.sqrt(diag)
    out[...] = dot(inverse, s, 1, 0, lax.Precision.HIGHEST)


def make_basis(src, mine, other, n_dp):
    chips, _, part = mine.shape
    din = 2 * chips * part
    vm = pl.BlockSpec(memory_space=pltpu.VMEM)
    return pl.pallas_call(
        functools.partial(basis_kernel, n_dp=n_dp, chips=chips, part=part),
        in_specs=[pl.BlockSpec(memory_space=pltpu.SMEM), vm, vm],
        out_specs=vm,
        out_shape=jax.ShapeDtypeStruct((RANK, din), F32),
        scratch_shapes=[pltpu.VMEM((RANK, din), F32)],
        compiler_params=params(24),
        cost_estimate=cost(6e9, 2e6),
        name="basis",
    )(src, mine, other)


def right_error_kernel(e_ref, b_ref, acc):
    @pl.when(pl.program_id(0) == 0)
    def _():
        acc[...] = jnp.zeros_like(acc)

    bh, bl = split(b_ref[...])
    eh, el = split(e_ref[...])
    main = dot(jnp.concatenate([bh, bl], axis=0), eh, 1, 0)
    acc[...] += main[0:RANK, :] + main[RANK:, :] + dot(bh, el, 1, 0)


def right_error(error, basis_t):
    din, outs = error.shape
    blk = 512
    return pl.pallas_call(
        right_error_kernel,
        grid=(din // blk,),
        in_specs=[
            pl.BlockSpec((blk, outs), lambda i: (i, 0)),
            pl.BlockSpec((RANK, blk), lambda i: (0, i)),
        ],
        out_specs=pl.BlockSpec((RANK, outs), lambda i: (0, 0)),
        out_shape=jax.ShapeDtypeStruct((RANK, outs), F32),
        compiler_params=params(48),
        cost_estimate=cost(8e9, error.size * 4, 1),
        name="right_error",
    )(error, basis_t)


def copies(sources, target, sems):
    made, at = [], 0
    for n, ref in enumerate(sources):
        size = ref.shape[0]
        made.append(pltpu.make_async_copy(ref, target.at[at : at + size], sems.at[n]))
        at += size
    return made


def right_grad_kernel(*refs, n_t, per, scale):
    b_ref, r_ref, g_ref = refs[1:4]
    x_refs = refs[4 : 4 + n_t * per]
    out, vacc, xbuf, sems = refs[4 + n_t * per :]
    r = pl.program_id(0)
    part = xbuf.shape[0] // n_t
    moves = copies(x_refs, xbuf, sems)

    @pl.when(r == 0)
    def _():
        for m in moves:
            m.start()
        vacc[...] = jnp.zeros_like(vacc)

    for n in range(n_t):

        @pl.when(r == n)
        def _(n=n):
            for m in moves[n * per : (n + 1) * per]:
                m.wait()

    both = jnp.concatenate(split(b_ref[...]), axis=0)
    v = dot(both, xbuf[pl.ds(pl.multiple_of(r * part, part), part), :], 1, 0)
    vacc[...] += v[0:RANK, :] + v[RANK:, :]

    @pl.when(r == n_t - 1)
    def _():
        w = dot(jnp.concatenate(split(vacc[...]), axis=0), g_ref[...], 1, 0)
        out[...] = r_ref[...] + (w[0:RANK, :] + w[RANK:, :]) * scale


def right_grad(src, basis_t, right_e, out_grad, pieces, scale):
    tok, outs = out_grad.shape
    n_t = src.shape[0]
    din = basis_t.shape[1]
    part = din // n_t
    same = lambda r, src: (0, 0)
    return pl.pallas_call(
        functools.partial(right_grad_kernel, n_t=n_t, per=len(pieces) // n_t, scale=scale),
        grid_spec=pltpu.PrefetchScalarGridSpec(
            num_scalar_prefetch=1,
            grid=(n_t,),
            in_specs=[
                pl.BlockSpec((RANK, part), lambda r, src: (0, src[r])),
                pl.BlockSpec((RANK, outs), same),
                pl.BlockSpec((tok, outs), same),
            ]
            + [pl.BlockSpec(memory_space=pl.ANY)] * len(pieces),
            out_specs=pl.BlockSpec((RANK, outs), same),
            scratch_shapes=[
                pltpu.VMEM((RANK, tok), F32),
                pltpu.VMEM((din, tok), BF16),
                pltpu.SemaphoreType.DMA((len(pieces),)),
            ],
        ),
        out_shape=jax.ShapeDtypeStruct((RANK, outs), F32),
        compiler_params=params(40),
        cost_estimate=cost(4e9, din * tok * 2, 1),
        name="right_grad",
    )(src, basis_t, right_e, out_grad, *pieces)


def update_kernel(*refs, n_t, per, n_dp, scale):
    e_ref, b_ref, g_ref, q_ref = refs[1:5]
    x_refs = refs[5 : 5 + n_t * per]
    out, qt_out, qs, xbuf, sems = refs[5 + n_t * per :]
    r = pl.program_id(0)
    part = xbuf.shape[0] // n_t
    moves = copies(x_refs, xbuf, sems)

    @pl.when(r == 0)
    def _():
        for m in moves:
            m.start()
        q_t = q_ref[...] * (1.0 / n_dp)
        qt_out[...] = q_t
        high, low = split(q_t)
        qs[0:RANK, :] = high
        qs[RANK : 2 * RANK, :] = low
        qs[2 * RANK : 3 * RANK, :] = high

    bh, bl = split(b_ref[...].T)
    low_rank = dot(jnp.concatenate([bh, bh, bl], axis=1), qs[...], 1, 0)
    for n in range(n_t):

        @pl.when(r == n)
        def _(n=n):
            for m in moves[n * per : (n + 1) * per]:
                m.wait()

    x = xbuf[pl.ds(pl.multiple_of(r * part, part), part), :]
    out[...] = e_ref[...] + dot(x, g_ref[...], 1, 0) * scale - low_rank


def update_error(src, error, basis_t, out_grad, pieces, q_t, n_dp, scale):
    tok, outs = out_grad.shape
    n_t = src.shape[0]
    din = error.shape[0]
    part = din // n_t
    block = pl.BlockSpec((part, outs), lambda r, src: (src[r], 0))
    same = lambda r, src: (0, 0)
    return pl.pallas_call(
        functools.partial(
            update_kernel, n_t=n_t, per=len(pieces) // n_t, n_dp=n_dp, scale=scale
        ),
        grid_spec=pltpu.PrefetchScalarGridSpec(
            num_scalar_prefetch=1,
            grid=(n_t,),
            in_specs=[
                block,
                pl.BlockSpec((RANK, part), lambda r, src: (0, src[r])),
                pl.BlockSpec((tok, outs), same),
                pl.BlockSpec((RANK, outs), same),
            ]
            + [pl.BlockSpec(memory_space=pl.ANY)] * len(pieces),
            out_specs=[block, pl.BlockSpec((RANK, outs), same)],
            scratch_shapes=[
                pltpu.VMEM((3 * RANK, outs), BF16),
                pltpu.VMEM((din, tok), BF16),
                pltpu.SemaphoreType.DMA((len(pieces),)),
            ],
        ),
        out_shape=[
            jax.ShapeDtypeStruct(error.shape, F32),
            jax.ShapeDtypeStruct((RANK, outs), F32),
        ],
        compiler_params=params(56),
        cost_estimate=cost(9e9, error.size * 8 + din * tok * 2, 1),
        name="update_error",
    )(src, error, basis_t, out_grad, q_t, *pieces)


def near_kernel(ids, g_ref, gs_ref, w_ref, ws_ref, out):
    out[...] = dot(g_ref[...], w_ref[...], 1, 1) + dot(gs_ref[...], ws_ref[...], 1, 1)


def near_input_grad(me_t, g_own, g_sib, weight, w_sib):
    tok, outs = g_own.shape
    part = w_sib.shape[0]
    blk = min(256, part)
    per = part // blk
    whole = pl.BlockSpec((tok, outs), lambda i, ids: (0, 0))
    return pl.pallas_call(
        near_kernel,
        grid_spec=pltpu.PrefetchScalarGridSpec(
            num_scalar_prefetch=1,
            grid=(per,),
            in_specs=[
                whole,
                whole,
                pl.BlockSpec((blk, outs), lambda i, ids: (ids[0] * per + i, 0)),
                pl.BlockSpec((blk, outs), lambda i, ids: (i, 0)),
            ],
            out_specs=pl.BlockSpec((tok, blk), lambda i, ids: (0, i)),
        ),
        out_shape=jax.ShapeDtypeStruct((tok, part), F32),
        compiler_params=params(48),
        cost_estimate=cost(4 * tok * outs * part, 12e6, 2),
        name="input_grad_near",
    )(jnp.reshape(me_t, (1,)), g_own, g_sib, weight, w_sib)


def far_kernel(*refs, n_far):
    prev, w_ref = refs[0], refs[1]
    g_refs = refs[2:-3]
    out, gbuf, sems = refs[-3:]
    tok = prev.shape[0]
    moves = copies(g_refs, gbuf, sems)

    @pl.when(pl.program_id(0) == 0)
    def _():
        for m in moves:
            m.start()
        for m in moves:
            m.wait()

    width = gbuf.shape[1]
    total = prev[...]
    for n in range(n_far):
        rows = gbuf[n * tok : (n + 1) * tok, :]
        total = total + dot(rows, w_ref[:, n * width : (n + 1) * width], 1, 1)
    out[...] = total


def far_input_grad(prev, w_far, gs):
    outs = gs[0].shape[1]
    tok, part = prev.shape
    n_far = w_far.shape[1] // outs
    blk = min(256, part)
    to = pl.BlockSpec((tok, blk), lambda i: (0, i))
    return pl.pallas_call(
        functools.partial(far_kernel, n_far=n_far),
        grid=(part // blk,),
        in_specs=[to, pl.BlockSpec((blk, w_far.shape[1]), lambda i: (i, 0))]
        + [pl.BlockSpec(memory_space=pl.ANY)] * len(gs),
        out_specs=to,
        out_shape=jax.ShapeDtypeStruct((tok, part), F32),
        scratch_shapes=[
            pltpu.VMEM((n_far * tok, outs), BF16),
            pltpu.SemaphoreType.DMA((len(gs),)),
        ],
        input_output_aliases={0: 0},
        compiler_params=params(48),
        cost_estimate=cost(2 * n_far * tok * outs * part, 10e6, 1),
        name="input_grad_far",
    )(prev, w_far, *gs)


def after(value, *others):
    return lax.optimization_barrier((value, others))[0]


def per_device(activations, out_grad, weight, error, q_start):
    scale = 1.0 / math.sqrt(TOK_DEV)
    n_dp = lax.axis_size("dp")
    chips = lax.axis_size("chip")
    n_t = 2 * chips
    d = lax.axis_index("dp").astype(jnp.int32)
    y = lax.axis_index("chip").astype(jnp.int32)
    c = lax.axis_index("core").astype(jnp.int32)
    t = 2 * y + c
    tok, part = activations.shape
    outs = out_grad.shape[1]
    din = weight.shape[0]
    error = error[0]
    q_t = q_start.T
    steps = range(1, chips)
    share = part // n_dp

    def to_sibling(a):
        return lax.ppermute(a, "core", [(0, 1), (1, 0)])

    def to_chip(a, k, flip=0):
        pairs = [(i, ((i // 2 + k) % chips) * 2 + ((i % 2) ^ flip)) for i in range(n_t)]
        return lax.ppermute(a, ("chip", "core"), pairs)

    def to_replica(a, k):
        return lax.ppermute(a, "dp", [(i, i ^ k) for i in range(n_dp)])

    def over_replicas(a, chunks):
        rounds = [1 << i for i in range(n_dp.bit_length() - 1)]
        for i, k in enumerate(rounds):
            if i == len(rounds) - 1:
                a = after(a, chunks)
            a = a + to_replica(a, k)
        return a

    src = jnp.stack([((y - k) % chips) * 2 + (c ^ e) for k in range(chips) for e in range(2)])
    src = src.astype(jnp.int32)

    y_t = project(out_grad, q_t)
    y_t = y_t + to_sibling(y_t)
    y_list = [y_t] + [to_chip(y_t, k) for k in steps]

    moves = [(k, e) for k in steps for e in range(2)]
    w_parts = []
    for k, e in moves:
        dest = ((y + k) % chips) * 2 + (c ^ e)
        w_parts.append(lax.dynamic_slice(weight, (dest * part + d * share, 0), (share, outs)))
    w_parts = after(w_parts, y_t)
    w_start = [to_chip(a, k, e) for a, (k, e) in zip(w_parts, moves)]
    send, keep = local_sketch(c, error, after(q_t, *w_parts), chips, part)
    w_parts, y_list = after((w_start, y_list), send)
    w_far = lax.all_gather(jnp.concatenate(w_parts, axis=1), "dp", axis=0, tiled=True)

    got = to_sibling(send)

    def block(k):
        at = (y + k) % chips
        return lax.dynamic_index_in_dim(keep, at, 0, False) + lax.dynamic_index_in_dim(got, at, 0, False)

    e_list = [block(0)] + [to_chip(block(k), k) for k in steps]
    sketch = sketch_rows(e_list, y_list, activations, scale)

    n_chunk = 4
    high = part // n_chunk
    acts = after(activations, send)
    x_rows = [acts[:, i * high : (i + 1) * high].T for i in range(n_chunk)]
    x_rows[0:2] = after(x_rows[0:2], e_list)
    x_far = [[to_chip(a, k) for k in steps] for a in x_rows[0:2]]
    sketch = after(over_replicas(sketch, x_far[0]), x_far[1])
    mine = jnp.stack([sketch] + [to_chip(sketch, k) for k in steps])
    x_rows[2:4] = after(x_rows[2:4], mine)
    x_far += [[to_chip(a, k) for k in steps] for a in x_rows[2:4]]
    basis_t = make_basis(src, mine, to_sibling(mine), n_dp)
    right_e = right_error(error, basis_t)

    g_sib = to_sibling(out_grad)
    w_sib = to_sibling(lax.dynamic_slice(after(weight, send), ((t ^ 1) * part, 0), (part, outs)))
    grad = near_input_grad(t, out_grad, g_sib, weight, after(w_sib, right_e, x_far[2]))

    x_far[0:2] = after(x_far[0:2], mine)
    x_far[2] = after(x_far[2], right_e)
    x_far[3] = after(x_far[3], grad)
    pieces = list(x_rows) + [to_sibling(a) for a in after(x_rows, mine)]
    for n in range(len(steps)):
        held = [a[n] for a in x_far]
        pieces += held + [to_sibling(a) for a in held]

    span = tok // n_chunk
    g_rows = after(out_grad, right_e)
    g_far = [
        [to_chip(g_rows[i * span : (i + 1) * span], k) for k in steps] for i in range(n_chunk)
    ]
    right = after(right_grad(src, basis_t, right_e, out_grad, pieces, scale), g_far[0])
    right = over_replicas(right, g_far[1])
    new_error, q_t = update_error(
        src, error, basis_t, out_grad, pieces, right, n_dp, scale
    )
    gs = []
    g_far = after(g_far, q_t)
    for n in range(len(steps)):
        held = [a[n] for a in g_far]
        gs += held + [to_sibling(a) for a in held]
    grad = far_input_grad(grad, w_far, gs)
    return (grad, new_error[None], q_t.T)


def solution(mesh):
    n_dp, n_t = mesh.devices.shape
    mesh = jax.sharding.Mesh(mesh.devices.reshape(n_dp, n_t // 2, 2), ("dp", "chip", "core"))
    tensor = ("chip", "core")
    placed = (
        P("dp", tensor),
        P("dp", tensor),
        P(None, tensor),
        P("dp", None, tensor),
        P(tensor, None),
    )
    return jax.shard_map(
        per_device,
        mesh=mesh,
        in_specs=placed,
        out_specs=(P("dp", tensor), P("dp", None, tensor), P(tensor, None)),
        check_vma=False,
    )
```

```python
import functools
import math

import jax
import jax.numpy as jnp
from jax import lax
from jax.experimental import pallas as pl
from jax.experimental.pallas import tpu as pltpu
from jax.sharding import PartitionSpec as P

TOK_DEV = 1024
RANK = 32
MIB = 1 << 20
F32 = jnp.float32
BF16 = jnp.bfloat16


def dot(a, b, ca, cb, precision=None):
    return lax.dot_general(
        a, b, (((ca,), (cb,)), ((), ())), precision=precision, preferred_element_type=F32
    )


def split(a):
    high = a.astype(BF16)
    return high, (a - high.astype(F32)).astype(BF16)


def params(mib):
    return pltpu.CompilerParams(vmem_limit_bytes=mib * MIB)


def cost(flops, nbytes, weight=0.001):
    return pl.CostEstimate(
        flops=int(flops * weight), bytes_accessed=int(nbytes * weight), transcendentals=0
    )


def sketch_kernel(ids, e_ref, qt_ref, g_hbm, send_ref, keep_ref, y_ref, qs_ref, g_ref, sem):
    phase, y = pl.program_id(0), pl.program_id(1)
    move = pltpu.make_async_copy(g_hbm, g_ref, sem)

    @pl.when((phase == 0) & (y == 0))
    def _():
        move.start()
        high, low = split(qt_ref[...])
        qs_ref[0:RANK, :] = high
        qs_ref[RANK : 2 * RANK, :] = low

    high, low = split(e_ref[...])
    main = dot(high, qs_ref[...], 1, 1)
    rest = dot(low, qs_ref[0:RANK, :], 1, 1)
    rows = (main[:, 0:RANK] + main[:, RANK : 2 * RANK] + rest).T

    @pl.when(phase == 0)
    def _():
        send_ref[0] = rows

    @pl.when(phase == 1)
    def _():
        keep_ref[0] = rows

    @pl.when((phase == 1) & (y == pl.num_programs(1) - 1))
    def _():
        move.wait()
        both = dot(qs_ref[...], g_ref[...], 1, 1)
        y_ref[...] = both[0:RANK, :] + both[RANK : 2 * RANK, :]


def local_sketch(core, error, q_t, out_grad, chips, part):
    tok, outs = out_grad.shape

    def e_map(p, y, ids):
        return (2 * y + jnp.where(p == 0, 1 - ids[0], ids[0]), 0)

    half = jax.ShapeDtypeStruct((chips, RANK, part), F32)
    return pl.pallas_call(
        sketch_kernel,
        grid_spec=pltpu.PrefetchScalarGridSpec(
            num_scalar_prefetch=1,
            grid=(2, chips),
            in_specs=[
                pl.BlockSpec((part, outs), e_map),
                pl.BlockSpec((RANK, outs), lambda p, y, ids: (0, 0)),
                pl.BlockSpec(memory_space=pl.ANY),
            ],
            out_specs=[
                pl.BlockSpec((1, RANK, part), lambda p, y, ids: (jnp.where(p == 0, y, chips - 1), 0, 0)),
                pl.BlockSpec((1, RANK, part), lambda p, y, ids: (jnp.where(p == 1, y, 0), 0, 0)),
                pl.BlockSpec((RANK, tok), lambda p, y, ids: (0, 0)),
            ],
            scratch_shapes=[
                pltpu.VMEM((2 * RANK, outs), BF16),
                pltpu.VMEM((tok, outs), BF16),
                pltpu.SemaphoreType.DMA,
            ],
        ),
        out_shape=[half, half, jax.ShapeDtypeStruct((RANK, tok), F32)],
        compiler_params=params(48),
        cost_estimate=cost(6e9, error.size * 4, 2),
        name="error_sketch",
    )(jnp.reshape(core, (1,)), error, q_t, out_grad)


def sketch_rows_kernel(*refs, n_e, scale):
    e_refs, y_refs, x_ref, out = refs[:n_e], refs[n_e:-2], refs[-2], refs[-1]
    y = y_refs[0][...]
    for r in y_refs[1:]:
        y = y + r[...]
    both = dot(jnp.concatenate(split(y), axis=0), x_ref[...], 1, 0)
    total = (both[0:RANK, :] + both[RANK:, :]) * scale
    for r in e_refs:
        total = total + r[...]
    out[...] = total


def sketch_rows(e_list, y_list, acts, scale):
    vm = pl.BlockSpec(memory_space=pltpu.VMEM)
    return pl.pallas_call(
        functools.partial(sketch_rows_kernel, n_e=len(e_list), scale=scale),
        in_specs=[vm] * (1 + len(e_list) + len(y_list)),
        out_specs=vm,
        out_shape=jax.ShapeDtypeStruct((RANK, acts.shape[1]), F32),
        compiler_params=params(24),
        cost_estimate=cost(1e9, 3e6),
        name="sketch_rows",
    )(*e_list, *y_list, acts)


def basis_kernel(src, mine, other, out, sk, *, n_dp, chips, part):
    for k in range(chips):
        for e, ref in enumerate((mine, other)):
            at = pl.multiple_of(src[2 * k + e] * part, part)
            sk[:, pl.ds(at, part)] = ref[k] * (1.0 / n_dp)
    s = sk[...]
    gram = dot(s, s, 1, 1, lax.Precision.HIGHEST)
    row = lax.broadcasted_iota(jnp.int32, (RANK, RANK), 0)
    col = lax.broadcasted_iota(jnp.int32, (RANK, RANK), 1)
    eye = (row == col).astype(F32)
    m = jnp.concatenate([gram, eye, jnp.zeros((RANK, 2 * RANK), F32)], axis=1)
    index = lax.broadcasted_iota(jnp.int32, (RANK, 1), 0)
    for j in range(RANK - 1):
        factor = jnp.where(index > j, m[:, j : j + 1] / m[j : j + 1, j : j + 1], 0.0)
        m = m - factor * m[j : j + 1, :]
    diag = jnp.sum(jnp.where(row == col, m[:, 0:RANK], 0.0), axis=1, keepdims=True)
    inverse = m[:, RANK : 2 * RANK] / jnp.sqrt(diag)
    out[...] = dot(inverse, s, 1, 0, lax.Precision.HIGHEST)


def make_basis(src, mine, other, n_dp):
    chips, _, part = mine.shape
    din = 2 * chips * part
    vm = pl.BlockSpec(memory_space=pltpu.VMEM)
    return pl.pallas_call(
        functools.partial(basis_kernel, n_dp=n_dp, chips=chips, part=part),
        in_specs=[pl.BlockSpec(memory_space=pltpu.SMEM), vm, vm],
        out_specs=vm,
        out_shape=jax.ShapeDtypeStruct((RANK, din), F32),
        scratch_shapes=[pltpu.VMEM((RANK, din), F32)],
        compiler_params=params(24),
        cost_estimate=cost(6e9, 2e6),
        name="basis",
    )(src, mine, other)


def right_error_kernel(e_ref, b_ref, acc):
    @pl.when(pl.program_id(0) == 0)
    def _():
        acc[...] = jnp.zeros_like(acc)

    bh, bl = split(b_ref[...])
    eh, el = split(e_ref[...])
    main = dot(jnp.concatenate([bh, bl], axis=0), eh, 1, 0)
    acc[...] += main[0:RANK, :] + main[RANK:, :] + dot(bh, el, 1, 0)


def right_error(error, basis_t):
    din, outs = error.shape
    blk = 512
    return pl.pallas_call(
        right_error_kernel,
        grid=(din // blk,),
        in_specs=[
            pl.BlockSpec((blk, outs), lambda i: (i, 0)),
            pl.BlockSpec((RANK, blk), lambda i: (0, i)),
        ],
        out_specs=pl.BlockSpec((RANK, outs), lambda i: (0, 0)),
        out_shape=jax.ShapeDtypeStruct((RANK, outs), F32),
        compiler_params=params(48),
        cost_estimate=cost(8e9, error.size * 4, 1),
        name="right_error",
    )(error, basis_t)


def copies(sources, target, sems):
    made, at = [], 0
    for n, ref in enumerate(sources):
        size = ref.shape[0]
        made.append(pltpu.make_async_copy(ref, target.at[at : at + size], sems.at[n]))
        at += size
    return made


def right_grad_kernel(*refs, n_t, per, scale):
    b_ref, r_ref, g_ref = refs[1:4]
    x_refs = refs[4 : 4 + n_t * per]
    out, vacc, xbuf, sems = refs[4 + n_t * per :]
    r = pl.program_id(0)
    part = xbuf.shape[0] // n_t
    moves = copies(x_refs, xbuf, sems)

    @pl.when(r == 0)
    def _():
        for m in moves:
            m.start()
        vacc[...] = jnp.zeros_like(vacc)

    for n in range(n_t):

        @pl.when(r == n)
        def _(n=n):
            for m in moves[n * per : (n + 1) * per]:
                m.wait()

    both = jnp.concatenate(split(b_ref[...]), axis=0)
    v = dot(both, xbuf[pl.ds(pl.multiple_of(r * part, part), part), :], 1, 0)
    vacc[...] += v[0:RANK, :] + v[RANK:, :]

    @pl.when(r == n_t - 1)
    def _():
        w = dot(jnp.concatenate(split(vacc[...]), axis=0), g_ref[...], 1, 0)
        out[...] = r_ref[...] + (w[0:RANK, :] + w[RANK:, :]) * scale


def right_grad(src, basis_t, right_e, out_grad, pieces, scale):
    tok, outs = out_grad.shape
    n_t = src.shape[0]
    din = basis_t.shape[1]
    part = din // n_t
    same = lambda r, src: (0, 0)
    return pl.pallas_call(
        functools.partial(right_grad_kernel, n_t=n_t, per=len(pieces) // n_t, scale=scale),
        grid_spec=pltpu.PrefetchScalarGridSpec(
            num_scalar_prefetch=1,
            grid=(n_t,),
            in_specs=[
                pl.BlockSpec((RANK, part), lambda r, src: (0, src[r])),
                pl.BlockSpec((RANK, outs), same),
                pl.BlockSpec((tok, outs), same),
            ]
            + [pl.BlockSpec(memory_space=pl.ANY)] * len(pieces),
            out_specs=pl.BlockSpec((RANK, outs), same),
            scratch_shapes=[
                pltpu.VMEM((RANK, tok), F32),
                pltpu.VMEM((din, tok), BF16),
                pltpu.SemaphoreType.DMA((len(pieces),)),
            ],
        ),
        out_shape=jax.ShapeDtypeStruct((RANK, outs), F32),
        compiler_params=params(40),
        cost_estimate=cost(4e9, din * tok * 2),
        name="right_grad",
    )(src, basis_t, right_e, out_grad, *pieces)


def update_kernel(*refs, n_t, per, n_dp, scale):
    e_ref, b_ref, g_ref, q_ref = refs[1:5]
    x_refs = refs[5 : 5 + n_t * per]
    out, qt_out, qs, xbuf, sems = refs[5 + n_t * per :]
    r = pl.program_id(0)
    part = xbuf.shape[0] // n_t
    moves = copies(x_refs, xbuf, sems)

    @pl.when(r == 0)
    def _():
        for m in moves[: 2 * per]:
            m.start()
        q_t = q_ref[...] * (1.0 / n_dp)
        qt_out[...] = q_t
        high, low = split(q_t)
        qs[0:RANK, :] = high
        qs[RANK : 2 * RANK, :] = low
        qs[2 * RANK : 3 * RANK, :] = high

    bh, bl = split(b_ref[...].T)
    low_rank = dot(jnp.concatenate([bh, bh, bl], axis=1), qs[...], 1, 0)
    for n in range(n_t):

        @pl.when(r == n)
        def _(n=n):
            if n > 0:
                for m in moves[(n + 1) * per : (n + 2) * per]:
                    m.start()
            for m in moves[n * per : (n + 1) * per]:
                m.wait()

    x = xbuf[pl.ds(pl.multiple_of(r * part, part), part), :]
    out[...] = e_ref[...] + dot(x, g_ref[...], 1, 0) * scale - low_rank


def update_error(src, error, basis_t, out_grad, pieces, q_t, n_dp, scale):
    tok, outs = out_grad.shape
    n_t = src.shape[0]
    din = error.shape[0]
    part = din // n_t
    block = pl.BlockSpec((part, outs), lambda r, src: (src[r], 0))
    same = lambda r, src: (0, 0)
    return pl.pallas_call(
        functools.partial(
            update_kernel, n_t=n_t, per=len(pieces) // n_t, n_dp=n_dp, scale=scale
        ),
        grid_spec=pltpu.PrefetchScalarGridSpec(
            num_scalar_prefetch=1,
            grid=(n_t,),
            in_specs=[
                block,
                pl.BlockSpec((RANK, part), lambda r, src: (0, src[r])),
                pl.BlockSpec((tok, outs), same),
                pl.BlockSpec((RANK, outs), same),
            ]
            + [pl.BlockSpec(memory_space=pl.ANY)] * len(pieces),
            out_specs=[block, pl.BlockSpec((RANK, outs), same)],
            scratch_shapes=[
                pltpu.VMEM((3 * RANK, outs), BF16),
                pltpu.VMEM((din, tok), BF16),
                pltpu.SemaphoreType.DMA((len(pieces),)),
            ],
        ),
        out_shape=[
            jax.ShapeDtypeStruct(error.shape, F32),
            jax.ShapeDtypeStruct((RANK, outs), F32),
        ],
        compiler_params=params(56),
        cost_estimate=cost(9e9, error.size * 8 + din * tok * 2, 1),
        name="update_error",
    )(src, error, basis_t, out_grad, q_t, *pieces)


def near_kernel(ids, g_ref, gs_ref, w_ref, ws_ref, out):
    out[...] = dot(g_ref[...], w_ref[...], 1, 1) + dot(gs_ref[...], ws_ref[...], 1, 1)


def near_input_grad(me_t, g_own, g_sib, weight, w_sib):
    tok, outs = g_own.shape
    part = w_sib.shape[0]
    blk = min(256, part)
    per = part // blk
    whole = pl.BlockSpec((tok, outs), lambda i, ids: (0, 0))
    return pl.pallas_call(
        near_kernel,
        grid_spec=pltpu.PrefetchScalarGridSpec(
            num_scalar_prefetch=1,
            grid=(per,),
            in_specs=[
                whole,
                whole,
                pl.BlockSpec((blk, outs), lambda i, ids: (ids[0] * per + i, 0)),
                pl.BlockSpec((blk, outs), lambda i, ids: (i, 0)),
            ],
            out_specs=pl.BlockSpec((tok, blk), lambda i, ids: (0, i)),
        ),
        out_shape=jax.ShapeDtypeStruct((tok, part), F32),
        compiler_params=params(48),
        cost_estimate=cost(4 * tok * outs * part, 12e6, 2),
        name="input_grad_near",
    )(jnp.reshape(me_t, (1,)), g_own, g_sib, weight, w_sib)


def far_kernel(*refs, n_far):
    prev, w_ref = refs[0], refs[1]
    g_refs = refs[2:-3]
    out, gbuf, sems = refs[-3:]
    tok = prev.shape[0]
    moves = copies(g_refs, gbuf, sems)

    @pl.when(pl.program_id(0) == 0)
    def _():
        for m in moves:
            m.start()
        for m in moves:
            m.wait()

    width = gbuf.shape[1]
    total = prev[...]
    for n in range(n_far):
        rows = gbuf[n * tok : (n + 1) * tok, :]
        total = total + dot(rows, w_ref[:, n * width : (n + 1) * width], 1, 1)
    out[...] = total


def far_input_grad(prev, w_far, gs):
    outs = gs[0].shape[1]
    tok, part = prev.shape
    n_far = w_far.shape[1] // outs
    blk = min(256, part)
    to = pl.BlockSpec((tok, blk), lambda i: (0, i))
    return pl.pallas_call(
        functools.partial(far_kernel, n_far=n_far),
        grid=(part // blk,),
        in_specs=[to, pl.BlockSpec((blk, w_far.shape[1]), lambda i: (i, 0))]
        + [pl.BlockSpec(memory_space=pl.ANY)] * len(gs),
        out_specs=to,
        out_shape=jax.ShapeDtypeStruct((tok, part), F32),
        scratch_shapes=[
            pltpu.VMEM((n_far * tok, outs), BF16),
            pltpu.SemaphoreType.DMA((len(gs),)),
        ],
        input_output_aliases={0: 0},
        compiler_params=params(24),
        cost_estimate=cost(2 * n_far * tok * outs * part, 10e6, 1),
        name="input_grad_far",
    )(prev, w_far, *gs)


def after(value, *others):
    return lax.optimization_barrier((value, others))[0]


def per_device(activations, out_grad, weight, error, q_start):
    scale = 1.0 / math.sqrt(TOK_DEV)
    n_dp = lax.axis_size("dp")
    chips = lax.axis_size("chip")
    n_t = 2 * chips
    d = lax.axis_index("dp").astype(jnp.int32)
    y = lax.axis_index("chip").astype(jnp.int32)
    c = lax.axis_index("core").astype(jnp.int32)
    t = 2 * y + c
    tok, part = activations.shape
    outs = out_grad.shape[1]
    din = weight.shape[0]
    error = error[0]
    q_t = q_start.T
    steps = range(1, chips)
    share = part // n_dp

    def to_sibling(a):
        return lax.ppermute(a, "core", [(0, 1), (1, 0)])

    def to_chip(a, k, flip=0):
        pairs = [(i, ((i // 2 + k) % chips) * 2 + ((i % 2) ^ flip)) for i in range(n_t)]
        return lax.ppermute(a, ("chip", "core"), pairs)

    def to_replica(a, k):
        return lax.ppermute(a, "dp", [(i, i ^ k) for i in range(n_dp)])

    def over_replicas(a, chunks):
        rounds = [1 << i for i in range(n_dp.bit_length() - 1)]
        for i, k in enumerate(rounds):
            if i == len(rounds) - 1:
                a = after(a, chunks)
            a = a + to_replica(a, k)
        return a

    src = jnp.stack([((y - k) % chips) * 2 + (c ^ e) for k in range(chips) for e in range(2)])
    src = src.astype(jnp.int32)

    moves = [(k, e) for k in steps for e in range(2)]
    w_parts = []
    for k, e in moves:
        dest = ((y + k) % chips) * 2 + (c ^ e)
        w_parts.append(lax.dynamic_slice(weight, (dest * part + d * share, 0), (share, outs)))
    w_start = [to_chip(a, k, e) for a, (k, e) in zip(w_parts, moves)]
    send, keep, y_own = local_sketch(c, error, after(q_t, *w_parts), out_grad, chips, part)

    got = to_sibling(send)
    y_t = y_own + to_sibling(y_own)

    def block(k):
        at = (y + k) % chips
        return lax.dynamic_index_in_dim(keep, at, 0, False) + lax.dynamic_index_in_dim(got, at, 0, False)

    blocks = [block(k) for k in range(chips)]
    e_list = [blocks[0]] + [to_chip(blocks[k], k) for k in steps]
    y_list = [y_t] + [to_chip(y_t, k) for k in steps]

    n_chunk = 4
    high = part // n_chunk
    acts = after(activations, blocks, y_t)
    x_rows = [acts[:, i * high : (i + 1) * high].T for i in range(n_chunk)]
    sketch = sketch_rows(e_list, y_list, activations, scale)
    w_parts = after(w_start, sketch)
    w_far = lax.all_gather(jnp.concatenate(w_parts, axis=1), "dp", axis=0, tiled=True)
    x_rows[0:2] = after(x_rows[0:2], e_list, y_list)
    x_far = [[to_chip(a, k) for k in steps] for a in x_rows[0:2]]
    w_sib = lax.dynamic_slice(after(weight, sketch), ((t ^ 1) * part, 0), (part, outs))
    sketch = after(over_replicas(sketch, x_far[0]), x_far[1])
    mine = jnp.stack([sketch] + [to_chip(sketch, k) for k in steps])
    x_rows[2:4] = after(x_rows[2:4], mine)
    x_far += [[to_chip(a, k) for k in steps] for a in x_rows[2:4]]
    basis_t = make_basis(src, mine, to_sibling(mine), n_dp)
    right_e = right_error(error, basis_t)

    g_sib = to_sibling(out_grad)
    w_sib = to_sibling(w_sib)
    grad = near_input_grad(t, out_grad, g_sib, weight, after(w_sib, right_e, x_far[2]))

    x_far[0:2] = after(x_far[0:2], mine)
    x_far[2] = after(x_far[2], right_e)
    x_far[3] = after(x_far[3], grad)
    pieces = list(x_rows) + [to_sibling(a) for a in after(x_rows, mine)]
    for n in range(len(steps)):
        held = [a[n] for a in x_far]
        pieces += held + [to_sibling(a) for a in held]

    span = tok // n_chunk
    g_rows = after(out_grad, basis_t)
    g_far = [
        [to_chip(g_rows[i * span : (i + 1) * span], k) for k in steps] for i in range(n_chunk)
    ]
    right = after(right_grad(src, basis_t, right_e, out_grad, pieces, scale), g_far[0])
    right = after(over_replicas(right, ()), g_far[1])
    new_error, q_t = update_error(
        src, error, basis_t, out_grad, pieces, right, n_dp, scale
    )
    gs = []
    g_far[2:] = after(g_far[2:], q_t)
    for n in range(len(steps)):
        held = [a[n] for a in g_far]
        gs += held + [to_sibling(a) for a in held]
    grad = far_input_grad(grad, w_far, gs)
    return (grad, new_error[None], q_t.T)


def solution(mesh):
    n_dp, n_t = mesh.devices.shape
    mesh = jax.sharding.Mesh(mesh.devices.reshape(n_dp, n_t // 2, 2), ("dp", "chip", "core"))
    tensor = ("chip", "core")
    placed = (
        P("dp", tensor),
        P("dp", tensor),
        P(None, tensor),
        P("dp", None, tensor),
        P(tensor, None),
    )
    return jax.shard_map(
        per_device,
        mesh=mesh,
        in_specs=placed,
        out_specs=(P("dp", tensor), P("dp", None, tensor), P(tensor, None)),
        check_vma=False,
    )
```

```python
import functools
import math

import jax
import jax.numpy as jnp
from jax import lax
from jax.experimental import pallas as pl
from jax.experimental.pallas import tpu as pltpu
from jax.sharding import PartitionSpec as P

TOK_DEV = 1024
RANK = 32
MIB = 1 << 20
F32 = jnp.float32
BF16 = jnp.bfloat16


def dot(a, b, ca, cb, precision=None):
    return lax.dot_general(
        a, b, (((ca,), (cb,)), ((), ())), precision=precision, preferred_element_type=F32
    )


def split(a):
    high = a.astype(BF16)
    return high, (a - high.astype(F32)).astype(BF16)


def params(mib):
    return pltpu.CompilerParams(vmem_limit_bytes=mib * MIB)


def cost(flops, nbytes, weight=0.001):
    return pl.CostEstimate(
        flops=int(flops * weight), bytes_accessed=int(nbytes * weight), transcendentals=0
    )


def sketch_kernel(ids, e_ref, qt_ref, g_hbm, send_ref, keep_ref, y_ref, qs_ref, g_ref, sem):
    phase, y = pl.program_id(0), pl.program_id(1)
    move = pltpu.make_async_copy(g_hbm, g_ref, sem)

    @pl.when((phase == 0) & (y == 0))
    def _():
        move.start()
        high, low = split(qt_ref[...])
        qs_ref[0:RANK, :] = high
        qs_ref[RANK : 2 * RANK, :] = low

    high, low = split(e_ref[...])
    main = dot(high, qs_ref[...], 1, 1)
    rest = dot(low, qs_ref[0:RANK, :], 1, 1)
    rows = (main[:, 0:RANK] + main[:, RANK : 2 * RANK] + rest).T

    @pl.when(phase == 0)
    def _():
        send_ref[0] = rows

    @pl.when(phase == 1)
    def _():
        keep_ref[0] = rows

    @pl.when((phase == 1) & (y == pl.num_programs(1) - 1))
    def _():
        move.wait()
        both = dot(qs_ref[...], g_ref[...], 1, 1)
        y_ref[...] = both[0:RANK, :] + both[RANK : 2 * RANK, :]


def local_sketch(core, error, q_t, out_grad, chips, part):
    tok, outs = out_grad.shape

    def e_map(p, y, ids):
        return (2 * y + jnp.where(p == 0, 1 - ids[0], ids[0]), 0)

    half = jax.ShapeDtypeStruct((chips, RANK, part), F32)
    return pl.pallas_call(
        sketch_kernel,
        grid_spec=pltpu.PrefetchScalarGridSpec(
            num_scalar_prefetch=1,
            grid=(2, chips),
            in_specs=[
                pl.BlockSpec((part, outs), e_map),
                pl.BlockSpec((RANK, outs), lambda p, y, ids: (0, 0)),
                pl.BlockSpec(memory_space=pl.ANY),
            ],
            out_specs=[
                pl.BlockSpec((1, RANK, part), lambda p, y, ids: (jnp.where(p == 0, y, chips - 1), 0, 0)),
                pl.BlockSpec((1, RANK, part), lambda p, y, ids: (jnp.where(p == 1, y, 0), 0, 0)),
                pl.BlockSpec((RANK, tok), lambda p, y, ids: (0, 0)),
            ],
            scratch_shapes=[
                pltpu.VMEM((2 * RANK, outs), BF16),
                pltpu.VMEM((tok, outs), BF16),
                pltpu.SemaphoreType.DMA,
            ],
        ),
        out_shape=[half, half, jax.ShapeDtypeStruct((RANK, tok), F32)],
        compiler_params=params(60),
        cost_estimate=cost(6e9, error.size * 4, 2),
        name="error_sketch",
    )(jnp.reshape(core, (1,)), error, q_t, out_grad)


def sketch_rows_kernel(*refs, n_e, scale):
    e_refs, y_refs, x_ref, out = refs[:n_e], refs[n_e:-2], refs[-2], refs[-1]
    y = y_refs[0][...]
    for r in y_refs[1:]:
        y = y + r[...]
    both = dot(jnp.concatenate(split(y), axis=0), x_ref[...], 1, 0)
    total = (both[0:RANK, :] + both[RANK:, :]) * scale
    for r in e_refs:
        total = total + r[...]
    out[...] = total


def sketch_rows(e_list, y_list, acts, scale):
    vm = pl.BlockSpec(memory_space=pltpu.VMEM)
    return pl.pallas_call(
        functools.partial(sketch_rows_kernel, n_e=len(e_list), scale=scale),
        in_specs=[vm] * (1 + len(e_list) + len(y_list)),
        out_specs=vm,
        out_shape=jax.ShapeDtypeStruct((RANK, acts.shape[1]), F32),
        compiler_params=params(24),
        cost_estimate=cost(1e9, 3e6),
        name="sketch_rows",
    )(*e_list, *y_list, acts)


def basis_kernel(src, mine, other, out, sk, *, n_dp, chips, part):
    for k in range(chips):
        for e, ref in enumerate((mine, other)):
            at = pl.multiple_of(src[2 * k + e] * part, part)
            sk[:, pl.ds(at, part)] = ref[k] * (1.0 / n_dp)
    s = sk[...]
    gram = dot(s, s, 1, 1, lax.Precision.HIGHEST)
    row = lax.broadcasted_iota(jnp.int32, (RANK, RANK), 0)
    col = lax.broadcasted_iota(jnp.int32, (RANK, RANK), 1)
    eye = (row == col).astype(F32)
    m = jnp.concatenate([gram, eye, jnp.zeros((RANK, 2 * RANK), F32)], axis=1)
    index = lax.broadcasted_iota(jnp.int32, (RANK, 1), 0)
    for j in range(RANK - 1):
        factor = jnp.where(index > j, m[:, j : j + 1] / m[j : j + 1, j : j + 1], 0.0)
        m = m - factor * m[j : j + 1, :]
    diag = jnp.sum(jnp.where(row == col, m[:, 0:RANK], 0.0), axis=1, keepdims=True)
    inverse = m[:, RANK : 2 * RANK] / jnp.sqrt(diag)
    out[...] = dot(inverse, s, 1, 0, lax.Precision.HIGHEST)


def make_basis(src, mine, other, n_dp):
    chips, _, part = mine.shape
    din = 2 * chips * part
    vm = pl.BlockSpec(memory_space=pltpu.VMEM)
    return pl.pallas_call(
        functools.partial(basis_kernel, n_dp=n_dp, chips=chips, part=part),
        in_specs=[pl.BlockSpec(memory_space=pltpu.SMEM), vm, vm],
        out_specs=vm,
        out_shape=jax.ShapeDtypeStruct((RANK, din), F32),
        scratch_shapes=[pltpu.VMEM((RANK, din), F32)],
        compiler_params=params(24),
        cost_estimate=cost(6e9, 2e6),
        name="basis",
    )(src, mine, other)


def right_error_kernel(e_ref, b_ref, acc):
    @pl.when(pl.program_id(0) == 0)
    def _():
        acc[...] = jnp.zeros_like(acc)

    bh, bl = split(b_ref[...])
    eh, el = split(e_ref[...])
    main = dot(jnp.concatenate([bh, bl], axis=0), eh, 1, 0)
    acc[...] += main[0:RANK, :] + main[RANK:, :] + dot(bh, el, 1, 0)


def right_error(error, basis_t):
    din, outs = error.shape
    blk = 512
    return pl.pallas_call(
        right_error_kernel,
        grid=(din // blk,),
        in_specs=[
            pl.BlockSpec((blk, outs), lambda i: (i, 0)),
            pl.BlockSpec((RANK, blk), lambda i: (0, i)),
        ],
        out_specs=pl.BlockSpec((RANK, outs), lambda i: (0, 0)),
        out_shape=jax.ShapeDtypeStruct((RANK, outs), F32),
        compiler_params=params(48),
        cost_estimate=cost(8e9, error.size * 4, 1),
        name="right_error",
    )(error, basis_t)


def copies(sources, target, sems):
    made, at = [], 0
    for n, ref in enumerate(sources):
        size = ref.shape[0]
        made.append(pltpu.make_async_copy(ref, target.at[at : at + size], sems.at[n]))
        at += size
    return made


def right_grad_kernel(*refs, n_t, per, scale):
    b_ref, r_ref, g_ref = refs[1:4]
    x_refs = refs[4 : 4 + n_t * per]
    out, vacc, xbuf, sems = refs[4 + n_t * per :]
    r = pl.program_id(0)
    part = xbuf.shape[0] // n_t
    moves = copies(x_refs, xbuf, sems)

    @pl.when(r == 0)
    def _():
        for m in moves:
            m.start()
        vacc[...] = jnp.zeros_like(vacc)

    for n in range(n_t):

        @pl.when(r == n)
        def _(n=n):
            for m in moves[n * per : (n + 1) * per]:
                m.wait()

    both = jnp.concatenate(split(b_ref[...]), axis=0)
    v = dot(both, xbuf[pl.ds(pl.multiple_of(r * part, part), part), :], 1, 0)
    vacc[...] += v[0:RANK, :] + v[RANK:, :]

    @pl.when(r == n_t - 1)
    def _():
        w = dot(jnp.concatenate(split(vacc[...]), axis=0), g_ref[...], 1, 0)
        out[...] = r_ref[...] + (w[0:RANK, :] + w[RANK:, :]) * scale


def right_grad(src, basis_t, right_e, out_grad, pieces, scale):
    tok, outs = out_grad.shape
    n_t = src.shape[0]
    din = basis_t.shape[1]
    part = din // n_t
    same = lambda r, src: (0, 0)
    return pl.pallas_call(
        functools.partial(right_grad_kernel, n_t=n_t, per=len(pieces) // n_t, scale=scale),
        grid_spec=pltpu.PrefetchScalarGridSpec(
            num_scalar_prefetch=1,
            grid=(n_t,),
            in_specs=[
                pl.BlockSpec((RANK, part), lambda r, src: (0, src[r])),
                pl.BlockSpec((RANK, outs), same),
                pl.BlockSpec((tok, outs), same),
            ]
            + [pl.BlockSpec(memory_space=pl.ANY)] * len(pieces),
            out_specs=pl.BlockSpec((RANK, outs), same),
            scratch_shapes=[
                pltpu.VMEM((RANK, tok), F32),
                pltpu.VMEM((din, tok), BF16),
                pltpu.SemaphoreType.DMA((len(pieces),)),
            ],
        ),
        out_shape=jax.ShapeDtypeStruct((RANK, outs), F32),
        compiler_params=params(40),
        cost_estimate=cost(4e9, din * tok * 2),
        name="right_grad",
    )(src, basis_t, right_e, out_grad, *pieces)


def update_kernel(*refs, n_t, per, n_dp, scale):
    e_ref, b_ref, g_ref, q_ref = refs[1:5]
    x_refs = refs[5 : 5 + n_t * per]
    out, qt_out, qs, xbuf, sems = refs[5 + n_t * per :]
    r = pl.program_id(0)
    part = xbuf.shape[0] // n_t
    moves = copies(x_refs, xbuf, sems)

    @pl.when(r == 0)
    def _():
        for m in moves[: 2 * per]:
            m.start()
        q_t = q_ref[...] * (1.0 / n_dp)
        qt_out[...] = q_t
        high, low = split(q_t)
        qs[0:RANK, :] = high
        qs[RANK : 2 * RANK, :] = low
        qs[2 * RANK : 3 * RANK, :] = high

    bh, bl = split(b_ref[...].T)
    low_rank = dot(jnp.concatenate([bh, bh, bl], axis=1), qs[...], 1, 0)
    for n in range(n_t):

        @pl.when(r == n)
        def _(n=n):
            if n > 0:
                for m in moves[(n + 1) * per : (n + 2) * per]:
                    m.start()
            for m in moves[n * per : (n + 1) * per]:
                m.wait()

    x = xbuf[pl.ds(pl.multiple_of(r * part, part), part), :]
    out[...] = e_ref[...] + dot(x, g_ref[...], 1, 0) * scale - low_rank


def update_error(src, error, basis_t, out_grad, pieces, q_t, n_dp, scale):
    tok, outs = out_grad.shape
    n_t = src.shape[0]
    din = error.shape[0]
    part = din // n_t
    block = pl.BlockSpec((part, outs), lambda r, src: (src[r], 0))
    same = lambda r, src: (0, 0)
    return pl.pallas_call(
        functools.partial(
            update_kernel, n_t=n_t, per=len(pieces) // n_t, n_dp=n_dp, scale=scale
        ),
        grid_spec=pltpu.PrefetchScalarGridSpec(
            num_scalar_prefetch=1,
            grid=(n_t,),
            in_specs=[
                block,
                pl.BlockSpec((RANK, part), lambda r, src: (0, src[r])),
                pl.BlockSpec((tok, outs), same),
                pl.BlockSpec((RANK, outs), same),
            ]
            + [pl.BlockSpec(memory_space=pl.ANY)] * len(pieces),
            out_specs=[block, pl.BlockSpec((RANK, outs), same)],
            scratch_shapes=[
                pltpu.VMEM((3 * RANK, outs), BF16),
                pltpu.VMEM((din, tok), BF16),
                pltpu.SemaphoreType.DMA((len(pieces),)),
            ],
        ),
        out_shape=[
            jax.ShapeDtypeStruct(error.shape, F32),
            jax.ShapeDtypeStruct((RANK, outs), F32),
        ],
        compiler_params=params(56),
        cost_estimate=cost(9e9, error.size * 8 + din * tok * 2, 1),
        name="update_error",
    )(src, error, basis_t, out_grad, q_t, *pieces)


def near_kernel(ids, g_ref, gs_ref, w_ref, ws_ref, out):
    out[...] = dot(g_ref[...], w_ref[...], 1, 1) + dot(gs_ref[...], ws_ref[...], 1, 1)


def near_input_grad(me_t, g_own, g_sib, weight, w_sib):
    tok, outs = g_own.shape
    part = w_sib.shape[0]
    blk = min(256, part)
    per = part // blk
    whole = pl.BlockSpec((tok, outs), lambda i, ids: (0, 0))
    return pl.pallas_call(
        near_kernel,
        grid_spec=pltpu.PrefetchScalarGridSpec(
            num_scalar_prefetch=1,
            grid=(per,),
            in_specs=[
                whole,
                whole,
                pl.BlockSpec((blk, outs), lambda i, ids: (ids[0] * per + i, 0)),
                pl.BlockSpec((blk, outs), lambda i, ids: (i, 0)),
            ],
            out_specs=pl.BlockSpec((tok, blk), lambda i, ids: (0, i)),
        ),
        out_shape=jax.ShapeDtypeStruct((tok, part), F32),
        compiler_params=params(48),
        cost_estimate=cost(4 * tok * outs * part, 12e6, 2),
        name="input_grad_near",
    )(jnp.reshape(me_t, (1,)), g_own, g_sib, weight, w_sib)


def far_kernel(*refs, n_far):
    prev, w_ref = refs[0], refs[1]
    g_refs = refs[2:-3]
    out, gbuf, sems = refs[-3:]
    tok = prev.shape[0]
    moves = copies(g_refs, gbuf, sems)

    @pl.when(pl.program_id(0) == 0)
    def _():
        for m in moves:
            m.start()
        for m in moves:
            m.wait()

    width = gbuf.shape[1]
    total = prev[...]
    for n in range(n_far):
        rows = gbuf[n * tok : (n + 1) * tok, :]
        total = total + dot(rows, w_ref[:, n * width : (n + 1) * width], 1, 1)
    out[...] = total


def far_input_grad(prev, w_far, gs, start):
    outs = gs[0].shape[1]
    tok, part = prev.shape
    n_far = w_far.shape[1] // outs
    rows = sum(g.shape[0] for g in gs) // n_far
    blk = min(256, part)
    to = pl.BlockSpec((rows, blk), lambda i: (start // rows, i))
    return pl.pallas_call(
        functools.partial(far_kernel, n_far=n_far),
        grid=(part // blk,),
        in_specs=[to, pl.BlockSpec((blk, w_far.shape[1]), lambda i: (i, 0))]
        + [pl.BlockSpec(memory_space=pl.ANY)] * len(gs),
        out_specs=to,
        out_shape=jax.ShapeDtypeStruct((tok, part), F32),
        scratch_shapes=[
            pltpu.VMEM((n_far * rows, outs), BF16),
            pltpu.SemaphoreType.DMA((len(gs),)),
        ],
        input_output_aliases={0: 0},
        compiler_params=params(24),
        cost_estimate=cost(2 * n_far * rows * outs * part, 10e6, 1),
        name="input_grad_far",
    )(prev, w_far, *gs)


def after(value, *others):
    return lax.optimization_barrier((value, others))[0]


def per_device(activations, out_grad, weight, error, q_start):
    scale = 1.0 / math.sqrt(TOK_DEV)
    n_dp = lax.axis_size("dp")
    chips = lax.axis_size("chip")
    n_t = 2 * chips
    d = lax.axis_index("dp").astype(jnp.int32)
    y = lax.axis_index("chip").astype(jnp.int32)
    c = lax.axis_index("core").astype(jnp.int32)
    t = 2 * y + c
    tok, part = activations.shape
    outs = out_grad.shape[1]
    din = weight.shape[0]
    error = error[0]
    q_t = q_start.T
    steps = range(1, chips)
    share = part // n_dp

    def to_sibling(a):
        return lax.ppermute(a, "core", [(0, 1), (1, 0)])

    def to_chip(a, k, flip=0):
        pairs = [(i, ((i // 2 + k) % chips) * 2 + ((i % 2) ^ flip)) for i in range(n_t)]
        return lax.ppermute(a, ("chip", "core"), pairs)

    def to_replica(a, k):
        return lax.ppermute(a, "dp", [(i, i ^ k) for i in range(n_dp)])

    def over_replicas(a, beside, chunks):
        rounds = [1 << i for i in range(n_dp.bit_length() - 1)]
        for i, k in enumerate(rounds):
            if i == len(rounds) - 1:
                a = after(a, chunks)
            got = to_replica(a, k)
            a = a + (after(got, beside) if i == 0 else got)
        return a

    src = jnp.stack([((y - k) % chips) * 2 + (c ^ e) for k in range(chips) for e in range(2)])
    src = src.astype(jnp.int32)

    moves = [(k, e) for k in steps for e in range(2)]
    w_parts = []
    for k, e in moves:
        dest = ((y + k) % chips) * 2 + (c ^ e)
        w_parts.append(lax.dynamic_slice(weight, (dest * part + d * share, 0), (share, outs)))
    w_start = [to_chip(a, k, e) for a, (k, e) in zip(w_parts, moves)]
    send, keep, y_own = local_sketch(c, error, after(q_t, *w_parts), out_grad, chips, part)

    w_parts = after(w_start, send)

    got = to_sibling(send)
    y_t = y_own + to_sibling(y_own)

    def block(k):
        at = (y + k) % chips
        return lax.dynamic_index_in_dim(keep, at, 0, False) + lax.dynamic_index_in_dim(got, at, 0, False)

    blocks = [block(k) for k in range(chips)]
    e_list = [blocks[0]] + [to_chip(blocks[k], k) for k in steps]
    y_list = [y_t] + [to_chip(y_t, k) for k in steps]

    n_chunk = 4
    high = part // n_chunk
    acts = after(activations, blocks, y_t)
    x_rows = [acts[:, i * high : (i + 1) * high].T for i in range(n_chunk)]
    sketch = sketch_rows(after(e_list, x_rows), y_list, activations, scale)
    w_far = lax.all_gather(jnp.concatenate(w_parts, axis=1), "dp", axis=0, tiled=True)
    x_rows[0:2] = after(x_rows[0:2], e_list, y_list)
    x_far = [[to_chip(a, k) for k in steps] for a in x_rows[0:2]]
    w_sib = lax.dynamic_slice(after(weight, sketch), ((t ^ 1) * part, 0), (part, outs))
    sketch = after(over_replicas(sketch, w_sib, x_far[0]), x_far[1])
    mine = jnp.stack([sketch] + [to_chip(sketch, k) for k in steps])
    x_rows[2:4] = after(x_rows[2:4], mine)
    x_far += [[to_chip(a, k) for k in steps] for a in x_rows[2:4]]
    basis_t = make_basis(src, mine, to_sibling(mine), n_dp)
    right_e = right_error(error, basis_t)

    g_sib = to_sibling(out_grad)
    w_sib = to_sibling(w_sib)
    grad = near_input_grad(t, out_grad, g_sib, weight, after(w_sib, right_e, x_far[2]))

    x_far[0:2] = after(x_far[0:2], mine)
    x_far[2] = after(x_far[2], right_e)
    x_far[3] = after(x_far[3], grad)
    pieces = list(x_rows) + [to_sibling(a) for a in after(x_rows, mine)]
    for n in range(len(steps)):
        held = [a[n] for a in x_far]
        pieces += held + [to_sibling(a) for a in held]

    cuts = [0, tok // 8, tok // 2, 3 * tok // 4, tok]
    g_rows = after(out_grad, basis_t)
    g_far = [[to_chip(g_rows[lo:hi], k) for k in steps] for lo, hi in zip(cuts[:-1], cuts[1:])]
    right = after(right_grad(src, basis_t, right_e, out_grad, pieces, scale), g_far[0])
    right = after(over_replicas(right, (), ()), g_far[1])
    new_error, q_t = update_error(
        src, error, basis_t, out_grad, pieces, right, n_dp, scale
    )

    def far(grad, chunks, start):
        gs = []
        for n in range(len(steps)):
            held = [a[n] for a in chunks]
            gs += held + [to_sibling(a) for a in held]
        return far_input_grad(grad, w_far, gs, start)

    g_far[2] = after(g_far[2], q_t)
    grad = far(after(grad, q_t), g_far[0:2], 0)
    for i in (2, 3):
        grad = far(grad, [g_far[i] if i == 2 else after(g_far[i], grad)], cuts[i])
    return (grad, new_error[None], q_t.T)


def solution(mesh):
    n_dp, n_t = mesh.devices.shape
    mesh = jax.sharding.Mesh(mesh.devices.reshape(n_dp, n_t // 2, 2), ("dp", "chip", "core"))
    tensor = ("chip", "core")
    placed = (
        P("dp", tensor),
        P("dp", tensor),
        P(None, tensor),
        P("dp", None, tensor),
        P(tensor, None),
    )
    return jax.shard_map(
        per_device,
        mesh=mesh,
        in_specs=placed,
        out_specs=(P("dp", tensor), P("dp", None, tensor), P(tensor, None)),
        check_vma=False,
    )
```

```python
import functools
import math

import jax
import jax.numpy as jnp
from jax import lax
from jax.experimental import pallas as pl
from jax.experimental.pallas import tpu as pltpu
from jax.sharding import PartitionSpec as P

TOK_DEV = 1024
RANK = 32
MIB = 1 << 20
F32 = jnp.float32
BF16 = jnp.bfloat16


def dot(a, b, ca, cb, precision=None):
    return lax.dot_general(
        a, b, (((ca,), (cb,)), ((), ())), precision=precision, preferred_element_type=F32
    )


def split(a):
    high = a.astype(BF16)
    return high, (a - high.astype(F32)).astype(BF16)


def params(mib):
    return pltpu.CompilerParams(vmem_limit_bytes=mib * MIB)


def cost(flops, nbytes, weight=0.001):
    return pl.CostEstimate(
        flops=int(flops * weight), bytes_accessed=int(nbytes * weight), transcendentals=0
    )


def sketch_kernel(ids, e_ref, qt_ref, g_hbm, w_hbm, send_ref, keep_ref, y_ref, w_out, qs_ref, g_ref, sem, w_sem):
    phase, y = pl.program_id(0), pl.program_id(1)
    move = pltpu.make_async_copy(g_hbm, g_ref, sem)
    part = w_out.shape[0]
    rows = pl.ds(pl.multiple_of(ids[1] * part, part), part)
    w_move = pltpu.make_async_copy(w_hbm.at[rows], w_out, w_sem)

    @pl.when((phase == 0) & (y == 0))
    def _():
        move.start()
        w_move.start()
        high, low = split(qt_ref[...])
        qs_ref[0:RANK, :] = high
        qs_ref[RANK : 2 * RANK, :] = low

    high, low = split(e_ref[...])
    main = dot(high, qs_ref[...], 1, 1)
    rest = dot(low, qs_ref[0:RANK, :], 1, 1)
    rows = (main[:, 0:RANK] + main[:, RANK : 2 * RANK] + rest).T

    @pl.when(phase == 0)
    def _():
        send_ref[0] = rows

    @pl.when(phase == 1)
    def _():
        keep_ref[0] = rows

    @pl.when((phase == 1) & (y == pl.num_programs(1) - 1))
    def _():
        move.wait()
        w_move.wait()
        both = dot(qs_ref[...], g_ref[...], 1, 1)
        y_ref[...] = both[0:RANK, :] + both[RANK : 2 * RANK, :]


def local_sketch(ids, error, q_t, out_grad, weight, chips, part):
    tok, outs = out_grad.shape

    def e_map(p, y, ids):
        return (2 * y + jnp.where(p == 0, 1 - ids[0], ids[0]), 0)

    half = jax.ShapeDtypeStruct((chips, RANK, part), F32)
    return pl.pallas_call(
        sketch_kernel,
        grid_spec=pltpu.PrefetchScalarGridSpec(
            num_scalar_prefetch=1,
            grid=(2, chips),
            in_specs=[
                pl.BlockSpec((part, outs), e_map),
                pl.BlockSpec((RANK, outs), lambda p, y, ids: (0, 0)),
                pl.BlockSpec(memory_space=pl.ANY),
                pl.BlockSpec(memory_space=pl.ANY),
            ],
            out_specs=[
                pl.BlockSpec((1, RANK, part), lambda p, y, ids: (jnp.where(p == 0, y, chips - 1), 0, 0)),
                pl.BlockSpec((1, RANK, part), lambda p, y, ids: (jnp.where(p == 1, y, 0), 0, 0)),
                pl.BlockSpec((RANK, tok), lambda p, y, ids: (0, 0)),
                pl.BlockSpec(memory_space=pl.ANY),
            ],
            scratch_shapes=[
                pltpu.VMEM((2 * RANK, outs), BF16),
                pltpu.VMEM((tok, outs), BF16),
                pltpu.SemaphoreType.DMA,
                pltpu.SemaphoreType.DMA,
            ],
        ),
        out_shape=[
            half,
            half,
            jax.ShapeDtypeStruct((RANK, tok), F32),
            jax.ShapeDtypeStruct((part, outs), BF16),
        ],
        compiler_params=params(60),
        cost_estimate=cost(6e9, error.size * 4, 2),
        name="error_sketch",
    )(ids, error, q_t, out_grad, weight)


def sketch_rows_kernel(*refs, n_e, scale):
    e_refs, y_refs, x_ref, out = refs[:n_e], refs[n_e:-2], refs[-2], refs[-1]
    y = y_refs[0][...]
    for r in y_refs[1:]:
        y = y + r[...]
    both = dot(jnp.concatenate(split(y), axis=0), x_ref[...], 1, 0)
    total = (both[0:RANK, :] + both[RANK:, :]) * scale
    for r in e_refs:
        total = total + r[...]
    out[...] = total


def sketch_rows(e_list, y_list, acts, scale):
    vm = pl.BlockSpec(memory_space=pltpu.VMEM)
    return pl.pallas_call(
        functools.partial(sketch_rows_kernel, n_e=len(e_list), scale=scale),
        in_specs=[vm] * (1 + len(e_list) + len(y_list)),
        out_specs=vm,
        out_shape=jax.ShapeDtypeStruct((RANK, acts.shape[1]), F32),
        compiler_params=params(24),
        cost_estimate=cost(1e9, 3e6),
        name="sketch_rows",
    )(*e_list, *y_list, acts)


def basis_kernel(src, mine, other, out, sk, *, n_dp, chips, part):
    for k in range(chips):
        for e, ref in enumerate((mine, other)):
            at = pl.multiple_of(src[2 * k + e] * part, part)
            sk[:, pl.ds(at, part)] = ref[k] * (1.0 / n_dp)
    s = sk[...]
    gram = dot(s, s, 1, 1, lax.Precision.HIGHEST)
    row = lax.broadcasted_iota(jnp.int32, (RANK, RANK), 0)
    col = lax.broadcasted_iota(jnp.int32, (RANK, RANK), 1)
    eye = (row == col).astype(F32)
    m = jnp.concatenate([gram, eye, jnp.zeros((RANK, 2 * RANK), F32)], axis=1)
    index = lax.broadcasted_iota(jnp.int32, (RANK, 1), 0)
    for j in range(RANK - 1):
        factor = jnp.where(index > j, m[:, j : j + 1] / m[j : j + 1, j : j + 1], 0.0)
        m = m - factor * m[j : j + 1, :]
    diag = jnp.sum(jnp.where(row == col, m[:, 0:RANK], 0.0), axis=1, keepdims=True)
    inverse = m[:, RANK : 2 * RANK] / jnp.sqrt(diag)
    out[...] = dot(inverse, s, 1, 0, lax.Precision.HIGHEST)


def make_basis(src, mine, other, n_dp):
    chips, _, part = mine.shape
    din = 2 * chips * part
    vm = pl.BlockSpec(memory_space=pltpu.VMEM)
    return pl.pallas_call(
        functools.partial(basis_kernel, n_dp=n_dp, chips=chips, part=part),
        in_specs=[pl.BlockSpec(memory_space=pltpu.SMEM), vm, vm],
        out_specs=vm,
        out_shape=jax.ShapeDtypeStruct((RANK, din), F32),
        scratch_shapes=[pltpu.VMEM((RANK, din), F32)],
        compiler_params=params(24),
        cost_estimate=cost(6e9, 2e6),
        name="basis",
    )(src, mine, other)


def right_error_kernel(e_ref, b_ref, g_hbm, acc, *rest, cuts):
    i = pl.program_id(0)
    outs, sems = rest[:-1], rest[-1]
    moves = [
        pltpu.make_async_copy(g_hbm.at[lo:hi], outs[n], sems.at[n])
        for n, (lo, hi) in enumerate(zip(cuts[:-1], cuts[1:]))
    ]

    @pl.when(i == 0)
    def _():
        for m in moves:
            m.start()
        acc[...] = jnp.zeros_like(acc)

    @pl.when(i == pl.num_programs(0) - 1)
    def _():
        for m in moves:
            m.wait()

    bh, bl = split(b_ref[...])
    eh, el = split(e_ref[...])
    main = dot(jnp.concatenate([bh, bl], axis=0), eh, 1, 0)
    acc[...] += main[0:RANK, :] + main[RANK:, :] + dot(bh, el, 1, 0)


def right_error(error, basis_t, out_grad, cuts):
    din, outs = error.shape
    blk = 512
    chunks = [jax.ShapeDtypeStruct((hi - lo, outs), BF16) for lo, hi in zip(cuts[:-1], cuts[1:])]
    anywhere = pl.BlockSpec(memory_space=pl.ANY)
    made = pl.pallas_call(
        functools.partial(right_error_kernel, cuts=cuts),
        grid=(din // blk,),
        in_specs=[
            pl.BlockSpec((blk, outs), lambda i: (i, 0)),
            pl.BlockSpec((RANK, blk), lambda i: (0, i)),
            anywhere,
        ],
        out_specs=[pl.BlockSpec((RANK, outs), lambda i: (0, 0))] + [anywhere] * len(chunks),
        out_shape=[jax.ShapeDtypeStruct((RANK, outs), F32)] + chunks,
        scratch_shapes=[pltpu.SemaphoreType.DMA((len(chunks),))],
        compiler_params=params(48),
        cost_estimate=cost(8e9, error.size * 4, 1),
        name="right_error",
    )(error, basis_t, out_grad)
    return made[0], made[1:]


def copies(sources, target, sems):
    made, at = [], 0
    for n, ref in enumerate(sources):
        size = ref.shape[0]
        made.append(pltpu.make_async_copy(ref, target.at[at : at + size], sems.at[n]))
        at += size
    return made


def right_grad_kernel(*refs, n_t, per, scale):
    b_ref, r_ref, g_ref = refs[1:4]
    x_refs = refs[4 : 4 + n_t * per]
    out, vacc, xbuf, sems = refs[4 + n_t * per :]
    r = pl.program_id(0)
    part = xbuf.shape[0] // n_t
    moves = copies(x_refs, xbuf, sems)

    @pl.when(r == 0)
    def _():
        for m in moves:
            m.start()
        vacc[...] = jnp.zeros_like(vacc)

    for n in range(n_t):

        @pl.when(r == n)
        def _(n=n):
            for m in moves[n * per : (n + 1) * per]:
                m.wait()

    both = jnp.concatenate(split(b_ref[...]), axis=0)
    v = dot(both, xbuf[pl.ds(pl.multiple_of(r * part, part), part), :], 1, 0)
    vacc[...] += v[0:RANK, :] + v[RANK:, :]

    @pl.when(r == n_t - 1)
    def _():
        w = dot(jnp.concatenate(split(vacc[...]), axis=0), g_ref[...], 1, 0)
        out[...] = r_ref[...] + (w[0:RANK, :] + w[RANK:, :]) * scale


def right_grad(src, basis_t, right_e, out_grad, pieces, scale):
    tok, outs = out_grad.shape
    n_t = src.shape[0]
    din = basis_t.shape[1]
    part = din // n_t
    same = lambda r, src: (0, 0)
    return pl.pallas_call(
        functools.partial(right_grad_kernel, n_t=n_t, per=len(pieces) // n_t, scale=scale),
        grid_spec=pltpu.PrefetchScalarGridSpec(
            num_scalar_prefetch=1,
            grid=(n_t,),
            in_specs=[
                pl.BlockSpec((RANK, part), lambda r, src: (0, src[r])),
                pl.BlockSpec((RANK, outs), same),
                pl.BlockSpec((tok, outs), same),
            ]
            + [pl.BlockSpec(memory_space=pl.ANY)] * len(pieces),
            out_specs=pl.BlockSpec((RANK, outs), same),
            scratch_shapes=[
                pltpu.VMEM((RANK, tok), F32),
                pltpu.VMEM((din, tok), BF16),
                pltpu.SemaphoreType.DMA((len(pieces),)),
            ],
        ),
        out_shape=jax.ShapeDtypeStruct((RANK, outs), F32),
        compiler_params=params(40),
        cost_estimate=cost(4e9, din * tok * 2),
        name="right_grad",
    )(src, basis_t, right_e, out_grad, *pieces)


def update_kernel(*refs, n_t, per, n_dp, scale):
    e_ref, b_ref, g_ref, q_ref = refs[1:5]
    x_refs = refs[5 : 5 + n_t * per]
    out, qt_out, qs, xbuf, sems = refs[5 + n_t * per :]
    r = pl.program_id(0)
    part = xbuf.shape[0] // n_t
    moves = copies(x_refs, xbuf, sems)

    @pl.when(r == 0)
    def _():
        for m in moves[: 2 * per]:
            m.start()
        q_t = q_ref[...] * (1.0 / n_dp)
        qt_out[...] = q_t
        high, low = split(q_t)
        qs[0:RANK, :] = high
        qs[RANK : 2 * RANK, :] = low
        qs[2 * RANK : 3 * RANK, :] = high

    bh, bl = split(b_ref[...].T)
    low_rank = dot(jnp.concatenate([bh, bh, bl], axis=1), qs[...], 1, 0)
    for n in range(n_t):

        @pl.when(r == n)
        def _(n=n):
            if n > 0:
                for m in moves[(n + 1) * per : (n + 2) * per]:
                    m.start()
            for m in moves[n * per : (n + 1) * per]:
                m.wait()

    x = xbuf[pl.ds(pl.multiple_of(r * part, part), part), :]
    out[...] = e_ref[...] + dot(x, g_ref[...], 1, 0) * scale - low_rank


def update_error(src, error, basis_t, out_grad, pieces, q_t, n_dp, scale):
    tok, outs = out_grad.shape
    n_t = src.shape[0]
    din = error.shape[0]
    part = din // n_t
    block = pl.BlockSpec((part, outs), lambda r, src: (src[r], 0))
    same = lambda r, src: (0, 0)
    return pl.pallas_call(
        functools.partial(
            update_kernel, n_t=n_t, per=len(pieces) // n_t, n_dp=n_dp, scale=scale
        ),
        grid_spec=pltpu.PrefetchScalarGridSpec(
            num_scalar_prefetch=1,
            grid=(n_t,),
            in_specs=[
                block,
                pl.BlockSpec((RANK, part), lambda r, src: (0, src[r])),
                pl.BlockSpec((tok, outs), same),
                pl.BlockSpec((RANK, outs), same),
            ]
            + [pl.BlockSpec(memory_space=pl.ANY)] * len(pieces),
            out_specs=[block, pl.BlockSpec((RANK, outs), same)],
            scratch_shapes=[
                pltpu.VMEM((3 * RANK, outs), BF16),
                pltpu.VMEM((din, tok), BF16),
                pltpu.SemaphoreType.DMA((len(pieces),)),
            ],
        ),
        out_shape=[
            jax.ShapeDtypeStruct(error.shape, F32),
            jax.ShapeDtypeStruct((RANK, outs), F32),
        ],
        compiler_params=params(56),
        cost_estimate=cost(9e9, error.size * 8 + din * tok * 2, 1),
        name="update_error",
    )(src, error, basis_t, out_grad, q_t, *pieces)


def near_kernel(ids, g_ref, gs_ref, w_ref, ws_ref, out):
    out[...] = dot(g_ref[...], w_ref[...], 1, 1) + dot(gs_ref[...], ws_ref[...], 1, 1)


def near_input_grad(me_t, g_own, g_sib, weight, w_sib):
    tok, outs = g_own.shape
    part = w_sib.shape[0]
    blk = min(256, part)
    per = part // blk
    whole = pl.BlockSpec((tok, outs), lambda i, ids: (0, 0))
    return pl.pallas_call(
        near_kernel,
        grid_spec=pltpu.PrefetchScalarGridSpec(
            num_scalar_prefetch=1,
            grid=(per,),
            in_specs=[
                whole,
                whole,
                pl.BlockSpec((blk, outs), lambda i, ids: (ids[0] * per + i, 0)),
                pl.BlockSpec((blk, outs), lambda i, ids: (i, 0)),
            ],
            out_specs=pl.BlockSpec((tok, blk), lambda i, ids: (0, i)),
        ),
        out_shape=jax.ShapeDtypeStruct((tok, part), F32),
        compiler_params=params(48),
        cost_estimate=cost(4 * tok * outs * part, 12e6, 2),
        name="input_grad_near",
    )(jnp.reshape(me_t, (1,)), g_own, g_sib, weight, w_sib)


def far_kernel(*refs, n_far):
    prev, w_ref = refs[0], refs[1]
    g_refs = refs[2:-3]
    out, gbuf, sems = refs[-3:]
    tok = prev.shape[0]
    moves = copies(g_refs, gbuf, sems)

    @pl.when(pl.program_id(0) == 0)
    def _():
        for m in moves:
            m.start()
        for m in moves:
            m.wait()

    width = gbuf.shape[1]
    total = prev[...]
    for n in range(n_far):
        rows = gbuf[n * tok : (n + 1) * tok, :]
        total = total + dot(rows, w_ref[:, n * width : (n + 1) * width], 1, 1)
    out[...] = total


def far_input_grad(prev, w_far, gs, start):
    outs = gs[0].shape[1]
    tok, part = prev.shape
    n_far = w_far.shape[1] // outs
    rows = sum(g.shape[0] for g in gs) // n_far
    blk = min(256, part)
    to = pl.BlockSpec((rows, blk), lambda i: (start // rows, i))
    return pl.pallas_call(
        functools.partial(far_kernel, n_far=n_far),
        grid=(part // blk,),
        in_specs=[to, pl.BlockSpec((blk, w_far.shape[1]), lambda i: (i, 0))]
        + [pl.BlockSpec(memory_space=pl.ANY)] * len(gs),
        out_specs=to,
        out_shape=jax.ShapeDtypeStruct((tok, part), F32),
        scratch_shapes=[
            pltpu.VMEM((n_far * rows, outs), BF16),
            pltpu.SemaphoreType.DMA((len(gs),)),
        ],
        input_output_aliases={0: 0},
        compiler_params=params(24),
        cost_estimate=cost(2 * n_far * rows * outs * part, 10e6, 1),
        name="input_grad_far",
    )(prev, w_far, *gs)


def after(value, *others):
    return lax.optimization_barrier((value, others))[0]


def per_device(activations, out_grad, weight, error, q_start):
    scale = 1.0 / math.sqrt(TOK_DEV)
    n_dp = lax.axis_size("dp")
    chips = lax.axis_size("chip")
    n_t = 2 * chips
    d = lax.axis_index("dp").astype(jnp.int32)
    y = lax.axis_index("chip").astype(jnp.int32)
    c = lax.axis_index("core").astype(jnp.int32)
    t = 2 * y + c
    tok, part = activations.shape
    outs = out_grad.shape[1]
    din = weight.shape[0]
    error = error[0]
    q_t = q_start.T
    steps = range(1, chips)
    share = part // n_dp

    def to_sibling(a):
        return lax.ppermute(a, "core", [(0, 1), (1, 0)])

    def to_chip(a, k, flip=0):
        pairs = [(i, ((i // 2 + k) % chips) * 2 + ((i % 2) ^ flip)) for i in range(n_t)]
        return lax.ppermute(a, ("chip", "core"), pairs)

    def to_replica(a, k):
        return lax.ppermute(a, "dp", [(i, i ^ k) for i in range(n_dp)])

    def over_replicas(a, chunks):
        rounds = [1 << i for i in range(n_dp.bit_length() - 1)]
        for i, k in enumerate(rounds):
            if i == len(rounds) - 1:
                a = after(a, chunks)
            a = a + to_replica(a, k)
        return a

    src = jnp.stack([((y - k) % chips) * 2 + (c ^ e) for k in range(chips) for e in range(2)])
    src = src.astype(jnp.int32)

    moves = [(k, e) for k in steps for e in range(2)]
    w_parts = []
    for k, e in moves:
        dest = ((y + k) % chips) * 2 + (c ^ e)
        w_parts.append(lax.dynamic_slice(weight, (dest * part + d * share, 0), (share, outs)))
    w_start = [to_chip(a, k, e) for a, (k, e) in zip(w_parts, moves)]
    send, keep, y_own, w_sib = local_sketch(
        jnp.stack([c, t ^ 1]), error, after(q_t, *w_parts), out_grad, weight, chips, part
    )

    w_parts = after(w_start, send)

    got = to_sibling(send)
    y_t = y_own + to_sibling(y_own)

    def block(k):
        at = (y + k) % chips
        return lax.dynamic_index_in_dim(keep, at, 0, False) + lax.dynamic_index_in_dim(got, at, 0, False)

    blocks = [block(k) for k in range(chips)]
    e_list = [blocks[0]] + [to_chip(blocks[k], k) for k in steps]
    y_list = [y_t] + [to_chip(y_t, k) for k in steps]

    n_chunk = 4
    high = part // n_chunk
    acts = after(activations, blocks, y_t)
    x_rows = [acts[:, i * high : (i + 1) * high].T for i in range(n_chunk)]
    sketch = sketch_rows(after(e_list, x_rows), y_list, activations, scale)
    w_far = lax.all_gather(jnp.concatenate(w_parts, axis=1), "dp", axis=0, tiled=True)
    x_rows[0:2] = after(x_rows[0:2], e_list, y_list)
    x_far = [[to_chip(a, k) for k in steps] for a in x_rows[0:2]]
    sketch = after(over_replicas(sketch, x_far[0]), x_far[1])
    mine = jnp.stack([sketch] + [to_chip(sketch, k) for k in steps])
    other = to_sibling(mine)
    x_rows[2], x_rows[3] = after(x_rows[2], mine), after(x_rows[3], other)
    x_far += [[to_chip(a, k) for k in steps] for a in x_rows[2:4]]
    basis_t = make_basis(src, mine, other, n_dp)
    cuts = [0, tok // 8, tok // 2, 3 * tok // 4, tok]
    right_e, g_rows = right_error(error, basis_t, out_grad, cuts)

    g_sib = to_sibling(after(out_grad, sketch))
    w_sib = to_sibling(after(w_sib, sketch))
    grad = near_input_grad(t, out_grad, g_sib, weight, after(w_sib, right_e, x_far[2]))

    x_far[0:2] = after(x_far[0:2], mine)
    x_far[2] = after(x_far[2], right_e)
    x_far[3] = after(x_far[3], grad)
    pieces = list(x_rows) + [to_sibling(a) for a in after(x_rows, mine)]
    for n in range(len(steps)):
        held = [a[n] for a in x_far]
        pieces += held + [to_sibling(a) for a in held]

    g_far = [[to_chip(a, k) for k in steps] for a in g_rows]
    right = after(right_grad(src, basis_t, right_e, out_grad, pieces, scale), g_far[0])
    right = after(over_replicas(right, ()), g_far[1])
    new_error, q_t = update_error(
        src, error, basis_t, out_grad, pieces, right, n_dp, scale
    )

    g_far[2:] = after(g_far[2:], q_t)
    gs = []
    for n in range(len(steps)):
        held = [a[n] for a in g_far]
        gs += held + [to_sibling(a) for a in held]
    grad = far_input_grad(after(grad, q_t), w_far, gs, 0)
    return (grad, new_error[None], q_t.T)


def solution(mesh):
    n_dp, n_t = mesh.devices.shape
    mesh = jax.sharding.Mesh(mesh.devices.reshape(n_dp, n_t // 2, 2), ("dp", "chip", "core"))
    tensor = ("chip", "core")
    placed = (
        P("dp", tensor),
        P("dp", tensor),
        P(None, tensor),
        P("dp", None, tensor),
        P(tensor, None),
    )
    return jax.shard_map(
        per_device,
        mesh=mesh,
        in_specs=placed,
        out_specs=(P("dp", tensor), P("dp", None, tensor), P(tensor, None)),
        check_vma=False,
    )
```

```python
import functools
import math

import jax
import jax.numpy as jnp
from jax import lax
from jax.experimental import pallas as pl
from jax.experimental.pallas import tpu as pltpu
from jax.sharding import PartitionSpec as P

TOK_DEV = 1024
RANK = 32
MIB = 1 << 20
F32 = jnp.float32
BF16 = jnp.bfloat16


def dot(a, b, ca, cb, precision=None):
    return lax.dot_general(
        a, b, (((ca,), (cb,)), ((), ())), precision=precision, preferred_element_type=F32
    )


def split(a):
    high = a.astype(BF16)
    return high, (a - high.astype(F32)).astype(BF16)


def params(mib):
    return pltpu.CompilerParams(vmem_limit_bytes=mib * MIB)


def cost(flops, nbytes, weight=0.001):
    return pl.CostEstimate(
        flops=int(flops * weight), bytes_accessed=int(nbytes * weight), transcendentals=0
    )


def sketch_kernel(ids, e_ref, qt_ref, g_hbm, w_hbm, send_ref, keep_ref, y_ref, w_out, qs_ref, g_ref, w_ref, sem, w_sem):
    phase, y = pl.program_id(0), pl.program_id(1)
    move = pltpu.make_async_copy(g_hbm, g_ref, sem)
    part = w_ref.shape[0]
    rows = pl.ds(pl.multiple_of(ids[1] * part, part), part)
    w_in = pltpu.make_async_copy(w_hbm.at[rows], w_ref, w_sem.at[0])
    w_back = pltpu.make_async_copy(w_ref, w_out, w_sem.at[1])

    @pl.when((phase == 0) & (y == 0))
    def _():
        move.start()
        w_in.start()
        high, low = split(qt_ref[...])
        qs_ref[0:RANK, :] = high
        qs_ref[RANK : 2 * RANK, :] = low

    @pl.when((phase == 1) & (y == 0))
    def _():
        w_in.wait()
        w_back.start()

    high, low = split(e_ref[...])
    main = dot(high, qs_ref[...], 1, 1)
    rest = dot(low, qs_ref[0:RANK, :], 1, 1)
    rows = (main[:, 0:RANK] + main[:, RANK : 2 * RANK] + rest).T

    @pl.when(phase == 0)
    def _():
        send_ref[0] = rows

    @pl.when(phase == 1)
    def _():
        keep_ref[0] = rows

    @pl.when((phase == 1) & (y == pl.num_programs(1) - 1))
    def _():
        move.wait()
        w_back.wait()
        both = dot(qs_ref[...], g_ref[...], 1, 1)
        y_ref[...] = both[0:RANK, :] + both[RANK : 2 * RANK, :]


def local_sketch(ids, error, q_t, out_grad, weight, chips, part):
    tok, outs = out_grad.shape

    def e_map(p, y, ids):
        return (2 * y + jnp.where(p == 0, 1 - ids[0], ids[0]), 0)

    half = jax.ShapeDtypeStruct((chips, RANK, part), F32)
    return pl.pallas_call(
        sketch_kernel,
        grid_spec=pltpu.PrefetchScalarGridSpec(
            num_scalar_prefetch=1,
            grid=(2, chips),
            in_specs=[
                pl.BlockSpec((part, outs), e_map),
                pl.BlockSpec((RANK, outs), lambda p, y, ids: (0, 0)),
                pl.BlockSpec(memory_space=pl.ANY),
                pl.BlockSpec(memory_space=pl.ANY),
            ],
            out_specs=[
                pl.BlockSpec((1, RANK, part), lambda p, y, ids: (jnp.where(p == 0, y, chips - 1), 0, 0)),
                pl.BlockSpec((1, RANK, part), lambda p, y, ids: (jnp.where(p == 1, y, 0), 0, 0)),
                pl.BlockSpec((RANK, tok), lambda p, y, ids: (0, 0)),
                pl.BlockSpec(memory_space=pl.ANY),
            ],
            scratch_shapes=[
                pltpu.VMEM((2 * RANK, outs), BF16),
                pltpu.VMEM((tok, outs), BF16),
                pltpu.VMEM((part, outs), BF16),
                pltpu.SemaphoreType.DMA,
                pltpu.SemaphoreType.DMA((2,)),
            ],
        ),
        out_shape=[
            half,
            half,
            jax.ShapeDtypeStruct((RANK, tok), F32),
            jax.ShapeDtypeStruct((part, outs), BF16),
        ],
        compiler_params=params(60),
        cost_estimate=cost(6e9, error.size * 4, 2),
        name="error_sketch",
    )(ids, error, q_t, out_grad, weight)


def sketch_rows_kernel(*refs, n_e, scale):
    e_refs, y_refs, x_ref, out = refs[:n_e], refs[n_e:-2], refs[-2], refs[-1]
    y = y_refs[0][...]
    for r in y_refs[1:]:
        y = y + r[...]
    both = dot(jnp.concatenate(split(y), axis=0), x_ref[...], 1, 0)
    total = (both[0:RANK, :] + both[RANK:, :]) * scale
    for r in e_refs:
        total = total + r[...]
    out[...] = total


def sketch_rows(e_list, y_list, acts, scale):
    vm = pl.BlockSpec(memory_space=pltpu.VMEM)
    return pl.pallas_call(
        functools.partial(sketch_rows_kernel, n_e=len(e_list), scale=scale),
        in_specs=[vm] * (1 + len(e_list) + len(y_list)),
        out_specs=vm,
        out_shape=jax.ShapeDtypeStruct((RANK, acts.shape[1]), F32),
        compiler_params=params(24),
        cost_estimate=cost(1e9, 3e6),
        name="sketch_rows",
    )(*e_list, *y_list, acts)


def basis_kernel(src, mine, other, out, sk, *, n_dp, chips, part):
    for k in range(chips):
        for e, ref in enumerate((mine, other)):
            at = pl.multiple_of(src[2 * k + e] * part, part)
            sk[:, pl.ds(at, part)] = ref[k] * (1.0 / n_dp)
    s = sk[...]
    gram = dot(s, s, 1, 1, lax.Precision.HIGHEST)
    row = lax.broadcasted_iota(jnp.int32, (RANK, RANK), 0)
    col = lax.broadcasted_iota(jnp.int32, (RANK, RANK), 1)
    eye = (row == col).astype(F32)
    m = jnp.concatenate([gram, eye, jnp.zeros((RANK, 2 * RANK), F32)], axis=1)
    index = lax.broadcasted_iota(jnp.int32, (RANK, 1), 0)
    for j in range(RANK - 1):
        factor = jnp.where(index > j, m[:, j : j + 1] / m[j : j + 1, j : j + 1], 0.0)
        m = m - factor * m[j : j + 1, :]
    diag = jnp.sum(jnp.where(row == col, m[:, 0:RANK], 0.0), axis=1, keepdims=True)
    inverse = m[:, RANK : 2 * RANK] / jnp.sqrt(diag)
    out[...] = dot(inverse, s, 1, 0, lax.Precision.HIGHEST)


def make_basis(src, mine, other, n_dp):
    chips, _, part = mine.shape
    din = 2 * chips * part
    vm = pl.BlockSpec(memory_space=pltpu.VMEM)
    return pl.pallas_call(
        functools.partial(basis_kernel, n_dp=n_dp, chips=chips, part=part),
        in_specs=[pl.BlockSpec(memory_space=pltpu.SMEM), vm, vm],
        out_specs=vm,
        out_shape=jax.ShapeDtypeStruct((RANK, din), F32),
        scratch_shapes=[pltpu.VMEM((RANK, din), F32)],
        compiler_params=params(24),
        cost_estimate=cost(6e9, 2e6),
        name="basis",
    )(src, mine, other)


def right_error_kernel(e_ref, b_ref, g_hbm, acc, *rest, cuts):
    i = pl.program_id(0)
    outs, g_ref, sem, sems = rest[:-3], rest[-3], rest[-2], rest[-1]
    move = pltpu.make_async_copy(g_hbm, g_ref, sem)
    moves = [
        pltpu.make_async_copy(g_ref.at[lo:hi], outs[n], sems.at[n])
        for n, (lo, hi) in enumerate(zip(cuts[:-1], cuts[1:]))
    ]

    @pl.when(i == 0)
    def _():
        move.start()
        acc[...] = jnp.zeros_like(acc)

    @pl.when(i == 2)
    def _():
        move.wait()
        for m in moves:
            m.start()

    @pl.when(i == pl.num_programs(0) - 1)
    def _():
        for m in moves:
            m.wait()

    bh, bl = split(b_ref[...])
    eh, el = split(e_ref[...])
    main = dot(jnp.concatenate([bh, bl], axis=0), eh, 1, 0)
    acc[...] += main[0:RANK, :] + main[RANK:, :] + dot(bh, el, 1, 0)


def right_error(error, basis_t, out_grad, cuts):
    din, outs = error.shape
    blk = 512
    chunks = [jax.ShapeDtypeStruct((hi - lo, outs), BF16) for lo, hi in zip(cuts[:-1], cuts[1:])]
    anywhere = pl.BlockSpec(memory_space=pl.ANY)
    made = pl.pallas_call(
        functools.partial(right_error_kernel, cuts=cuts),
        grid=(din // blk,),
        in_specs=[
            pl.BlockSpec((blk, outs), lambda i: (i, 0)),
            pl.BlockSpec((RANK, blk), lambda i: (0, i)),
            anywhere,
        ],
        out_specs=[pl.BlockSpec((RANK, outs), lambda i: (0, 0))] + [anywhere] * len(chunks),
        out_shape=[jax.ShapeDtypeStruct((RANK, outs), F32)] + chunks,
        scratch_shapes=[
            pltpu.VMEM(out_grad.shape, BF16),
            pltpu.SemaphoreType.DMA,
            pltpu.SemaphoreType.DMA((len(chunks),)),
        ],
        compiler_params=params(48),
        cost_estimate=cost(8e9, error.size * 4, 1),
        name="right_error",
    )(error, basis_t, out_grad)
    return made[0], made[1:]


def copies(sources, target, sems):
    made, at = [], 0
    for n, ref in enumerate(sources):
        size = ref.shape[0]
        made.append(pltpu.make_async_copy(ref, target.at[at : at + size], sems.at[n]))
        at += size
    return made


def right_grad_kernel(*refs, n_t, per, scale):
    b_ref, r_ref, g_ref = refs[1:4]
    x_refs = refs[4 : 4 + n_t * per]
    out, vacc, xbuf, sems = refs[4 + n_t * per :]
    r = pl.program_id(0)
    part = xbuf.shape[0] // n_t
    moves = copies(x_refs, xbuf, sems)

    @pl.when(r == 0)
    def _():
        for m in moves:
            m.start()
        vacc[...] = jnp.zeros_like(vacc)

    for n in range(n_t):

        @pl.when(r == n)
        def _(n=n):
            for m in moves[n * per : (n + 1) * per]:
                m.wait()

    both = jnp.concatenate(split(b_ref[...]), axis=0)
    v = dot(both, xbuf[pl.ds(pl.multiple_of(r * part, part), part), :], 1, 0)
    vacc[...] += v[0:RANK, :] + v[RANK:, :]

    @pl.when(r == n_t - 1)
    def _():
        w = dot(jnp.concatenate(split(vacc[...]), axis=0), g_ref[...], 1, 0)
        out[...] = r_ref[...] + (w[0:RANK, :] + w[RANK:, :]) * scale


def right_grad(src, basis_t, right_e, out_grad, pieces, scale):
    tok, outs = out_grad.shape
    n_t = src.shape[0]
    din = basis_t.shape[1]
    part = din // n_t
    same = lambda r, src: (0, 0)
    return pl.pallas_call(
        functools.partial(right_grad_kernel, n_t=n_t, per=len(pieces) // n_t, scale=scale),
        grid_spec=pltpu.PrefetchScalarGridSpec(
            num_scalar_prefetch=1,
            grid=(n_t,),
            in_specs=[
                pl.BlockSpec((RANK, part), lambda r, src: (0, src[r])),
                pl.BlockSpec((RANK, outs), same),
                pl.BlockSpec((tok, outs), same),
            ]
            + [pl.BlockSpec(memory_space=pl.ANY)] * len(pieces),
            out_specs=pl.BlockSpec((RANK, outs), same),
            scratch_shapes=[
                pltpu.VMEM((RANK, tok), F32),
                pltpu.VMEM((din, tok), BF16),
                pltpu.SemaphoreType.DMA((len(pieces),)),
            ],
        ),
        out_shape=jax.ShapeDtypeStruct((RANK, outs), F32),
        compiler_params=params(40),
        cost_estimate=cost(4e9, din * tok * 2),
        name="right_grad",
    )(src, basis_t, right_e, out_grad, *pieces)


def update_kernel(*refs, n_t, per, n_dp, scale):
    e_ref, b_ref, g_ref, q_ref = refs[1:5]
    x_refs = refs[5 : 5 + n_t * per]
    out, qt_out, qs, xbuf, sems = refs[5 + n_t * per :]
    r = pl.program_id(0)
    part = xbuf.shape[0] // n_t
    moves = copies(x_refs, xbuf, sems)

    @pl.when(r == 0)
    def _():
        for m in moves[: 2 * per]:
            m.start()
        q_t = q_ref[...] * (1.0 / n_dp)
        qt_out[...] = q_t
        high, low = split(q_t)
        qs[0:RANK, :] = high
        qs[RANK : 2 * RANK, :] = low
        qs[2 * RANK : 3 * RANK, :] = high

    bh, bl = split(b_ref[...].T)
    low_rank = dot(jnp.concatenate([bh, bh, bl], axis=1), qs[...], 1, 0)
    for n in range(n_t):

        @pl.when(r == n)
        def _(n=n):
            if n > 0:
                for m in moves[(n + 1) * per : (n + 2) * per]:
                    m.start()
            for m in moves[n * per : (n + 1) * per]:
                m.wait()

    x = xbuf[pl.ds(pl.multiple_of(r * part, part), part), :]
    out[...] = e_ref[...] + dot(x, g_ref[...], 1, 0) * scale - low_rank


def update_error(src, error, basis_t, out_grad, pieces, q_t, n_dp, scale):
    tok, outs = out_grad.shape
    n_t = src.shape[0]
    din = error.shape[0]
    part = din // n_t
    block = pl.BlockSpec((part, outs), lambda r, src: (src[r], 0))
    same = lambda r, src: (0, 0)
    return pl.pallas_call(
        functools.partial(
            update_kernel, n_t=n_t, per=len(pieces) // n_t, n_dp=n_dp, scale=scale
        ),
        grid_spec=pltpu.PrefetchScalarGridSpec(
            num_scalar_prefetch=1,
            grid=(n_t,),
            in_specs=[
                block,
                pl.BlockSpec((RANK, part), lambda r, src: (0, src[r])),
                pl.BlockSpec((tok, outs), same),
                pl.BlockSpec((RANK, outs), same),
            ]
            + [pl.BlockSpec(memory_space=pl.ANY)] * len(pieces),
            out_specs=[block, pl.BlockSpec((RANK, outs), same)],
            scratch_shapes=[
                pltpu.VMEM((3 * RANK, outs), BF16),
                pltpu.VMEM((din, tok), BF16),
                pltpu.SemaphoreType.DMA((len(pieces),)),
            ],
        ),
        out_shape=[
            jax.ShapeDtypeStruct(error.shape, F32),
            jax.ShapeDtypeStruct((RANK, outs), F32),
        ],
        compiler_params=params(56),
        cost_estimate=cost(9e9, error.size * 8 + din * tok * 2, 1),
        name="update_error",
    )(src, error, basis_t, out_grad, q_t, *pieces)


def near_kernel(ids, g_ref, gs_ref, w_ref, ws_ref, out):
    out[...] = dot(g_ref[...], w_ref[...], 1, 1) + dot(gs_ref[...], ws_ref[...], 1, 1)


def near_input_grad(me_t, g_own, g_sib, weight, w_sib):
    tok, outs = g_own.shape
    part = w_sib.shape[0]
    blk = min(256, part)
    per = part // blk
    whole = pl.BlockSpec((tok, outs), lambda i, ids: (0, 0))
    return pl.pallas_call(
        near_kernel,
        grid_spec=pltpu.PrefetchScalarGridSpec(
            num_scalar_prefetch=1,
            grid=(per,),
            in_specs=[
                whole,
                whole,
                pl.BlockSpec((blk, outs), lambda i, ids: (ids[0] * per + i, 0)),
                pl.BlockSpec((blk, outs), lambda i, ids: (i, 0)),
            ],
            out_specs=pl.BlockSpec((tok, blk), lambda i, ids: (0, i)),
        ),
        out_shape=jax.ShapeDtypeStruct((tok, part), F32),
        compiler_params=params(48),
        cost_estimate=cost(4 * tok * outs * part, 12e6, 2),
        name="input_grad_near",
    )(jnp.reshape(me_t, (1,)), g_own, g_sib, weight, w_sib)


def far_kernel(*refs, n_far):
    prev, w_ref = refs[0], refs[1]
    g_refs = refs[2:-3]
    out, gbuf, sems = refs[-3:]
    tok = prev.shape[0]
    moves = copies(g_refs, gbuf, sems)

    @pl.when(pl.program_id(0) == 0)
    def _():
        for m in moves:
            m.start()
        for m in moves:
            m.wait()

    width = gbuf.shape[1]
    total = prev[...]
    for n in range(n_far):
        rows = gbuf[n * tok : (n + 1) * tok, :]
        total = total + dot(rows, w_ref[:, n * width : (n + 1) * width], 1, 1)
    out[...] = total


def far_input_grad(prev, w_far, gs, start):
    outs = gs[0].shape[1]
    tok, part = prev.shape
    n_far = w_far.shape[1] // outs
    rows = sum(g.shape[0] for g in gs) // n_far
    blk = min(256, part)
    to = pl.BlockSpec((rows, blk), lambda i: (start // rows, i))
    return pl.pallas_call(
        functools.partial(far_kernel, n_far=n_far),
        grid=(part // blk,),
        in_specs=[to, pl.BlockSpec((blk, w_far.shape[1]), lambda i: (i, 0))]
        + [pl.BlockSpec(memory_space=pl.ANY)] * len(gs),
        out_specs=to,
        out_shape=jax.ShapeDtypeStruct((tok, part), F32),
        scratch_shapes=[
            pltpu.VMEM((n_far * rows, outs), BF16),
            pltpu.SemaphoreType.DMA((len(gs),)),
        ],
        input_output_aliases={0: 0},
        compiler_params=params(24),
        cost_estimate=cost(2 * n_far * rows * outs * part, 10e6, 1),
        name="input_grad_far",
    )(prev, w_far, *gs)


def after(value, *others):
    return lax.optimization_barrier((value, others))[0]


def per_device(activations, out_grad, weight, error, q_start):
    scale = 1.0 / math.sqrt(TOK_DEV)
    n_dp = lax.axis_size("dp")
    chips = lax.axis_size("chip")
    n_t = 2 * chips
    d = lax.axis_index("dp").astype(jnp.int32)
    y = lax.axis_index("chip").astype(jnp.int32)
    c = lax.axis_index("core").astype(jnp.int32)
    t = 2 * y + c
    tok, part = activations.shape
    outs = out_grad.shape[1]
    din = weight.shape[0]
    error = error[0]
    q_t = q_start.T
    steps = range(1, chips)
    share = part // n_dp

    def to_sibling(a):
        return lax.ppermute(a, "core", [(0, 1), (1, 0)])

    def to_chip(a, k, flip=0):
        pairs = [(i, ((i // 2 + k) % chips) * 2 + ((i % 2) ^ flip)) for i in range(n_t)]
        return lax.ppermute(a, ("chip", "core"), pairs)

    def to_replica(a, k):
        return lax.ppermute(a, "dp", [(i, i ^ k) for i in range(n_dp)])

    def over_replicas(a, chunks):
        rounds = [1 << i for i in range(n_dp.bit_length() - 1)]
        for i, k in enumerate(rounds):
            if i == len(rounds) - 1:
                a = after(a, chunks)
            a = a + to_replica(a, k)
        return a

    src = jnp.stack([((y - k) % chips) * 2 + (c ^ e) for k in range(chips) for e in range(2)])
    src = src.astype(jnp.int32)

    moves = [(k, e) for k in steps for e in range(2)]
    w_parts = []
    for k, e in moves:
        dest = ((y + k) % chips) * 2 + (c ^ e)
        w_parts.append(lax.dynamic_slice(weight, (dest * part + d * share, 0), (share, outs)))
    w_start = [to_chip(a, k, e) for a, (k, e) in zip(w_parts, moves)]
    send, keep, y_own, w_sib = local_sketch(
        jnp.stack([c, t ^ 1]), error, after(q_t, *w_parts), out_grad, weight, chips, part
    )

    w_parts = after(w_start, send)

    got = to_sibling(send)
    y_t = y_own + to_sibling(y_own)

    def block(k):
        at = (y + k) % chips
        return lax.dynamic_index_in_dim(keep, at, 0, False) + lax.dynamic_index_in_dim(got, at, 0, False)

    blocks = [block(k) for k in range(chips)]
    e_list = [blocks[0]] + [to_chip(blocks[k], k) for k in steps]
    y_list = [y_t] + [to_chip(y_t, k) for k in steps]

    n_chunk = 4
    high = part // n_chunk
    acts = after(activations, blocks, y_t)
    x_rows = [acts[:, i * high : (i + 1) * high].T for i in range(n_chunk)]
    sketch = sketch_rows(after(e_list, x_rows), y_list, activations, scale)
    w_far = lax.all_gather(jnp.concatenate(w_parts, axis=1), "dp", axis=0, tiled=True)
    x_rows[0:2] = after(x_rows[0:2], e_list, y_list)
    x_far = [[to_chip(a, k) for k in steps] for a in x_rows[0:2]]
    sketch = after(over_replicas(sketch, x_far[0]), x_far[1])
    mine = jnp.stack([sketch] + [to_chip(sketch, k) for k in steps])
    other = to_sibling(mine)
    x_rows[2], x_rows[3] = after(x_rows[2], mine), after(x_rows[3], other)
    x_far += [[to_chip(a, k) for k in steps] for a in x_rows[2:4]]
    basis_t = make_basis(src, mine, other, n_dp)
    cuts = [0, tok // 8, tok // 2, 3 * tok // 4, tok]
    right_e, g_rows = right_error(error, basis_t, out_grad, cuts)

    g_sib = to_sibling(after(out_grad, sketch))
    w_sib = to_sibling(after(w_sib, sketch))
    grad = near_input_grad(t, out_grad, g_sib, weight, after(w_sib, right_e, x_far[2]))

    x_far[0:2] = after(x_far[0:2], mine)
    x_far[2] = after(x_far[2], right_e)
    x_far[3] = after(x_far[3], grad)
    pieces = list(x_rows) + [to_sibling(a) for a in after(x_rows, mine)]
    for n in range(len(steps)):
        held = [a[n] for a in x_far]
        pieces += held + [to_sibling(a) for a in held]

    right = right_grad(src, basis_t, right_e, out_grad, pieces, scale)
    g_rows = [g_rows[0]] + [after(a, right) for a in g_rows[1:]]
    g_far = [[to_chip(a, k) for k in steps] for a in g_rows]
    right = after(right, g_far[0])
    right = after(over_replicas(right, ()), g_far[1])
    new_error, q_t = update_error(
        src, error, basis_t, out_grad, pieces, right, n_dp, scale
    )

    g_far[2:] = after(g_far[2:], q_t)
    gs = []
    for n in range(len(steps)):
        held = [a[n] for a in g_far]
        gs += held + [to_sibling(a) for a in held]
    grad = far_input_grad(after(grad, q_t), w_far, gs, 0)
    return (grad, new_error[None], q_t.T)


def solution(mesh):
    n_dp, n_t = mesh.devices.shape
    mesh = jax.sharding.Mesh(mesh.devices.reshape(n_dp, n_t // 2, 2), ("dp", "chip", "core"))
    tensor = ("chip", "core")
    placed = (
        P("dp", tensor),
        P("dp", tensor),
        P(None, tensor),
        P("dp", None, tensor),
        P(tensor, None),
    )
    return jax.shard_map(
        per_device,
        mesh=mesh,
        in_specs=placed,
        out_specs=(P("dp", tensor), P("dp", None, tensor), P(tensor, None)),
        check_vma=False,
    )
```
